512 devices in a mesh: wide: 64 (over z_lo, y, core), beta: 8 (over z_hi, x).
Axes of the slice: x: 4, y: 4, z: 16 (z_hi: 2, z_lo: 8; z = z_hi * 8 + z_lo), core: 2. Of those that a mesh axis runs over, the one named last changes fastest.
Arguments:
- samples: float32 [2, 8, 1024, 1024], P(None, None, 'wide', 'beta'), may hold values from -6 to 6
- wigner: bfloat16 [8, 1024, 512, 2, 128], P(None, 'wide', 'beta'), may hold values from -0.25 to 0.25
Outputs:
- transform: float32 [2, 8, 1024, 2, 128], P(None, None, 'wide', None, 'beta')
The draws below stay inside these ranges and needn't reach their ends.
All inputs are finite; a program needn't handle non-finite values.
Results may differ from the reference program's by a relative error of at most 0.0029.
Values may be sent and summed in bfloat16 or wider, within the bound.
A program may use at most 64 MiB of HBM per device.

```python
import math
import jax
import jax.numpy as jnp
from jax import lax

G = 1024
R = 1024
L = 256
MW = 8
N_BETA = 8


def steps_of(key, shape, split, smallest, top_value):
    def one(axis_at, shards_of):
        steps = jax.random.uniform(jax.random.fold_in(jax.random.fold_in(key, 6), axis_at), (shards_of,), jnp.float32, smallest / len(split), top_value / len(split))
        return jnp.repeat(jnp.exp(steps), shape[axis_at] // shards_of).reshape((-1,) + (1,) * (len(shape) - axis_at - 1))

    gain = one(*split[0])
    for cut in split[1:]:
        gain = gain * one(*cut)
    return gain


def noise(stream_key, dims, scale, reach, split=(), kind=jnp.bfloat16):
    loudness = steps_of(stream_key, dims, split, -0.22, 0.18) if split else 1.0
    drawn = jax.random.normal(stream_key, dims, jnp.float32) * scale * loudness
    return jnp.minimum(jnp.maximum(drawn, -reach), reach).astype(kind)


def setup_inputs(seed: int = 0) -> dict:
    keys = jax.random.split(jax.random.key(seed), 3)
    samples = noise(keys[0], (2, MW, G, R), 1.0, 6.0, ((2, 64), (3, 8)), jnp.float32)
    wigner = noise(keys[1], (MW, G, R // 2, 2, L // 2), (R // 2) ** -0.5, 0.25, ((1, 64), (2, 8)))
    return dict(samples=samples, wigner=wigner)


def reference(samples, wigner):
    complex_field = samples[0] + 1j * samples[1]
    spectrum = jnp.fft.fft(complex_field, axis=1) / math.sqrt(G)
    pair_index = jnp.arange(R // 2, dtype=jnp.int32)
    band_span = R // (2 * N_BETA)
    block_index = pair_index // band_span
    offset = pair_index % band_span
    own_position = 2 * pair_index - offset
    partner_block = (block_index + N_BETA // 2) % N_BETA
    mirror_position = partner_block * (2 * band_span) + 2 * band_span - 1 - offset
    low_side = spectrum[:, :, own_position]
    high_side = spectrum[:, :, mirror_position]
    sign_factor = jnp.where(block_index < N_BETA // 2, 1.0, -1.0)
    even_sum = low_side + high_side
    odd_sum = sign_factor * (low_side - high_side)
    even_part = jnp.stack([even_sum.real, even_sum.imag], axis=1).astype(jnp.bfloat16)
    odd_part = jnp.stack([odd_sum.real, odd_sum.imag], axis=1).astype(jnp.bfloat16)

    def single(operands):
        even_one, odd_one, table_one = operands
        even_term = jnp.einsum('ckp,kpl->ckl', even_one.astype(jnp.float32), table_one[:, :, 0, :].astype(jnp.float32))
        odd_term = jnp.einsum('ckp,kpl->ckl', odd_one.astype(jnp.float32), table_one[:, :, 1, :].astype(jnp.float32))
        return jnp.stack([even_term, odd_term], axis=2)
    result = lax.map(single, (even_part, odd_part, wigner))
    return jnp.transpose(result, (1, 0, 2, 3, 4))
```

```python
import math

import jax
import jax.numpy as jnp
import ml_dtypes
import numpy as np
from jax import lax
from jax.experimental import pallas as pl
from jax.experimental.pallas import tpu as pltpu
from jax.sharding import PartitionSpec as P

MESH = pl.DeviceIdType.MESH
BF16 = jnp.bfloat16
F32 = jnp.float32
N_COPIES = 40


def tables():
    lane = np.arange(128)
    k1, n3 = lane // 16, lane % 16
    rows = []
    for v in range(8):
        angle = 2 * math.pi * ((16 * v + n3) * k1 % 1024) / 1024
        rows.append(np.stack([np.cos(angle), -np.sin(angle)]) / 32)
    for k2 in range(8):
        angle = 2 * math.pi * (n3 * k2 % 128) / 128
        rows.append(np.stack([np.cos(angle), -np.sin(angle)]))
    twiddle = np.stack(rows).astype(np.float32)

    step = np.zeros((2, 2, 8, 16, 2, 2, 8, 16))
    three = np.arange(16)
    for e in range(2):
        for first in range(8):
            for h in range(2):
                for z in range(8):
                    angle = 2 * math.pi * (three * (2 * z + h) % 16) / 16
                    cosine, sine = np.cos(angle), np.sin(angle)
                    column = first + 8 * e
                    step[e, 0, first, :, h, 0, z, column] = cosine
                    step[e, 0, first, :, h, 1, z, column] = -sine
                    step[e, 1, first, :, h, 0, z, column] = sine
                    step[e, 1, first, :, h, 1, z, column] = cosine
    step = step.reshape(512, 512)
    high = step.astype(ml_dtypes.bfloat16)
    low = (step - high.astype(np.float64)).astype(ml_dtypes.bfloat16)
    step = np.concatenate([high, low])

    order = np.zeros((2, 128, 2, 2, 64))
    spread = np.zeros((2, 2, 64, 2, 128))
    for part in range(2):
        for o in range(64):
            order[part, o, 0, part, o] = 1
            order[part, 127 - o, 1, part, o] = 1
            for parity in range(2):
                spread[parity, part, o, part, 2 * o + parity] = 1
    select = np.concatenate([order.reshape(256, 256), spread.reshape(256, 256)])
    return twiddle, step, select.astype(ml_dtypes.bfloat16)


def turn(value, eighths):
    re, im = value
    root = math.sqrt(0.5)
    if eighths == 0:
        return value
    if eighths == 1:
        return (re + im) * root, (im - re) * root
    if eighths == 2:
        return im, -re
    return (im - re) * root, -(re + im) * root


def butterfly(values):
    count = len(values)
    if count == 1:
        return values
    even, odd = butterfly(values[0::2]), butterfly(values[1::2])
    low, high = [], []
    for k in range(count // 2):
        a, b = even[k], turn(odd[k], k * 8 // count)
        low.append((a[0] + b[0], a[1] + b[1]))
        high.append((a[0] - b[0], a[1] - b[1]))
    return low + high


def kernel(
    samples, wigner, step_hbm, select_hbm, twiddle, out,
    wig, step, select, buf_a, send_b, buf_b, send_c, buf_c, send_d, buf_d,
    own_e, send_e, buf_e, send_f, buf_f, send_sem, recv_sem, load_sem,
):
    wide, beta = lax.axis_index("wide"), lax.axis_index("beta")
    z, v = wide // 8, wide % 8
    z_hi, x = beta // 4, beta % 4
    other = (beta + 4) % 8

    loads = [
        pltpu.make_async_copy(step_hbm, step, load_sem.at[0]),
        pltpu.make_async_copy(select_hbm, select, load_sem.at[1]),
        pltpu.make_async_copy(wigner, wig, load_sem.at[2]),
        pltpu.make_async_copy(samples.at[:, z], buf_a.at[z], load_sem.at[3]),
    ]

    line = [(((z + d) % 8) * 8 + v, beta) for d in range(1, 8)]
    far = [(((z + d) % 8) * 8 + v, other) for d in range(8)]
    plane = [(z * 8 + (v + d) % 8, beta) for d in range(1, 8)]
    ring = [(wide, z_hi * 4 + (x + d) % 4) for d in range(1, 4)]
    peers = line + far + plane + ring
    barrier = pltpu.get_barrier_semaphore()
    for at_wide, at_beta in peers:
        pl.semaphore_signal(
            barrier, inc=1, device_id={"wide": at_wide, "beta": at_beta}, device_id_type=MESH
        )
    for load in loads:
        load.start()
    pl.semaphore_wait(barrier, len(peers))

    sent = []

    def send(source, target, to):
        slot = len(sent)
        copy = pltpu.make_async_remote_copy(
            src_ref=source,
            dst_ref=target,
            send_sem=send_sem.at[slot],
            recv_sem=recv_sem.at[slot],
            device_id={"wide": to[0], "beta": to[1]},
            device_id_type=MESH,
        )
        copy.start()
        sent.append(copy)
        return copy

    copies = [send(samples.at[:, (z + d) % 8], buf_a.at[z], line[d - 1]) for d in range(1, 8)]
    loads[3].wait()
    for copy in copies:
        copy.wait_recv()
    done = butterfly([(buf_a[n, 0], buf_a[n, 1]) for n in range(8)])
    re = jnp.concatenate([value[0] for value in done], axis=0).T
    im = jnp.concatenate([value[1] for value in done], axis=0).T
    factor = twiddle[v]
    cosine, sine = factor[0:1], factor[1:2]
    send_b[:, 0] = (re * cosine - im * sine).reshape(8, 16, 128)
    send_b[:, 1] = (re * sine + im * cosine).reshape(8, 16, 128)

    keep = pltpu.make_async_copy(send_b.at[v], buf_b.at[v], load_sem.at[4])
    keep.start()
    copies = [send(send_b.at[(v + d) % 8], buf_b.at[v], plane[d - 1]) for d in range(1, 8)]
    loads[0].wait()
    loads[1].wait()
    keep.wait()
    for copy in copies:
        copy.wait_recv()
    done = butterfly([(buf_b[n, 0], buf_b[n, 1]) for n in range(8)])
    turned = []
    for k2 in range(8):
        re, im = done[k2]
        factor = twiddle[8 + k2]
        cosine, sine = factor[0:1], factor[1:2]
        turned.append((re * cosine - im * sine, re * sine + im * cosine))
    values = jnp.concatenate(
        [jnp.concatenate([*turned[2 * j], *turned[2 * j + 1]], axis=1) for j in range(4)], axis=0
    )
    high = values.astype(BF16)
    low = (values - high.astype(F32)).astype(BF16)
    both = jnp.concatenate([high, low], axis=0)
    main = jnp.dot(both, step[0:512], preferred_element_type=F32)
    rest = jnp.dot(high, step[512:1024], preferred_element_type=F32)
    spectrum = main[0:64] + (main[64:128] + rest)
    for j in range(4):
        for h in range(2):
            for part in range(2):
                column = 256 * h + 128 * part
                send_c[j + 4 * h, part] = spectrum[16 * j : 16 * j + 16, column : column + 128]

    keep = pltpu.make_async_copy(send_c.at[v], buf_c.at[v], load_sem.at[5])
    keep.start()
    copies = [send(send_c.at[(v + d) % 8], buf_c.at[v], plane[d - 1]) for d in range(1, 8)]
    keep.wait()
    for copy in copies:
        copy.wait_recv()
    values = jnp.concatenate([buf_c[:, part].reshape(128, 128).T for part in range(2)], axis=1)
    high = values.astype(BF16)
    left = values - high.astype(F32)
    middle = left.astype(BF16)
    low = (left - middle.astype(F32)).astype(BF16)
    parts = jnp.concatenate([high, middle, low], axis=0)
    moved = jnp.dot(parts, select[0:256], preferred_element_type=F32)
    moved = moved[0:128] + moved[128:256] + moved[256:384]
    for side in range(2):
        send_d[side] = moved[:, 128 * side : 128 * side + 128].reshape(8, 16, 128)

    keep = pltpu.make_async_copy(send_d.at[0, z], buf_d.at[0, z], load_sem.at[6])
    keep.start()
    copies = [send(send_d.at[1, (z + d) % 8], buf_d.at[1, z], far[d]) for d in range(8)]
    copies += [send(send_d.at[0, (z + d) % 8], buf_d.at[0, z], line[d - 1]) for d in range(1, 8)]
    loads[2].wait()
    keep.wait()
    for copy in copies:
        copy.wait_recv()
    own = buf_d[0].reshape(128, 128)
    mirror = buf_d[1].reshape(128, 128)
    sign = (1 - 2 * z_hi).astype(F32)
    even = (own + mirror).astype(BF16)
    odd = ((own - mirror) * sign).astype(BF16)
    even = jnp.dot(even, select[256:384], preferred_element_type=F32)
    odd = jnp.dot(odd, select[384:512], preferred_element_type=F32)
    order = lax.broadcasted_iota(jnp.int32, (128, 128), 0) % 16
    for g in range(4):
        rows = []
        for m in (2 * g, 2 * g + 1):
            for part in range(2):
                for side in (even, odd):
                    rows.append(side[16 * m : 16 * m + 16, 128 * part : 128 * part + 128])
        rows = jnp.concatenate(rows, axis=0)
        total = jnp.zeros((128, 256), F32)
        for i in range(8):
            pair = [jnp.where(order == 2 * i + e, rows, 0.0).astype(BF16) for e in range(2)]
            weights = [wig[2 * g + e, 256 * i : 256 * i + 256] for e in range(2)]
            total += jnp.dot(
                jnp.concatenate(pair, axis=1),
                jnp.concatenate(weights, axis=1),
                preferred_element_type=F32,
            )
        terms = jnp.concatenate([total[0:64, 0:128], total[64:128, 128:256]], axis=0).T
        own_e[:, g] = terms.reshape(8, 16, 128)
        terms = terms.astype(BF16)
        for owner in range(8):
            send_e[owner % 4, owner // 4, g] = terms[16 * owner : 16 * owner + 16]

    copies = [send(send_e.at[(x + d) % 4], buf_e.at[d - 1], ring[d - 1]) for d in range(1, 4)]
    for copy in copies:
        copy.wait_recv()

    def total_of(half):
        total = own_e[half * 4 + x]
        for d in range(3):
            total += buf_e[d, half].astype(F32)
        return total

    send_f[...] = total_of(1 - z_hi).astype(BF16)
    copy = send(send_f, buf_f, far[0])
    mine = total_of(z_hi)
    copy.wait_recv()
    out[...] = mine + buf_f[...].astype(F32)
    for copy in sent:
        copy.wait_send()


def body(samples, wigner):
    twiddle, step, select = tables()
    anywhere = pl.BlockSpec(memory_space=pl.ANY)
    in_vmem = pl.BlockSpec(memory_space=pltpu.VMEM)
    terms = pl.pallas_call(
        kernel,
        out_shape=jax.ShapeDtypeStruct((4, 16, 128), F32),
        in_specs=[anywhere, anywhere, anywhere, anywhere, in_vmem],
        out_specs=in_vmem,
        scratch_shapes=[
            pltpu.VMEM((8, 2048, 128), BF16),
            pltpu.VMEM((1024, 512), BF16),
            pltpu.VMEM((512, 256), BF16),
            pltpu.VMEM((8, 2, 16, 128), F32),
            pltpu.VMEM((8, 2, 16, 128), F32),
            pltpu.VMEM((8, 2, 16, 128), F32),
            pltpu.VMEM((8, 2, 16, 128), F32),
            pltpu.VMEM((8, 2, 16, 128), F32),
            pltpu.VMEM((2, 8, 16, 128), F32),
            pltpu.VMEM((2, 8, 16, 128), F32),
            pltpu.VMEM((8, 4, 16, 128), F32),
            pltpu.VMEM((4, 2, 4, 16, 128), BF16),
            pltpu.VMEM((3, 2, 4, 16, 128), BF16),
            pltpu.VMEM((4, 16, 128), BF16),
            pltpu.VMEM((4, 16, 128), BF16),
            pltpu.SemaphoreType.DMA((N_COPIES,)),
            pltpu.SemaphoreType.DMA((N_COPIES,)),
            pltpu.SemaphoreType.DMA((7,)),
        ],
        compiler_params=pltpu.CompilerParams(
            collective_id=0, has_side_effects=True, vmem_limit_bytes=60 * 1024 * 1024
        ),
    )(
        samples,
        wigner.reshape(8, 2048, 128),
        jnp.asarray(step),
        jnp.asarray(select),
        jnp.asarray(twiddle),
    )
    terms = terms.reshape(4, 16, 2, 2, 2, 16).transpose(3, 0, 2, 5, 4, 1)
    return terms.reshape(2, 8, 16, 2, 16)


def solution(mesh):
    return jax.shard_map(
        body,
        mesh=mesh,
        in_specs=(P(None, None, "wide", "beta"), P(None, "wide", "beta", None, None)),
        out_specs=P(None, None, "wide", None, "beta"),
        check_vma=False,
    )
```

```python
import math

import jax
import jax.numpy as jnp
import ml_dtypes
import numpy as np
from jax import lax
from jax.experimental import pallas as pl
from jax.experimental.pallas import tpu as pltpu
from jax.sharding import PartitionSpec as P

MESH = pl.DeviceIdType.MESH
BF16 = jnp.bfloat16
F32 = jnp.float32
N_COPIES = 52


def tables():
    lane = np.arange(128)
    k1, n3 = lane // 16, lane % 16
    rows = []
    for v in range(8):
        angle = 2 * math.pi * ((16 * v + n3) * k1 % 1024) / 1024
        rows.append(np.stack([np.cos(angle), -np.sin(angle)]) / 32)
    for k2 in range(8):
        angle = 2 * math.pi * (n3 * k2 % 128) / 128
        rows.append(np.stack([np.cos(angle), -np.sin(angle)]))
    twiddle = np.stack(rows).astype(np.float32)

    step = np.zeros((2, 8, 16, 2, 2, 8, 8))
    three = np.arange(16)
    for first in range(8):
        for h in range(2):
            for z in range(8):
                angle = 2 * math.pi * (three * (2 * z + h) % 16) / 16
                cosine, sine = np.cos(angle), np.sin(angle)
                step[0, first, :, h, 0, z, first] = cosine
                step[0, first, :, h, 1, z, first] = -sine
                step[1, first, :, h, 0, z, first] = sine
                step[1, first, :, h, 1, z, first] = cosine
    step = step.reshape(256, 256)
    high = step.astype(ml_dtypes.bfloat16)
    low = (step - high.astype(np.float64)).astype(ml_dtypes.bfloat16)
    step = np.concatenate([high, low])

    spread = np.zeros((2, 64, 2, 2, 128))
    for part in range(2):
        for p in range(64):
            for parity in range(2):
                spread[part, p, parity, part, 2 * p + parity] = 1
    place = np.zeros((4, 16, 2, 3, 4, 2, 16))
    for block in range(4):
        for k in range(16):
            for parity in range(2):
                place[block, k, parity, :, block, parity, k] = 1
    select = np.concatenate([spread.reshape(128, 512), place.reshape(128, 384)], axis=1)
    return twiddle, step, select.astype(ml_dtypes.bfloat16)


def turn(value, eighths):
    re, im = value
    root = math.sqrt(0.5)
    if eighths == 0:
        return value
    if eighths == 1:
        return (re + im) * root, (im - re) * root
    if eighths == 2:
        return im, -re
    return (im - re) * root, -(re + im) * root


def butterfly(values):
    count = len(values)
    if count == 1:
        return values
    even, odd = butterfly(values[0::2]), butterfly(values[1::2])
    low, high = [], []
    for k in range(count // 2):
        a, b = even[k], turn(odd[k], k * 8 // count)
        low.append((a[0] + b[0], a[1] + b[1]))
        high.append((a[0] - b[0], a[1] - b[1]))
    return low + high


def kernel(
    samples, wigner, step_hbm, select_hbm, twiddle_hbm, out,
    wig, step, select, twiddle, buf_a, send_b, buf_b, send_c, buf_c, send_d, buf_d,
    own_e, send_e, buf_e, send_f, buf_f, send_sem, recv_sem, load_sem, send_c_sem, recv_c_sem,
):
    wide, beta = lax.axis_index("wide"), lax.axis_index("beta")
    z, v = wide // 8, wide % 8
    z_hi, x = beta // 4, beta % 4
    other = (beta + 4) % 8

    load_samples = pltpu.make_async_copy(samples.at[:, z], buf_a.at[z], load_sem.at[0])
    load_twiddle = pltpu.make_async_copy(twiddle_hbm, twiddle, load_sem.at[1])
    load_step = pltpu.make_async_copy(step_hbm, step, load_sem.at[2])
    load_select = pltpu.make_async_copy(select_hbm, select, load_sem.at[3])
    load_wigner = pltpu.make_async_copy(wigner, wig, load_sem.at[4])

    line = [(((z + d) % 8) * 8 + v, beta) for d in range(1, 8)]
    far = [(((z + d) % 8) * 8 + v, other) for d in range(8)]
    plane = [(z * 8 + (v + d) % 8, beta) for d in range(1, 8)]
    ring = [(wide, z_hi * 4 + (x + d) % 4) for d in range(1, 4)]
    peers = far + line + plane + ring
    barrier = pltpu.get_barrier_semaphore()
    for at_wide, at_beta in peers:
        pl.semaphore_signal(
            barrier, inc=1, device_id={"wide": at_wide, "beta": at_beta}, device_id_type=MESH
        )
    for load in (load_samples, load_twiddle, load_step, load_select):
        load.start()
    pl.semaphore_wait(barrier, len(peers))

    sent = []

    def send(source, target, to, semaphores=None):
        if semaphores is None:
            slot = len(sent)
            semaphores = send_sem.at[slot], recv_sem.at[slot]
        copy = pltpu.make_async_remote_copy(
            src_ref=source,
            dst_ref=target,
            send_sem=semaphores[0],
            recv_sem=semaphores[1],
            device_id={"wide": to[0], "beta": to[1]},
            device_id_type=MESH,
        )
        copy.start()
        sent.append(copy)
        return copy

    copies = [send(samples.at[:, (z + d) % 8], buf_a.at[z], line[d - 1]) for d in range(1, 8)]
    load_wigner.start()
    load_samples.wait()
    load_twiddle.wait()
    for copy in copies:
        copy.wait_recv()
    done = butterfly([(buf_a[n, 0], buf_a[n, 1]) for n in range(8)])
    re = jnp.concatenate([value[0] for value in done], axis=0).T
    im = jnp.concatenate([value[1] for value in done], axis=0).T
    factor = twiddle[v]
    cosine, sine = factor[0:1], factor[1:2]
    send_b[:, 0] = (re * cosine - im * sine).reshape(8, 16, 128)
    send_b[:, 1] = (re * sine + im * cosine).reshape(8, 16, 128)

    keep = pltpu.make_async_copy(send_b.at[v], buf_b.at[v], load_sem.at[5])
    keep.start()
    copies = [send(send_b.at[(v + d) % 8], buf_b.at[v], plane[d - 1]) for d in range(1, 8)]
    load_step.wait()
    load_select.wait()
    keep.wait()
    for copy in copies:
        copy.wait_recv()
    done = butterfly([(buf_b[n, 0], buf_b[n, 1]) for n in range(8)])
    turned = []
    for k2 in range(8):
        re, im = done[k2]
        factor = twiddle[8 + k2]
        cosine, sine = factor[0:1], factor[1:2]
        turned.append(
            jnp.concatenate([re * cosine - im * sine, re * sine + im * cosine], axis=1)
        )
    values = jnp.concatenate(turned[0::2] + turned[1::2], axis=0)
    high = values.astype(BF16)
    low = (values - high.astype(F32)).astype(BF16)
    both = jnp.concatenate([high, low], axis=0)
    main = jnp.dot(both, step[0:256], preferred_element_type=F32)
    rest = jnp.dot(high, step[256:512], preferred_element_type=F32)
    spectrum = main[0:128] + (main[128:256] + rest)
    first_half = lax.broadcasted_iota(jnp.int32, (64, 128), 1) < 64
    for h in range(2):
        a = spectrum[0:64, 128 * h : 128 * h + 128]
        b = spectrum[64:128, 128 * h : 128 * h + 128]
        re = jnp.where(first_half, a, pltpu.roll(b, 64, 1))
        im = jnp.where(first_half, pltpu.roll(a, 64, 1), b)
        send_c[4 * h : 4 * h + 4, 0] = re.reshape(4, 16, 128)
        send_c[4 * h : 4 * h + 4, 1] = im.reshape(4, 16, 128)

    keep = pltpu.make_async_copy(send_c.at[v], buf_c.at[v], recv_c_sem.at[v])
    keep.start()
    for d in range(1, 8):
        semaphores = send_c_sem.at[d], recv_c_sem.at[v]
        send(send_c.at[(v + d) % 8], buf_c.at[v], plane[d - 1], semaphores)

    def gathered(side):
        for block in range(4 * side, 4 * side + 4):
            pltpu.make_async_copy(buf_c.at[block], buf_c.at[block], recv_c_sem.at[block]).wait()
        cycles = [buf_c[4 * side : 4 * side + 4, part].reshape(64, 128) for part in range(2)]
        return jnp.concatenate(cycles, axis=0).T

    def stage(side, values):
        for e in range(2):
            send_d[side, :, 8 * e : 8 * e + 8] = values[64 * e : 64 * e + 64].reshape(8, 8, 128)

    lane = lax.broadcasted_iota(jnp.int32, (128, 128), 1)
    turned = jnp.take_along_axis(gathered(1), 63 - lane % 64 + lane // 64 * 64, axis=1)
    stage(1, turned)
    mirrors = [send(send_d.at[1, (z + d) % 8], buf_d.at[1, z], far[d]) for d in range(8)]
    stage(0, gathered(0))
    owns = [pltpu.make_async_copy(send_d.at[0, z], buf_d.at[0, z], load_sem.at[6])]
    owns[0].start()
    owns += [send(send_d.at[0, (z + d) % 8], buf_d.at[0, z], line[d - 1]) for d in range(1, 8)]

    sign = (1 - 2 * z_hi).astype(F32)
    order = lax.broadcasted_iota(jnp.int32, (128, 128), 0) % 16
    to_sum, to_add = [], []

    def products(g):
        steps = (2 * g, 2 * g + 1)
        orders = [(z + 8 - d) % 8 for d in steps]
        for d in steps:
            mirrors[d].wait_recv()
            if d == 0:
                owns[d].wait()
            else:
                owns[d].wait_recv()
        own = jnp.concatenate([buf_d[0, m] for m in orders], axis=0)
        mirror = jnp.concatenate([buf_d[1, m] for m in orders], axis=0)
        even = (own + mirror).astype(BF16)
        odd = ((own - mirror) * sign).astype(BF16)
        even = jnp.dot(even, select[:, 0:256], preferred_element_type=F32)
        odd = jnp.dot(odd, select[:, 256:512], preferred_element_type=F32)
        rows = [
            side[16 * at : 16 * at + 16, 128 * part : 128 * part + 128]
            for at in range(2)
            for part in range(2)
            for side in (even, odd)
        ]
        rows = jnp.concatenate(rows, axis=0)
        total = jnp.zeros((128, 256), F32)
        for i in range(8):
            pair = [jnp.where(order == 2 * i + e, rows, 0.0).astype(BF16) for e in range(2)]
            weights = [wig[m, 256 * i : 256 * i + 256] for m in orders]
            total += jnp.dot(
                jnp.concatenate(pair, axis=1),
                jnp.concatenate(weights, axis=1),
                preferred_element_type=F32,
            )
        terms = jnp.concatenate([total[0:64, 0:128], total[64:128, 128:256]], axis=0).T
        own_e[g] = terms.reshape(8, 16, 128)
        terms = terms.astype(BF16)
        for owner in range(8):
            send_e[g, owner % 4, owner // 4] = terms[16 * owner : 16 * owner + 16]
        to_sum.append(
            [send(send_e.at[g, (x + d) % 4], buf_e.at[g, d - 1], ring[d - 1]) for d in range(1, 4)]
        )

    def total_of(g, half):
        total = own_e[g, half * 4 + x]
        for d in range(3):
            total += buf_e[g, d, half].astype(F32)
        return total

    def sum_x(g):
        for copy in to_sum[g]:
            copy.wait_recv()
        send_f[g] = total_of(g, 1 - z_hi).astype(BF16)
        to_add.append(send(send_f.at[g], buf_f.at[g], far[0]))
        own_e[g, z_hi * 4 + x] = total_of(g, z_hi)

    def finish(g):
        to_add[g].wait_recv()
        total = own_e[g, z_hi * 4 + x] + buf_f[g].astype(F32)
        high = total.astype(BF16)
        left = total - high.astype(F32)
        middle = left.astype(BF16)
        low = (left - middle.astype(F32)).astype(BF16)
        placed = lax.dot_general(
            select[:, 512:896],
            jnp.concatenate([high, middle, low], axis=1),
            (((1,), (1,)), ((), ())),
            preferred_element_type=F32,
        )
        for at in range(2):
            for part in range(2):
                row = 64 * at + 32 * part
                out[part, (z + 8 - 2 * g - at) % 8] = placed[row : row + 32]

    load_wigner.wait()
    products(0)
    products(1)
    sum_x(0)
    products(2)
    sum_x(1)
    products(3)
    sum_x(2)
    finish(0)
    finish(1)
    sum_x(3)
    finish(2)
    finish(3)
    for copy in sent:
        copy.wait_send()


def body(samples, wigner):
    twiddle, step, select = tables()
    anywhere = pl.BlockSpec(memory_space=pl.ANY)
    terms = pl.pallas_call(
        kernel,
        out_shape=jax.ShapeDtypeStruct((2, 8, 32, 16), F32),
        in_specs=[anywhere] * 5,
        out_specs=pl.BlockSpec(memory_space=pltpu.VMEM),
        scratch_shapes=[
            pltpu.VMEM((8, 2048, 128), BF16),
            pltpu.VMEM((512, 256), BF16),
            pltpu.VMEM((128, 896), BF16),
            pltpu.VMEM((16, 2, 128), F32),
            pltpu.VMEM((8, 2, 16, 128), F32),
            pltpu.VMEM((8, 2, 16, 128), F32),
            pltpu.VMEM((8, 2, 16, 128), F32),
            pltpu.VMEM((8, 2, 16, 128), F32),
            pltpu.VMEM((8, 2, 16, 128), F32),
            pltpu.VMEM((2, 8, 16, 128), F32),
            pltpu.VMEM((2, 8, 16, 128), F32),
            pltpu.VMEM((4, 8, 16, 128), F32),
            pltpu.VMEM((4, 4, 2, 16, 128), BF16),
            pltpu.VMEM((4, 3, 2, 16, 128), BF16),
            pltpu.VMEM((4, 16, 128), BF16),
            pltpu.VMEM((4, 16, 128), BF16),
            pltpu.SemaphoreType.DMA((N_COPIES,)),
            pltpu.SemaphoreType.DMA((N_COPIES,)),
            pltpu.SemaphoreType.DMA((7,)),
            pltpu.SemaphoreType.DMA((8,)),
            pltpu.SemaphoreType.DMA((8,)),
        ],
        compiler_params=pltpu.CompilerParams(
            collective_id=0, has_side_effects=True, vmem_limit_bytes=60 * 1024 * 1024
        ),
    )(
        samples,
        wigner.reshape(8, 2048, 128),
        jnp.asarray(step),
        jnp.asarray(select),
        jnp.asarray(twiddle),
    )
    return terms.reshape(2, 8, 16, 2, 16)


def solution(mesh):
    return jax.shard_map(
        body,
        mesh=mesh,
        in_specs=(P(None, None, "wide", "beta"), P(None, "wide", "beta", None, None)),
        out_specs=P(None, None, "wide", None, "beta"),
        check_vma=False,
    )
```

```python
import math

import jax
import jax.numpy as jnp
import ml_dtypes
import numpy as np
from jax import lax
from jax.experimental import pallas as pl
from jax.experimental.pallas import tpu as pltpu
from jax.sharding import PartitionSpec as P

MESH = pl.DeviceIdType.MESH
BF16 = jnp.bfloat16
F32 = jnp.float32
N_COPIES = 44


def tables():
    lane = np.arange(128)
    k1, n3 = lane // 16, lane % 16
    rows = []
    for v in range(8):
        angle = 2 * math.pi * ((16 * v + n3) * k1 % 1024) / 1024
        rows.append(np.stack([np.cos(angle), -np.sin(angle)]) / 32)
    for k2 in range(8):
        angle = 2 * math.pi * (n3 * k2 % 128) / 128
        rows.append(np.stack([np.cos(angle), -np.sin(angle)]))
    twiddle = np.stack(rows).astype(np.float32)

    step = np.zeros((2, 8, 16, 2, 2, 8, 8))
    three = np.arange(16)
    for first in range(8):
        for h in range(2):
            for z in range(8):
                angle = 2 * math.pi * (three * (2 * z + h) % 16) / 16
                cosine, sine = np.cos(angle), np.sin(angle)
                step[0, first, :, h, 0, z, first] = cosine
                step[0, first, :, h, 1, z, first] = -sine
                step[1, first, :, h, 0, z, first] = sine
                step[1, first, :, h, 1, z, first] = cosine
    step = step.reshape(256, 256)
    high = step.astype(ml_dtypes.bfloat16)
    low = (step - high.astype(np.float64)).astype(ml_dtypes.bfloat16)
    step = np.concatenate([high, low])

    spread = np.zeros((2, 64, 2, 2, 128))
    for part in range(2):
        for p in range(64):
            for parity in range(2):
                spread[part, p, parity, part, 2 * p + parity] = 1
    place = np.zeros((4, 16, 2, 3, 4, 2, 16))
    for block in range(4):
        for k in range(16):
            for parity in range(2):
                place[block, k, parity, :, block, parity, k] = 1
    select = np.concatenate([spread.reshape(128, 512), place.reshape(128, 384)], axis=1)
    return twiddle, step, select.astype(ml_dtypes.bfloat16)


def turn(value, eighths):
    re, im = value
    root = math.sqrt(0.5)
    if eighths == 0:
        return value
    if eighths == 1:
        return (re + im) * root, (im - re) * root
    if eighths == 2:
        return im, -re
    return (im - re) * root, -(re + im) * root


def butterfly(values):
    count = len(values)
    if count == 1:
        return values
    even, odd = butterfly(values[0::2]), butterfly(values[1::2])
    low, high = [], []
    for k in range(count // 2):
        a, b = even[k], turn(odd[k], k * 8 // count)
        low.append((a[0] + b[0], a[1] + b[1]))
        high.append((a[0] - b[0], a[1] - b[1]))
    return low + high


def kernel(
    samples, wigner, step_hbm, select_hbm, twiddle_hbm, out,
    wig, step, select, twiddle, buf_a, send_b, buf_b, send_c, buf_c, send_d, buf_d,
    own_e, send_e, buf_e, send_f, buf_f, send_sem, recv_sem, load_sem, send_c_sem, recv_c_sem,
):
    wide, beta = lax.axis_index("wide"), lax.axis_index("beta")
    z, v = wide // 8, wide % 8
    z_hi, x = beta // 4, beta % 4
    other = (beta + 4) % 8

    load_samples = pltpu.make_async_copy(samples.at[:, z], buf_a.at[z], load_sem.at[0])
    load_twiddle = pltpu.make_async_copy(twiddle_hbm, twiddle, load_sem.at[1])
    load_step = pltpu.make_async_copy(step_hbm, step, load_sem.at[2])
    load_select = pltpu.make_async_copy(select_hbm, select, load_sem.at[3])
    load_wigner = pltpu.make_async_copy(wigner, wig, load_sem.at[4])

    line = [(((z + d) % 8) * 8 + v, beta) for d in range(1, 8)]
    far = [(((z + d) % 8) * 8 + v, other) for d in range(8)]
    plane = [(z * 8 + (v + d) % 8, beta) for d in range(1, 8)]
    ring = [(wide, z_hi * 4 + (x + d) % 4) for d in range(1, 4)]
    peers = far + line + plane + ring
    barrier = pltpu.get_barrier_semaphore()
    for at_wide, at_beta in peers:
        pl.semaphore_signal(
            barrier, inc=1, device_id={"wide": at_wide, "beta": at_beta}, device_id_type=MESH
        )
    for load in (load_samples, load_twiddle, load_step, load_select):
        load.start()
    pl.semaphore_wait(barrier, len(peers))

    sent, settled = [], []

    def send(source, target, to, semaphores=None):
        if semaphores is None:
            slot = len(sent)
            semaphores = send_sem.at[slot], recv_sem.at[slot]
        copy = pltpu.make_async_remote_copy(
            src_ref=source,
            dst_ref=target,
            send_sem=semaphores[0],
            recv_sem=semaphores[1],
            device_id={"wide": to[0], "beta": to[1]},
            device_id_type=MESH,
        )
        copy.start()
        sent.append(copy)
        return copy

    def settle(in_flight=0):
        for copy in sent[len(settled) : len(sent) - in_flight]:
            copy.wait_send()
            settled.append(copy)

    copies = [send(samples.at[:, (z + d) % 8], buf_a.at[z], line[d - 1]) for d in range(1, 8)]
    load_wigner.start()
    load_samples.wait()
    load_twiddle.wait()
    for copy in copies:
        copy.wait_recv()
    done = butterfly([(buf_a[n, 0], buf_a[n, 1]) for n in range(8)])
    re = jnp.concatenate([value[0] for value in done], axis=0).T
    im = jnp.concatenate([value[1] for value in done], axis=0).T
    factor = twiddle[v]
    cosine, sine = factor[0:1], factor[1:2]
    send_b[:, 0] = (re * cosine - im * sine).reshape(8, 16, 128)
    send_b[:, 1] = (re * sine + im * cosine).reshape(8, 16, 128)

    keep = pltpu.make_async_copy(send_b.at[v], buf_b.at[v], load_sem.at[5])
    keep.start()
    copies = [send(send_b.at[(v + d) % 8], buf_b.at[v], plane[d - 1]) for d in range(1, 8)]
    settle(7)
    load_step.wait()
    load_select.wait()
    keep.wait()
    for copy in copies:
        copy.wait_recv()
    done = butterfly([(buf_b[n, 0], buf_b[n, 1]) for n in range(8)])
    turned = []
    for k2 in range(8):
        re, im = done[k2]
        factor = twiddle[8 + k2]
        cosine, sine = factor[0:1], factor[1:2]
        turned.append(
            jnp.concatenate([re * cosine - im * sine, re * sine + im * cosine], axis=1)
        )
    values = jnp.concatenate(turned[0::2] + turned[1::2], axis=0)
    high = values.astype(BF16)
    low = (values - high.astype(F32)).astype(BF16)
    both = jnp.concatenate([high, low], axis=0)
    main = jnp.dot(both, step[0:256], preferred_element_type=F32)
    rest = jnp.dot(high, step[256:512], preferred_element_type=F32)
    spectrum = main[0:128] + (main[128:256] + rest)
    first_half = lax.broadcasted_iota(jnp.int32, (64, 128), 1) < 64
    for h in range(2):
        a = spectrum[0:64, 128 * h : 128 * h + 128]
        b = spectrum[64:128, 128 * h : 128 * h + 128]
        re = jnp.where(first_half, a, pltpu.roll(b, 64, 1))
        im = jnp.where(first_half, pltpu.roll(a, 64, 1), b)
        send_c[4 * h : 4 * h + 4, 0] = re.reshape(4, 16, 128)
        send_c[4 * h : 4 * h + 4, 1] = im.reshape(4, 16, 128)

    keep = pltpu.make_async_copy(send_c.at[v], buf_c.at[v], recv_c_sem.at[v])
    keep.start()
    for d in range(1, 8):
        semaphores = send_c_sem.at[d], recv_c_sem.at[v]
        send(send_c.at[(v + d) % 8], buf_c.at[v], plane[d - 1], semaphores)
    settle(7)

    def gathered(side):
        for block in range(4 * side, 4 * side + 4):
            pltpu.make_async_copy(buf_c.at[block], buf_c.at[block], recv_c_sem.at[block]).wait()
        cycles = [buf_c[4 * side : 4 * side + 4, part].reshape(64, 128) for part in range(2)]
        return jnp.concatenate(cycles, axis=0).T

    def stage(side, values):
        for e in range(2):
            send_d[side, :, 8 * e : 8 * e + 8] = values[64 * e : 64 * e + 64].reshape(8, 8, 128)

    lane = lax.broadcasted_iota(jnp.int32, (128, 128), 1)
    turned = jnp.take_along_axis(gathered(1), 63 - lane % 64 + lane // 64 * 64, axis=1)
    stage(1, turned)
    mirrors = [send(send_d.at[1, (z + d) % 8], buf_d.at[1, z], far[d]) for d in range(8)]
    stage(0, gathered(0))
    owns = [pltpu.make_async_copy(send_d.at[0, z], buf_d.at[0, z], load_sem.at[6])]
    owns[0].start()
    owns += [send(send_d.at[0, (z + d) % 8], buf_d.at[0, z], line[d - 1]) for d in range(1, 8)]

    sign = (1 - 2 * z_hi).astype(F32)
    order = lax.broadcasted_iota(jnp.int32, (128, 128), 0) % 16
    to_sum, to_add = [], []

    def products(g):
        steps = (2 * g, 2 * g + 1)
        orders = [(z + 8 - d) % 8 for d in steps]
        for d in steps:
            mirrors[d].wait_recv()
            if d == 0:
                owns[d].wait()
            else:
                owns[d].wait_recv()
        own = jnp.concatenate([buf_d[0, m] for m in orders], axis=0)
        mirror = jnp.concatenate([buf_d[1, m] for m in orders], axis=0)
        even = (own + mirror).astype(BF16)
        odd = ((own - mirror) * sign).astype(BF16)
        even = jnp.dot(even, select[:, 0:256], preferred_element_type=F32)
        odd = jnp.dot(odd, select[:, 256:512], preferred_element_type=F32)
        rows = [
            side[16 * at : 16 * at + 16, 128 * part : 128 * part + 128]
            for at in range(2)
            for part in range(2)
            for side in (even, odd)
        ]
        rows = jnp.concatenate(rows, axis=0)
        total = jnp.zeros((128, 256), F32)
        for i in range(8):
            pair = [jnp.where(order == 2 * i + e, rows, 0.0).astype(BF16) for e in range(2)]
            weights = [wig[m, 256 * i : 256 * i + 256] for m in orders]
            total += jnp.dot(
                jnp.concatenate(pair, axis=1),
                jnp.concatenate(weights, axis=1),
                preferred_element_type=F32,
            )
        terms = jnp.concatenate([total[0:64, 0:128], total[64:128, 128:256]], axis=0).T
        own_e[g // 2, :, g % 2] = terms.reshape(8, 16, 128)
        terms = terms.astype(BF16)
        for owner in range(8):
            rows = terms[16 * owner : 16 * owner + 16]
            send_e[g // 2, owner % 4, owner // 4, g % 2] = rows

    def spread_x(half):
        to_sum.append(
            [
                send(send_e.at[half, (x + d) % 4], buf_e.at[half, d - 1], ring[d - 1])
                for d in range(1, 4)
            ]
        )

    def total_of(half, owner):
        total = own_e[half, owner * 4 + x]
        for d in range(3):
            total += buf_e[half, d, owner].astype(F32)
        return total

    def sum_x(half):
        for copy in to_sum[half]:
            copy.wait_recv()
        send_f[half] = total_of(half, 1 - z_hi).astype(BF16)
        to_add.append(send(send_f.at[half], buf_f.at[half], far[0]))
        own_e[half, z_hi * 4 + x] = total_of(half, z_hi)

    def finish(g):
        half = g // 2
        if g % 2 == 0:
            to_add[half].wait_recv()
        total = own_e[half, z_hi * 4 + x, g % 2] + buf_f[half, g % 2].astype(F32)
        high = total.astype(BF16)
        left = total - high.astype(F32)
        middle = left.astype(BF16)
        low = (left - middle.astype(F32)).astype(BF16)
        placed = lax.dot_general(
            select[:, 512:896],
            jnp.concatenate([high, middle, low], axis=1),
            (((1,), (1,)), ((), ())),
            preferred_element_type=F32,
        )
        for at in range(2):
            for part in range(2):
                row = 64 * at + 32 * part
                out[part, (z + 8 - 2 * g - at) % 8] = placed[row : row + 32]

    load_wigner.wait()
    products(0)
    products(1)
    spread_x(0)
    products(2)
    products(3)
    spread_x(1)
    settle(3)
    sum_x(0)
    sum_x(1)
    settle(2)
    finish(0)
    finish(1)
    finish(2)
    finish(3)
    settle()


def body(samples, wigner):
    twiddle, step, select = tables()
    anywhere = pl.BlockSpec(memory_space=pl.ANY)
    terms = pl.pallas_call(
        kernel,
        out_shape=jax.ShapeDtypeStruct((2, 8, 32, 16), F32),
        in_specs=[anywhere] * 5,
        out_specs=pl.BlockSpec(memory_space=pltpu.VMEM),
        scratch_shapes=[
            pltpu.VMEM((8, 2048, 128), BF16),
            pltpu.VMEM((512, 256), BF16),
            pltpu.VMEM((128, 896), BF16),
            pltpu.VMEM((16, 2, 128), F32),
            pltpu.VMEM((8, 2, 16, 128), F32),
            pltpu.VMEM((8, 2, 16, 128), F32),
            pltpu.VMEM((8, 2, 16, 128), F32),
            pltpu.VMEM((8, 2, 16, 128), F32),
            pltpu.VMEM((8, 2, 16, 128), F32),
            pltpu.VMEM((2, 8, 16, 128), F32),
            pltpu.VMEM((2, 8, 16, 128), F32),
            pltpu.VMEM((2, 8, 2, 16, 128), F32),
            pltpu.VMEM((2, 4, 2, 2, 16, 128), BF16),
            pltpu.VMEM((2, 3, 2, 2, 16, 128), BF16),
            pltpu.VMEM((2, 2, 16, 128), BF16),
            pltpu.VMEM((2, 2, 16, 128), BF16),
            pltpu.SemaphoreType.DMA((N_COPIES,)),
            pltpu.SemaphoreType.DMA((N_COPIES,)),
            pltpu.SemaphoreType.DMA((7,)),
            pltpu.SemaphoreType.DMA((8,)),
            pltpu.SemaphoreType.DMA((8,)),
        ],
        compiler_params=pltpu.CompilerParams(
            collective_id=0, has_side_effects=True, vmem_limit_bytes=60 * 1024 * 1024
        ),
    )(
        samples,
        wigner.reshape(8, 2048, 128),
        jnp.asarray(step),
        jnp.asarray(select),
        jnp.asarray(twiddle),
    )
    return terms.reshape(2, 8, 16, 2, 16)


def solution(mesh):
    return jax.shard_map(
        body,
        mesh=mesh,
        in_specs=(P(None, None, "wide", "beta"), P(None, "wide", "beta", None, None)),
        out_specs=P(None, None, "wide", None, "beta"),
        check_vma=False,
    )
```

```python
import math

import jax
import jax.numpy as jnp
import ml_dtypes
import numpy as np
from jax import lax
from jax.experimental import pallas as pl
from jax.experimental.pallas import tpu as pltpu
from jax.sharding import PartitionSpec as P

MESH = pl.DeviceIdType.MESH
BF16 = jnp.bfloat16
F32 = jnp.float32
N_COPIES = 44


def tables():
    lane = np.arange(128)
    k1, n3 = lane // 16, lane % 16
    rows = []
    for v in range(8):
        angle = 2 * math.pi * ((16 * v + n3) * k1 % 1024) / 1024
        rows.append(np.stack([np.cos(angle), -np.sin(angle)]) / 32)
    for k2 in range(8):
        angle = 2 * math.pi * (n3 * k2 % 128) / 128
        rows.append(np.stack([np.cos(angle), -np.sin(angle)]))
    twiddle = np.stack(rows).astype(np.float32)

    step = np.zeros((2, 8, 16, 2, 2, 8, 8))
    three = np.arange(16)
    for first in range(8):
        for h in range(2):
            for z in range(8):
                angle = 2 * math.pi * (three * (2 * z + h) % 16) / 16
                cosine, sine = np.cos(angle), np.sin(angle)
                step[0, first, :, h, 0, z, first] = cosine
                step[0, first, :, h, 1, z, first] = -sine
                step[1, first, :, h, 0, z, first] = sine
                step[1, first, :, h, 1, z, first] = cosine
    step = step.reshape(256, 256)
    high = step.astype(ml_dtypes.bfloat16)
    low = (step - high.astype(np.float64)).astype(ml_dtypes.bfloat16)
    step = np.concatenate([high, low])

    spread = np.zeros((2, 64, 2, 2, 128))
    for part in range(2):
        for p in range(64):
            for parity in range(2):
                spread[part, p, parity, part, 2 * p + parity] = 1
    place = np.zeros((4, 16, 2, 3, 4, 2, 16))
    for block in range(4):
        for k in range(16):
            for parity in range(2):
                place[block, k, parity, :, block, parity, k] = 1
    select = np.concatenate([spread.reshape(128, 512), place.reshape(128, 384)], axis=1)
    return twiddle, step, select.astype(ml_dtypes.bfloat16)


def turn(value, eighths):
    re, im = value
    root = math.sqrt(0.5)
    if eighths == 0:
        return value
    if eighths == 1:
        return (re + im) * root, (im - re) * root
    if eighths == 2:
        return im, -re
    return (im - re) * root, -(re + im) * root


def butterfly(values):
    count = len(values)
    if count == 1:
        return values
    even, odd = butterfly(values[0::2]), butterfly(values[1::2])
    low, high = [], []
    for k in range(count // 2):
        a, b = even[k], turn(odd[k], k * 8 // count)
        low.append((a[0] + b[0], a[1] + b[1]))
        high.append((a[0] - b[0], a[1] - b[1]))
    return low + high


def kernel(
    samples, wigner, step_hbm, select_hbm, twiddle_hbm, out,
    wig, step, select, twiddle, buf_a, send_b, buf_b, send_c, buf_c, send_d, buf_d,
    own_e, send_e, buf_e, send_f, buf_f, send_sem, recv_sem, load_sem, send_c_sem, recv_c_sem,
    send_d_sem, recv_d_sem,
):
    wide, beta = lax.axis_index("wide"), lax.axis_index("beta")
    z, v = wide // 8, wide % 8
    z_hi, x = beta // 4, beta % 4
    other = (beta + 4) % 8

    load_samples = pltpu.make_async_copy(samples.at[:, z], buf_a.at[z], load_sem.at[0])
    load_twiddle = pltpu.make_async_copy(twiddle_hbm, twiddle, load_sem.at[1])
    load_step = pltpu.make_async_copy(step_hbm, step, load_sem.at[2])
    load_select = pltpu.make_async_copy(select_hbm, select, load_sem.at[3])
    load_wigner = pltpu.make_async_copy(wigner, wig, load_sem.at[4])

    line = [(((z + d) % 8) * 8 + v, beta) for d in range(1, 8)]
    far = [(((z + d) % 8) * 8 + v, other) for d in range(8)]
    plane = [(z * 8 + (v + d) % 8, beta) for d in range(1, 8)]
    ring = [(wide, z_hi * 4 + (x + d) % 4) for d in range(1, 4)]
    peers = far + line + plane + ring
    barrier = pltpu.get_barrier_semaphore()
    for at_wide, at_beta in peers:
        pl.semaphore_signal(
            barrier, inc=1, device_id={"wide": at_wide, "beta": at_beta}, device_id_type=MESH
        )
    for load in (load_samples, load_twiddle, load_step, load_select):
        load.start()
    pl.semaphore_wait(barrier, len(peers))

    sent, settled = [], []

    def send(source, target, to, semaphores=None):
        if semaphores is None:
            slot = len(sent)
            semaphores = send_sem.at[slot], recv_sem.at[slot]
        copy = pltpu.make_async_remote_copy(
            src_ref=source,
            dst_ref=target,
            send_sem=semaphores[0],
            recv_sem=semaphores[1],
            device_id={"wide": to[0], "beta": to[1]},
            device_id_type=MESH,
        )
        copy.start()
        sent.append(copy)
        return copy

    def settle(in_flight=0):
        for copy in sent[len(settled) : len(sent) - in_flight]:
            copy.wait_send()
            settled.append(copy)

    copies = [send(samples.at[:, (z + d) % 8], buf_a.at[z], line[d - 1]) for d in range(1, 8)]
    load_wigner.start()
    load_samples.wait()
    load_twiddle.wait()
    for copy in copies:
        copy.wait_recv()
    done = butterfly([(buf_a[n, 0], buf_a[n, 1]) for n in range(8)])
    re = jnp.concatenate([value[0] for value in done], axis=0).T
    im = jnp.concatenate([value[1] for value in done], axis=0).T
    factor = twiddle[v]
    cosine, sine = factor[0:1], factor[1:2]
    send_b[:, 0] = (re * cosine - im * sine).reshape(8, 16, 128)
    send_b[:, 1] = (re * sine + im * cosine).reshape(8, 16, 128)

    keep = pltpu.make_async_copy(send_b.at[v], buf_b.at[v], load_sem.at[5])
    keep.start()
    copies = [send(send_b.at[(v + d) % 8], buf_b.at[v], plane[d - 1]) for d in range(1, 8)]
    settle(7)
    load_step.wait()
    load_select.wait()
    keep.wait()
    for copy in copies:
        copy.wait_recv()
    done = butterfly([(buf_b[n, 0], buf_b[n, 1]) for n in range(8)])
    turned = []
    for k2 in range(8):
        re, im = done[k2]
        factor = twiddle[8 + k2]
        cosine, sine = factor[0:1], factor[1:2]
        turned.append(
            jnp.concatenate([re * cosine - im * sine, re * sine + im * cosine], axis=1)
        )
    values = jnp.concatenate(turned[0::2] + turned[1::2], axis=0)
    high = values.astype(BF16)
    low = (values - high.astype(F32)).astype(BF16)
    both = jnp.concatenate([high, low], axis=0)
    main = jnp.dot(both, step[0:256], preferred_element_type=F32)
    rest = jnp.dot(high, step[256:512], preferred_element_type=F32)
    spectrum = main[0:128] + (main[128:256] + rest)
    first_half = lax.broadcasted_iota(jnp.int32, (64, 128), 1) < 64
    for h in range(2):
        a = spectrum[0:64, 128 * h : 128 * h + 128]
        b = spectrum[64:128, 128 * h : 128 * h + 128]
        re = jnp.where(first_half, a, pltpu.roll(b, 64, 1))
        im = jnp.where(first_half, pltpu.roll(a, 64, 1), b)
        send_c[4 * h : 4 * h + 4, 0] = re.reshape(4, 16, 128)
        send_c[4 * h : 4 * h + 4, 1] = im.reshape(4, 16, 128)

    keep = pltpu.make_async_copy(send_c.at[v], buf_c.at[v], recv_c_sem.at[v])
    keep.start()
    for d in range(1, 8):
        semaphores = send_c_sem.at[d], recv_c_sem.at[v]
        send(send_c.at[(v + d) % 8], buf_c.at[v], plane[d - 1], semaphores)
    settle(7)

    def gathered(side):
        for block in range(4 * side, 4 * side + 4):
            pltpu.make_async_copy(buf_c.at[block], buf_c.at[block], recv_c_sem.at[block]).wait()
        cycles = [buf_c[4 * side : 4 * side + 4, part].reshape(64, 128) for part in range(2)]
        return jnp.concatenate(cycles, axis=0).T

    def stage(side, values):
        for e in range(2):
            send_d[side, :, 8 * e : 8 * e + 8] = values[64 * e : 64 * e + 64].reshape(8, 8, 128)

    lane = lax.broadcasted_iota(jnp.int32, (128, 128), 1)
    turned = jnp.take_along_axis(gathered(1), 63 - lane % 64 + lane // 64 * 64, axis=1)
    stage(1, turned)
    stage(0, gathered(0))
    keep = pltpu.make_async_copy(send_d.at[0, z], buf_d.at[0, z], recv_d_sem.at[0, 0])
    keep.start()
    for wave in range(2):
        for d in range(4 * wave, 4 * wave + 4):
            for side in (1, 0):
                if side or d:
                    to = far[d] if side else line[d - 1]
                    semaphores = send_d_sem.at[side, d], recv_d_sem.at[side, d]
                    send(send_d.at[side, (z + d) % 8], buf_d.at[side, z], to, semaphores)
        if wave == 0:
            settle()

    sign = (1 - 2 * z_hi).astype(F32)
    order = lax.broadcasted_iota(jnp.int32, (128, 128), 0) % 16

    def products(g):
        steps = (2 * g, 2 * g + 1)
        orders = [(z + 8 - d) % 8 for d in steps]
        for d, m in zip(steps, orders):
            for side in range(2):
                block = buf_d.at[side, m]
                pltpu.make_async_copy(block, block, recv_d_sem.at[side, d]).wait()
        own = jnp.concatenate([buf_d[0, m] for m in orders], axis=0)
        mirror = jnp.concatenate([buf_d[1, m] for m in orders], axis=0)
        even = (own + mirror).astype(BF16)
        odd = ((own - mirror) * sign).astype(BF16)
        even = jnp.dot(even, select[:, 0:256], preferred_element_type=F32)
        odd = jnp.dot(odd, select[:, 256:512], preferred_element_type=F32)
        rows = [
            side[16 * at : 16 * at + 16, 128 * part : 128 * part + 128]
            for at in range(2)
            for part in range(2)
            for side in (even, odd)
        ]
        rows = jnp.concatenate(rows, axis=0)
        total = jnp.zeros((128, 256), F32)
        for i in range(8):
            pair = [jnp.where(order == 2 * i + e, rows, 0.0).astype(BF16) for e in range(2)]
            weights = [wig[m, 256 * i : 256 * i + 256] for m in orders]
            total += jnp.dot(
                jnp.concatenate(pair, axis=1),
                jnp.concatenate(weights, axis=1),
                preferred_element_type=F32,
            )
        terms = jnp.concatenate([total[0:64, 0:128], total[64:128, 128:256]], axis=0).T
        half, at = g // 2, g % 2
        own_e[half, :, at] = terms.reshape(8, 16, 128)
        terms = terms.astype(BF16)
        for owner in range(8):
            rows = terms[16 * owner : 16 * owner + 16]
            send_e[half, owner % 4, owner // 4, at] = rows

    to_sum, to_add = [], []

    def spread_x(half):
        to_sum.append(
            [
                send(send_e.at[half, (x + d) % 4], buf_e.at[half, d - 1], ring[d - 1])
                for d in range(1, 4)
            ]
        )

    def total_of(half, owner):
        total = own_e[half, owner * 4 + x]
        for d in range(3):
            total += buf_e[half, d, owner].astype(F32)
        return total

    def sum_x(half):
        for copy in to_sum[half]:
            copy.wait_recv()
        send_f[half] = total_of(half, 1 - z_hi).astype(BF16)
        to_add.append(send(send_f.at[half], buf_f.at[half], far[0]))
        own_e[half, z_hi * 4 + x] = total_of(half, z_hi)

    def finish(g):
        half = g // 2
        if g % 2 == 0:
            to_add[half].wait_recv()
        total = own_e[half, z_hi * 4 + x, g % 2] + buf_f[half, g % 2].astype(F32)
        high = total.astype(BF16)
        left = total - high.astype(F32)
        middle = left.astype(BF16)
        low = (left - middle.astype(F32)).astype(BF16)
        placed = lax.dot_general(
            select[:, 512:896],
            jnp.concatenate([high, middle, low], axis=1),
            (((1,), (1,)), ((), ())),
            preferred_element_type=F32,
        )
        for at in range(2):
            for part in range(2):
                row = 64 * at + 32 * part
                out[part, (z + 8 - 2 * g - at) % 8] = placed[row : row + 32]

    load_wigner.wait()

    @pl.loop(0, 4)
    def _(g):
        products(g)

    spread_x(0)
    spread_x(1)
    settle(3)
    sum_x(0)
    sum_x(1)
    settle(2)
    finish(0)
    finish(1)
    finish(2)
    finish(3)
    settle()


def body(samples, wigner):
    twiddle, step, select = tables()
    anywhere = pl.BlockSpec(memory_space=pl.ANY)
    terms = pl.pallas_call(
        kernel,
        out_shape=jax.ShapeDtypeStruct((2, 8, 32, 16), F32),
        in_specs=[anywhere] * 5,
        out_specs=pl.BlockSpec(memory_space=pltpu.VMEM),
        scratch_shapes=[
            pltpu.VMEM((8, 2048, 128), BF16),
            pltpu.VMEM((512, 256), BF16),
            pltpu.VMEM((128, 896), BF16),
            pltpu.VMEM((16, 2, 128), F32),
            pltpu.VMEM((8, 2, 16, 128), F32),
            pltpu.VMEM((8, 2, 16, 128), F32),
            pltpu.VMEM((8, 2, 16, 128), F32),
            pltpu.VMEM((8, 2, 16, 128), F32),
            pltpu.VMEM((8, 2, 16, 128), F32),
            pltpu.VMEM((2, 8, 16, 128), F32),
            pltpu.VMEM((2, 8, 16, 128), F32),
            pltpu.VMEM((2, 8, 2, 16, 128), F32),
            pltpu.VMEM((2, 4, 2, 2, 16, 128), BF16),
            pltpu.VMEM((2, 3, 2, 2, 16, 128), BF16),
            pltpu.VMEM((2, 2, 16, 128), BF16),
            pltpu.VMEM((2, 2, 16, 128), BF16),
            pltpu.SemaphoreType.DMA((N_COPIES,)),
            pltpu.SemaphoreType.DMA((N_COPIES,)),
            pltpu.SemaphoreType.DMA((7,)),
            pltpu.SemaphoreType.DMA((8,)),
            pltpu.SemaphoreType.DMA((8,)),
            pltpu.SemaphoreType.DMA((2, 8)),
            pltpu.SemaphoreType.DMA((2, 8)),
        ],
        compiler_params=pltpu.CompilerParams(
            collective_id=0, has_side_effects=True, vmem_limit_bytes=60 * 1024 * 1024
        ),
    )(
        samples,
        wigner.reshape(8, 2048, 128),
        jnp.asarray(step),
        jnp.asarray(select),
        jnp.asarray(twiddle),
    )
    return terms.reshape(2, 8, 16, 2, 16)


def solution(mesh):
    return jax.shard_map(
        body,
        mesh=mesh,
        in_specs=(P(None, None, "wide", "beta"), P(None, "wide", "beta", None, None)),
        out_specs=P(None, None, "wide", None, "beta"),
        check_vma=False,
    )
```

```python
import math

import jax
import jax.numpy as jnp
import ml_dtypes
import numpy as np
from jax import lax
from jax.experimental import pallas as pl
from jax.experimental.pallas import tpu as pltpu
from jax.sharding import PartitionSpec as P

MESH = pl.DeviceIdType.MESH
BF16 = jnp.bfloat16
F32 = jnp.float32
N_COPIES = 44


def tables():
    lane = np.arange(128)
    k1, n3 = lane // 16, lane % 16
    rows = []
    for v in range(8):
        angle = 2 * math.pi * ((16 * v + n3) * k1 % 1024) / 1024
        rows.append(np.stack([np.cos(angle), -np.sin(angle)]) / 32)
    for k2 in range(8):
        angle = 2 * math.pi * (n3 * k2 % 128) / 128
        rows.append(np.stack([np.cos(angle), -np.sin(angle)]))
    twiddle = np.stack(rows).astype(np.float32)

    step = np.zeros((2, 8, 16, 2, 2, 8, 8))
    three = np.arange(16)
    for first in range(8):
        for h in range(2):
            for z in range(8):
                angle = 2 * math.pi * (three * (2 * z + h) % 16) / 16
                cosine, sine = np.cos(angle), np.sin(angle)
                step[0, first, :, h, 0, z, first] = cosine
                step[0, first, :, h, 1, z, first] = -sine
                step[1, first, :, h, 0, z, first] = sine
                step[1, first, :, h, 1, z, first] = cosine
    step = step.reshape(256, 256)
    high = step.astype(ml_dtypes.bfloat16)
    low = (step - high.astype(np.float64)).astype(ml_dtypes.bfloat16)
    step = np.concatenate([high, low])

    place = np.zeros((4, 16, 2, 3, 4, 2, 16))
    for block in range(4):
        for k in range(16):
            for parity in range(2):
                place[block, k, parity, :, block, parity, k] = 1
    return twiddle, step, place.reshape(128, 384).astype(ml_dtypes.bfloat16)


def turn(value, eighths):
    re, im = value
    root = math.sqrt(0.5)
    if eighths == 0:
        return value
    if eighths == 1:
        return (re + im) * root, (im - re) * root
    if eighths == 2:
        return im, -re
    return (im - re) * root, -(re + im) * root


def butterfly(values):
    count = len(values)
    if count == 1:
        return values
    even, odd = butterfly(values[0::2]), butterfly(values[1::2])
    low, high = [], []
    for k in range(count // 2):
        a, b = even[k], turn(odd[k], k * 8 // count)
        low.append((a[0] + b[0], a[1] + b[1]))
        high.append((a[0] - b[0], a[1] - b[1]))
    return low + high


def kernel(
    samples_hbm, wigner, step_hbm, place_hbm, twiddle_hbm, out,
    samples, wig, step, place, twiddle, send_a, buf_a, send_b, buf_b, send_c, buf_c, send_d, buf_d,
    own_e, send_e, buf_e, send_f, buf_f, send_sem, recv_sem, load_sem,
):
    wide, beta = lax.axis_index("wide"), lax.axis_index("beta")
    z, v = wide // 8, wide % 8
    z_hi, x = beta // 4, beta % 4
    other = (beta + 4) % 8

    load_samples = pltpu.make_async_copy(samples_hbm, samples, load_sem.at[0])
    load_twiddle = pltpu.make_async_copy(twiddle_hbm, twiddle, load_sem.at[1])
    load_step = pltpu.make_async_copy(step_hbm, step, load_sem.at[2])
    load_place = pltpu.make_async_copy(place_hbm, place, load_sem.at[3])
    load_wigner = pltpu.make_async_copy(wigner, wig, load_sem.at[4])
    load_samples.start()

    line = [(((z + d) % 8) * 8 + v, beta) for d in range(1, 8)]
    far = [(((z + d) % 8) * 8 + v, other) for d in range(8)]
    plane = [(z * 8 + (v + d) % 8, beta) for d in range(1, 8)]
    ring = [(wide, z_hi * 4 + (x + d) % 4) for d in range(1, 4)]
    peers = far + line + plane + ring
    barrier = pltpu.get_barrier_semaphore()
    for at_wide, at_beta in peers:
        pl.semaphore_signal(
            barrier, inc=1, device_id={"wide": at_wide, "beta": at_beta}, device_id_type=MESH
        )
    for load in (load_twiddle, load_step, load_place):
        load.start()

    lane = lax.broadcasted_iota(jnp.int32, (16, 128), 1)
    load_samples.wait()
    for m in range(8):
        re, im = samples[0, m], samples[1, m]
        send_a[0, m] = jnp.where(lane < 64, re, pltpu.roll(im, 64, 1))
        flipped = [
            jnp.take_along_axis(part, jnp.where(lane < 64, 127 - lane, 191 - lane), axis=1)
            for part in (re, im)
        ]
        send_a[1, m] = jnp.where(lane < 64, *flipped)
    pl.semaphore_wait(barrier, len(peers))

    sent, settled = [], []

    def send(source, target, to):
        slot = len(sent)
        copy = pltpu.make_async_remote_copy(
            src_ref=source,
            dst_ref=target,
            send_sem=send_sem.at[slot],
            recv_sem=recv_sem.at[slot],
            device_id={"wide": to[0], "beta": to[1]},
            device_id_type=MESH,
        )
        copy.start()
        sent.append(copy)
        return copy

    def settle(in_flight=0):
        for copy in sent[len(settled) : len(sent) - in_flight]:
            copy.wait_send()
            settled.append(copy)

    keep = pltpu.make_async_copy(send_a.at[0, z], buf_a.at[0, z], load_sem.at[5])
    keep.start()
    copies = [send(send_a.at[1, z], buf_a.at[1, z], far[0])]
    for d in range(1, 8):
        to = (z + d) % 8
        copies.append(send(send_a.at[1, to], buf_a.at[1, z], far[d]))
        copies.append(send(send_a.at[0, to], buf_a.at[0, z], line[d - 1]))
    load_wigner.start()
    load_twiddle.wait()
    keep.wait()
    for copy in copies:
        copy.wait_recv()
    sign = (1 - 2 * z_hi).astype(F32)
    own_factor = jnp.where(lane % 2 == 0, 1.0, sign)
    mirror_factor = jnp.where(lane % 2 == 0, 1.0, -sign)

    def mixed(n, part):
        own, mirror = [
            jnp.take_along_axis(buf_a[side, n], lane // 2 + 64 * part, axis=1) for side in range(2)
        ]
        return own * own_factor + mirror * mirror_factor

    done = butterfly([(mixed(n, 0), mixed(n, 1)) for n in range(8)])
    re = jnp.concatenate([value[0] for value in done], axis=0).T
    im = jnp.concatenate([value[1] for value in done], axis=0).T
    factor = twiddle[v]
    cosine, sine = factor[0:1], factor[1:2]
    send_b[:, 0] = (re * cosine - im * sine).reshape(8, 16, 128)
    send_b[:, 1] = (re * sine + im * cosine).reshape(8, 16, 128)

    keep = pltpu.make_async_copy(send_b.at[v], buf_b.at[v], load_sem.at[6])
    keep.start()
    copies = [send(send_b.at[(v + d) % 8], buf_b.at[v], plane[d - 1]) for d in range(1, 8)]
    settle(7)
    load_step.wait()
    load_place.wait()
    keep.wait()
    for copy in copies:
        copy.wait_recv()
    done = butterfly([(buf_b[n, 0], buf_b[n, 1]) for n in range(8)])
    turned = []
    for k2 in range(8):
        re, im = done[k2]
        factor = twiddle[8 + k2]
        cosine, sine = factor[0:1], factor[1:2]
        turned.append(
            jnp.concatenate([re * cosine - im * sine, re * sine + im * cosine], axis=1)
        )
    values = jnp.concatenate(turned[0::2] + turned[1::2], axis=0)
    high = values.astype(BF16)
    low = (values - high.astype(F32)).astype(BF16)
    both = jnp.concatenate([high, low], axis=0)
    main = jnp.dot(both, step[0:256], preferred_element_type=F32)
    rest = jnp.dot(high, step[256:512], preferred_element_type=F32)
    spectrum = main[0:128] + (main[128:256] + rest)
    first_half = lax.broadcasted_iota(jnp.int32, (64, 128), 1) < 64
    for h in range(2):
        a = spectrum[0:64, 128 * h : 128 * h + 128]
        b = spectrum[64:128, 128 * h : 128 * h + 128]
        re = jnp.where(first_half, a, pltpu.roll(b, 64, 1))
        im = jnp.where(first_half, pltpu.roll(a, 64, 1), b)
        send_c[4 * h : 4 * h + 4, 0] = re.astype(BF16).reshape(4, 16, 128)
        send_c[4 * h : 4 * h + 4, 1] = im.astype(BF16).reshape(4, 16, 128)

    keep = pltpu.make_async_copy(send_c.at[v], buf_c.at[v], load_sem.at[7])
    keep.start()
    copies = [send(send_c.at[(v + d) % 8], buf_c.at[v], plane[d - 1]) for d in range(1, 8)]
    settle(7)
    keep.wait()
    for copy in copies:
        copy.wait_recv()
    for part in range(2):
        values = buf_c[:, part].reshape(128, 128).astype(F32).T
        values = [values[64 * e : 64 * e + 64].reshape(8, 8, 128) for e in range(2)]
        send_d[:, part] = jnp.concatenate(values, axis=1).astype(BF16)

    arrivals = [pltpu.make_async_copy(send_d.at[z], buf_d.at[z], load_sem.at[8])]
    arrivals[0].start()
    arrivals += [send(send_d.at[(z + d) % 8], buf_d.at[z], line[d - 1]) for d in range(1, 8)]

    row = lax.broadcasted_iota(jnp.int32, (128, 128), 0)
    lane = lax.broadcasted_iota(jnp.int32, (128, 128), 1)
    order, fits = row % 16, lane % 2 == row // 16 % 2
    to_sum, to_add = [], []

    def products(g):
        steps = (2 * g, 2 * g + 1)
        orders = [(z + 8 - d) % 8 for d in steps]
        for d in steps:
            if d == 0:
                arrivals[d].wait()
            else:
                arrivals[d].wait_recv()
        rows = [buf_d[m, part].astype(F32) for m in orders for part in (0, 0, 1, 1)]
        rows = jnp.where(fits, jnp.concatenate(rows, axis=0), 0.0)
        total = jnp.zeros((128, 256), F32)
        for i in range(8):
            pair = [jnp.where(order == 2 * i + e, rows, 0.0).astype(BF16) for e in range(2)]
            weights = [wig[m, 256 * i : 256 * i + 256] for m in orders]
            total += jnp.dot(
                jnp.concatenate(pair, axis=1),
                jnp.concatenate(weights, axis=1),
                preferred_element_type=F32,
            )
        terms = jnp.concatenate([total[0:64, 0:128], total[64:128, 128:256]], axis=0).T
        own_e[g // 2, :, g % 2] = terms.reshape(8, 16, 128)
        terms = terms.astype(BF16)
        for owner in range(8):
            rows = terms[16 * owner : 16 * owner + 16]
            send_e[g // 2, owner % 4, owner // 4, g % 2] = rows

    def spread_x(half):
        to_sum.append(
            [
                send(send_e.at[half, (x + d) % 4], buf_e.at[half, d - 1], ring[d - 1])
                for d in range(1, 4)
            ]
        )

    def total_of(half, owner):
        total = own_e[half, owner * 4 + x]
        for d in range(3):
            total += buf_e[half, d, owner].astype(F32)
        return total

    def sum_x(half):
        for copy in to_sum[half]:
            copy.wait_recv()
        send_f[half] = total_of(half, 1 - z_hi).astype(BF16)
        to_add.append(send(send_f.at[half], buf_f.at[half], far[0]))
        own_e[half, z_hi * 4 + x] = total_of(half, z_hi)

    def finish(g):
        half = g // 2
        if g % 2 == 0:
            to_add[half].wait_recv()
        total = own_e[half, z_hi * 4 + x, g % 2] + buf_f[half, g % 2].astype(F32)
        high = total.astype(BF16)
        left = total - high.astype(F32)
        middle = left.astype(BF16)
        low = (left - middle.astype(F32)).astype(BF16)
        placed = lax.dot_general(
            place[...],
            jnp.concatenate([high, middle, low], axis=1),
            (((1,), (1,)), ((), ())),
            preferred_element_type=F32,
        )
        for at in range(2):
            for part in range(2):
                row = 64 * at + 32 * part
                out[part, (z + 8 - 2 * g - at) % 8] = placed[row : row + 32]

    load_wigner.wait()
    products(0)
    products(1)
    spread_x(0)
    products(2)
    products(3)
    spread_x(1)
    settle(3)
    sum_x(0)
    sum_x(1)
    settle(2)
    finish(0)
    finish(1)
    finish(2)
    finish(3)
    settle()


def body(samples, wigner):
    twiddle, step, place = tables()
    anywhere = pl.BlockSpec(memory_space=pl.ANY)
    terms = pl.pallas_call(
        kernel,
        out_shape=jax.ShapeDtypeStruct((2, 8, 32, 16), F32),
        in_specs=[anywhere] * 5,
        out_specs=pl.BlockSpec(memory_space=pltpu.VMEM),
        scratch_shapes=[
            pltpu.VMEM((2, 8, 16, 128), F32),
            pltpu.VMEM((8, 2048, 128), BF16),
            pltpu.VMEM((512, 256), BF16),
            pltpu.VMEM((128, 384), BF16),
            pltpu.VMEM((16, 2, 128), F32),
            pltpu.VMEM((2, 8, 16, 128), F32),
            pltpu.VMEM((2, 8, 16, 128), F32),
            pltpu.VMEM((8, 2, 16, 128), F32),
            pltpu.VMEM((8, 2, 16, 128), F32),
            pltpu.VMEM((8, 2, 16, 128), BF16),
            pltpu.VMEM((8, 2, 16, 128), BF16),
            pltpu.VMEM((8, 2, 16, 128), BF16),
            pltpu.VMEM((8, 2, 16, 128), BF16),
            pltpu.VMEM((2, 8, 2, 16, 128), F32),
            pltpu.VMEM((2, 4, 2, 2, 16, 128), BF16),
            pltpu.VMEM((2, 3, 2, 2, 16, 128), BF16),
            pltpu.VMEM((2, 2, 16, 128), BF16),
            pltpu.VMEM((2, 2, 16, 128), BF16),
            pltpu.SemaphoreType.DMA((N_COPIES,)),
            pltpu.SemaphoreType.DMA((N_COPIES,)),
            pltpu.SemaphoreType.DMA((9,)),
        ],
        compiler_params=pltpu.CompilerParams(
            collective_id=0, has_side_effects=True, vmem_limit_bytes=60 * 1024 * 1024
        ),
    )(
        samples,
        wigner.reshape(8, 2048, 128),
        jnp.asarray(step),
        jnp.asarray(place),
        jnp.asarray(twiddle),
    )
    return terms.reshape(2, 8, 16, 2, 16)


def solution(mesh):
    return jax.shard_map(
        body,
        mesh=mesh,
        in_specs=(P(None, None, "wide", "beta"), P(None, "wide", "beta", None, None)),
        out_specs=P(None, None, "wide", None, "beta"),
        check_vma=False,
    )
```

```python
import math

import jax
import jax.numpy as jnp
import ml_dtypes
import numpy as np
from jax import lax
from jax.experimental import pallas as pl
from jax.experimental.pallas import tpu as pltpu
from jax.sharding import PartitionSpec as P

MESH = pl.DeviceIdType.MESH
BF16 = jnp.bfloat16
F32 = jnp.float32
N_COPIES = 40


def tables():
    lane = np.arange(128)
    k1, n3 = lane // 16, lane % 16
    rows = []
    for v in range(8):
        angle = 2 * math.pi * ((16 * v + n3) * k1 % 1024) / 1024
        rows.append(np.stack([np.cos(angle), -np.sin(angle)]) / 32)
    for k2 in range(8):
        angle = 2 * math.pi * (n3 * k2 % 128) / 128
        rows.append(np.stack([np.cos(angle), -np.sin(angle)]))
    twiddle = np.stack(rows).astype(np.float32)

    step = np.zeros((2, 8, 16, 2, 2, 8, 8))
    three = np.arange(16)
    for first in range(8):
        for h in range(2):
            for z in range(8):
                angle = 2 * math.pi * (three * (2 * z + h) % 16) / 16
                cosine, sine = np.cos(angle), np.sin(angle)
                step[0, first, :, h, 0, z, first] = cosine
                step[0, first, :, h, 1, z, first] = -sine
                step[1, first, :, h, 0, z, first] = sine
                step[1, first, :, h, 1, z, first] = cosine
    step = step.reshape(256, 256)
    high = step.astype(ml_dtypes.bfloat16)
    low = (step - high.astype(np.float64)).astype(ml_dtypes.bfloat16)
    step = np.concatenate([high, low])

    place = np.zeros((4, 16, 2, 3, 4, 2, 16))
    for block in range(4):
        for k in range(16):
            for parity in range(2):
                place[block, k, parity, :, block, parity, k] = 1
    return twiddle, step, place.reshape(128, 384).astype(ml_dtypes.bfloat16)


def turn(value, eighths):
    re, im = value
    root = math.sqrt(0.5)
    if eighths == 0:
        return value
    if eighths == 1:
        return (re + im) * root, (im - re) * root
    if eighths == 2:
        return im, -re
    return (im - re) * root, -(re + im) * root


def butterfly(values):
    count = len(values)
    if count == 1:
        return values
    even, odd = butterfly(values[0::2]), butterfly(values[1::2])
    low, high = [], []
    for k in range(count // 2):
        a, b = even[k], turn(odd[k], k * 8 // count)
        low.append((a[0] + b[0], a[1] + b[1]))
        high.append((a[0] - b[0], a[1] - b[1]))
    return low + high


def kernel(
    samples_hbm, wigner, step_hbm, place_hbm, twiddle_hbm, out,
    samples, wig, step, place, twiddle, send_a, buf_a, send_b, buf_b, send_c, buf_c, send_d, buf_d,
    own_e, send_e, buf_e, send_f, buf_f, send_sem, recv_sem, load_sem,
):
    wide, beta = lax.axis_index("wide"), lax.axis_index("beta")
    z, v = wide // 8, wide % 8
    z_hi, x = beta // 4, beta % 4
    other = (beta + 4) % 8

    load_samples = pltpu.make_async_copy(samples_hbm, samples, load_sem.at[0])
    load_twiddle = pltpu.make_async_copy(twiddle_hbm, twiddle, load_sem.at[1])
    load_step = pltpu.make_async_copy(step_hbm, step, load_sem.at[2])
    load_place = pltpu.make_async_copy(place_hbm, place, load_sem.at[3])
    load_wigner = pltpu.make_async_copy(wigner, wig, load_sem.at[4])
    load_samples.start()

    line = [(((z + d) % 8) * 8 + v, beta) for d in range(1, 8)]
    far = [(((z + d) % 8) * 8 + v, other) for d in range(8)]
    plane = [(z * 8 + (v + d) % 8, beta) for d in range(1, 8)]
    ring = [(wide, z_hi * 4 + (x + d) % 4) for d in range(1, 4)]
    peers = far + line + plane + ring
    barrier = pltpu.get_barrier_semaphore()
    for at_wide, at_beta in peers:
        pl.semaphore_signal(
            barrier, inc=1, device_id={"wide": at_wide, "beta": at_beta}, device_id_type=MESH
        )
    for load in (load_twiddle, load_step, load_place):
        load.start()

    lane = lax.broadcasted_iota(jnp.int32, (16, 128), 1)
    first = lane % 2 == 0
    load_samples.wait()
    for m in range(8):
        for side in range(2):
            cycle = 127 - lane // 2 if side else lane // 2
            re, im = [jnp.take_along_axis(samples[part, m], cycle, axis=1) for part in range(2)]
            send_a[side, m] = jnp.where(first, re, im)
    pl.semaphore_wait(barrier, len(peers))

    sent, settled = [], []

    def send(source, target, to):
        slot = len(sent)
        copy = pltpu.make_async_remote_copy(
            src_ref=source,
            dst_ref=target,
            send_sem=send_sem.at[slot],
            recv_sem=recv_sem.at[slot],
            device_id={"wide": to[0], "beta": to[1]},
            device_id_type=MESH,
        )
        copy.start()
        sent.append(copy)
        return copy

    def settle(in_flight=0):
        for copy in sent[len(settled) : len(sent) - in_flight]:
            copy.wait_send()
            settled.append(copy)

    keep = pltpu.make_async_copy(send_a.at[0, z], buf_a.at[0, z], load_sem.at[5])
    keep.start()
    copies = [send(send_a.at[1, z], buf_a.at[1, z], far[0])]
    for d in range(1, 8):
        to = (z + d) % 8
        copies.append(send(send_a.at[1, to], buf_a.at[1, z], far[d]))
        copies.append(send(send_a.at[0, to], buf_a.at[0, z], line[d - 1]))
    load_wigner.start()
    load_twiddle.wait()
    keep.wait()
    for copy in copies:
        copy.wait_recv()
    sign = (1 - 2 * z_hi).astype(F32)
    values = []
    for n in range(8):
        own, mirror = buf_a[0, n], buf_a[1, n]
        even, odd = own + mirror, (own - mirror) * sign
        re = jnp.where(first, even, pltpu.roll(odd, 1, 1))
        im = jnp.where(first, pltpu.roll(even, 127, 1), odd)
        values.append((re, im))
    done = butterfly(values)
    re = jnp.concatenate([value[0] for value in done], axis=0).T
    im = jnp.concatenate([value[1] for value in done], axis=0).T
    factor = twiddle[v]
    cosine, sine = factor[0:1], factor[1:2]
    send_b[:, 0] = (re * cosine - im * sine).reshape(8, 16, 128)
    send_b[:, 1] = (re * sine + im * cosine).reshape(8, 16, 128)

    keep = pltpu.make_async_copy(send_b.at[v], buf_b.at[v], load_sem.at[6])
    keep.start()
    copies = [send(send_b.at[(v + d) % 8], buf_b.at[v], plane[d - 1]) for d in range(1, 8)]
    settle(7)
    load_step.wait()
    load_place.wait()
    keep.wait()
    for copy in copies:
        copy.wait_recv()
    done = butterfly([(buf_b[n, 0], buf_b[n, 1]) for n in range(8)])
    turned = []
    for k2 in range(8):
        re, im = done[k2]
        factor = twiddle[8 + k2]
        cosine, sine = factor[0:1], factor[1:2]
        turned.append(
            jnp.concatenate([re * cosine - im * sine, re * sine + im * cosine], axis=1)
        )
    values = jnp.concatenate(turned[0::2] + turned[1::2], axis=0)
    high = values.astype(BF16)
    low = (values - high.astype(F32)).astype(BF16)
    both = jnp.concatenate([high, low], axis=0)
    main = jnp.dot(both, step[0:256], preferred_element_type=F32)
    rest = jnp.dot(high, step[256:512], preferred_element_type=F32)
    spectrum = main[0:128] + (main[128:256] + rest)
    first_half = lax.broadcasted_iota(jnp.int32, (64, 128), 1) < 64
    for h in range(2):
        a = spectrum[0:64, 128 * h : 128 * h + 128]
        b = spectrum[64:128, 128 * h : 128 * h + 128]
        re = jnp.where(first_half, a, pltpu.roll(b, 64, 1))
        im = jnp.where(first_half, pltpu.roll(a, 64, 1), b)
        send_c[4 * h : 4 * h + 4, 0] = re.astype(BF16).reshape(4, 16, 128)
        send_c[4 * h : 4 * h + 4, 1] = im.astype(BF16).reshape(4, 16, 128)

    keep = pltpu.make_async_copy(send_c.at[v], buf_c.at[v], load_sem.at[7])
    keep.start()
    copies = [send(send_c.at[(v + d) % 8], buf_c.at[v], plane[d - 1]) for d in range(1, 8)]
    settle(7)
    keep.wait()
    for copy in copies:
        copy.wait_recv()
    for part in range(2):
        values = buf_c[:, part].reshape(128, 128).astype(F32).T
        values = [values[64 * e : 64 * e + 64].reshape(8, 8, 128) for e in range(2)]
        send_d[:, part] = jnp.concatenate(values, axis=1).astype(BF16)

    arrivals = [pltpu.make_async_copy(send_d.at[z], buf_d.at[z], load_sem.at[8])]
    arrivals[0].start()
    arrivals += [send(send_d.at[(z + d) % 8], buf_d.at[z], line[d - 1]) for d in range(1, 8)]

    row = lax.broadcasted_iota(jnp.int32, (128, 128), 0)
    lane = lax.broadcasted_iota(jnp.int32, (128, 128), 1)
    order, fits = row % 16, lane % 2 == row // 16 % 2

    def products(g):
        steps = (2 * g, 2 * g + 1)
        orders = [(z + 8 - d) % 8 for d in steps]
        for d in steps:
            if d == 0:
                arrivals[d].wait()
            else:
                arrivals[d].wait_recv()
        rows = [buf_d[m, part].astype(F32) for m in orders for part in (0, 0, 1, 1)]
        rows = jnp.where(fits, jnp.concatenate(rows, axis=0), 0.0)
        total = jnp.zeros((128, 256), F32)
        for i in range(8):
            pair = [jnp.where(order == 2 * i + e, rows, 0.0).astype(BF16) for e in range(2)]
            weights = [wig[m, 256 * i : 256 * i + 256] for m in orders]
            total += jnp.dot(
                jnp.concatenate(pair, axis=1),
                jnp.concatenate(weights, axis=1),
                preferred_element_type=F32,
            )
        terms = jnp.concatenate([total[0:64, 0:128], total[64:128, 128:256]], axis=0).T
        own_e[:, g] = terms.reshape(8, 16, 128)
        terms = terms.astype(BF16)
        for owner in range(8):
            send_e[owner % 4, owner // 4, g] = terms[16 * owner : 16 * owner + 16]

    def total_of(owner):
        total = own_e[owner * 4 + x]
        for d in range(3):
            total += buf_e[d, owner].astype(F32)
        return total

    load_wigner.wait()
    for g in range(4):
        products(g)

    copies = [send(send_e.at[(x + d) % 4], buf_e.at[d - 1], ring[d - 1]) for d in range(1, 4)]
    settle(3)
    for copy in copies:
        copy.wait_recv()

    send_f[...] = total_of(1 - z_hi).astype(BF16)
    copy = send(send_f, buf_f, far[0])
    mine = total_of(z_hi)
    settle(1)
    copy.wait_recv()
    total = mine + buf_f[...].astype(F32)
    high = total.astype(BF16)
    left = total - high.astype(F32)
    middle = left.astype(BF16)
    low = (left - middle.astype(F32)).astype(BF16)
    total = jnp.concatenate([high, middle, low], axis=2)
    for g in range(4):
        rows = lax.dot_general(
            place[...], total[g], (((1,), (1,)), ((), ())), preferred_element_type=F32
        )
        for at in range(2):
            for part in range(2):
                row = 64 * at + 32 * part
                out[part, (z + 8 - 2 * g - at) % 8] = rows[row : row + 32]
    settle()


def body(samples, wigner):
    twiddle, step, place = tables()
    anywhere = pl.BlockSpec(memory_space=pl.ANY)
    terms = pl.pallas_call(
        kernel,
        out_shape=jax.ShapeDtypeStruct((2, 8, 32, 16), F32),
        in_specs=[anywhere] * 5,
        out_specs=pl.BlockSpec(memory_space=pltpu.VMEM),
        scratch_shapes=[
            pltpu.VMEM((2, 8, 16, 128), F32),
            pltpu.VMEM((8, 2048, 128), BF16),
            pltpu.VMEM((512, 256), BF16),
            pltpu.VMEM((128, 384), BF16),
            pltpu.VMEM((16, 2, 128), F32),
            pltpu.VMEM((2, 8, 16, 128), F32),
            pltpu.VMEM((2, 8, 16, 128), F32),
            pltpu.VMEM((8, 2, 16, 128), F32),
            pltpu.VMEM((8, 2, 16, 128), F32),
            pltpu.VMEM((8, 2, 16, 128), BF16),
            pltpu.VMEM((8, 2, 16, 128), BF16),
            pltpu.VMEM((8, 2, 16, 128), BF16),
            pltpu.VMEM((8, 2, 16, 128), BF16),
            pltpu.VMEM((8, 4, 16, 128), F32),
            pltpu.VMEM((4, 2, 4, 16, 128), BF16),
            pltpu.VMEM((3, 2, 4, 16, 128), BF16),
            pltpu.VMEM((4, 16, 128), BF16),
            pltpu.VMEM((4, 16, 128), BF16),
            pltpu.SemaphoreType.DMA((N_COPIES,)),
            pltpu.SemaphoreType.DMA((N_COPIES,)),
            pltpu.SemaphoreType.DMA((9,)),
        ],
        compiler_params=pltpu.CompilerParams(
            collective_id=0, has_side_effects=True, vmem_limit_bytes=60 * 1024 * 1024
        ),
    )(
        samples,
        wigner.reshape(8, 2048, 128),
        jnp.asarray(step),
        jnp.asarray(place),
        jnp.asarray(twiddle),
    )
    return terms.reshape(2, 8, 16, 2, 16)


def solution(mesh):
    return jax.shard_map(
        body,
        mesh=mesh,
        in_specs=(P(None, None, "wide", "beta"), P(None, "wide", "beta", None, None)),
        out_specs=P(None, None, "wide", None, "beta"),
        check_vma=False,
    )
```

```python
import math

import jax
import jax.numpy as jnp
import ml_dtypes
import numpy as np
from jax import lax
from jax.experimental import pallas as pl
from jax.experimental.pallas import tpu as pltpu
from jax.sharding import PartitionSpec as P

MESH = pl.DeviceIdType.MESH
BF16 = jnp.bfloat16
F32 = jnp.float32
N_COPIES = 40


def tables():
    lane = np.arange(128)
    k1, n3 = lane // 16, lane % 16
    rows = []
    for v in range(8):
        angle = 2 * math.pi * ((16 * v + n3) * k1 % 1024) / 1024
        rows.append(np.stack([np.cos(angle), -np.sin(angle)]) / 32)
    for k2 in range(8):
        angle = 2 * math.pi * (n3 * k2 % 128) / 128
        rows.append(np.stack([np.cos(angle), -np.sin(angle)]))
    twiddle = np.stack(rows).astype(np.float32)

    step = np.zeros((2, 8, 16, 2, 2, 8, 8))
    three = np.arange(16)
    for first in range(8):
        for h in range(2):
            for z in range(8):
                angle = 2 * math.pi * (three * (2 * z + h) % 16) / 16
                cosine, sine = np.cos(angle), np.sin(angle)
                step[0, first, :, h, 0, z, first] = cosine
                step[0, first, :, h, 1, z, first] = -sine
                step[1, first, :, h, 0, z, first] = sine
                step[1, first, :, h, 1, z, first] = cosine
    step = step.reshape(256, 256)
    high = step.astype(ml_dtypes.bfloat16)
    low = (step - high.astype(np.float64)).astype(ml_dtypes.bfloat16)
    step = np.concatenate([high, low])

    place = np.zeros((2, 2, 8, 2, 2, 3, 8, 2, 2, 2, 2))
    for m, part, half, low, parity in np.ndindex(2, 2, 8, 2, 2):
        place[m, part, half, low, parity, :, half, parity, low, m, part] = 1
    return twiddle, step, place.reshape(128, 384).astype(ml_dtypes.bfloat16)


def turn(value, eighths):
    re, im = value
    root = math.sqrt(0.5)
    if eighths == 0:
        return value
    if eighths == 1:
        return (re + im) * root, (im - re) * root
    if eighths == 2:
        return im, -re
    return (im - re) * root, -(re + im) * root


def butterfly(values):
    count = len(values)
    if count == 1:
        return values
    even, odd = butterfly(values[0::2]), butterfly(values[1::2])
    low, high = [], []
    for k in range(count // 2):
        a, b = even[k], turn(odd[k], k * 8 // count)
        low.append((a[0] + b[0], a[1] + b[1]))
        high.append((a[0] - b[0], a[1] - b[1]))
    return low + high


def kernel(
    samples_hbm, wigner, step_hbm, place_hbm, twiddle_hbm, out,
    samples, wig, step, place, twiddle, send_a, buf_a, send_b, buf_b, send_c, buf_c, send_d, buf_d,
    gathered, own_e, send_e, buf_e, send_f, buf_f, send_sem, recv_sem, load_sem,
):
    wide, beta = lax.axis_index("wide"), lax.axis_index("beta")
    z, v = wide // 8, wide % 8
    z_hi, x = beta // 4, beta % 4
    other = (beta + 4) % 8

    load_samples = pltpu.make_async_copy(samples_hbm, samples, load_sem.at[0])
    load_twiddle = pltpu.make_async_copy(twiddle_hbm, twiddle, load_sem.at[1])
    load_step = pltpu.make_async_copy(step_hbm, step, load_sem.at[2])
    load_place = pltpu.make_async_copy(place_hbm, place, load_sem.at[3])
    load_wigner = pltpu.make_async_copy(wigner, wig, load_sem.at[4])
    load_samples.start()

    line = [(((z + d) % 8) * 8 + v, beta) for d in range(1, 8)]
    far = [(((z + d) % 8) * 8 + v, other) for d in range(8)]
    plane = [(z * 8 + (v + d) % 8, beta) for d in range(1, 8)]
    ring = [(wide, z_hi * 4 + (x + d) % 4) for d in range(1, 4)]
    peers = far + line + plane + ring
    barrier = pltpu.get_barrier_semaphore()
    for at_wide, at_beta in peers:
        pl.semaphore_signal(
            barrier, inc=1, device_id={"wide": at_wide, "beta": at_beta}, device_id_type=MESH
        )
    for load in (load_twiddle, load_step, load_place):
        load.start()

    lane = lax.broadcasted_iota(jnp.int32, (16, 128), 1)
    first = lane % 2 == 0
    load_samples.wait()
    for m in range(8):
        for side in range(2):
            cycle = 127 - lane // 2 if side else lane // 2
            re, im = [jnp.take_along_axis(samples[part, m], cycle, axis=1) for part in range(2)]
            send_a[side, m] = jnp.where(first, re, im)
    pl.semaphore_wait(barrier, len(peers))

    sent, settled = [], []

    def send(source, target, to):
        slot = len(sent)
        copy = pltpu.make_async_remote_copy(
            src_ref=source,
            dst_ref=target,
            send_sem=send_sem.at[slot],
            recv_sem=recv_sem.at[slot],
            device_id={"wide": to[0], "beta": to[1]},
            device_id_type=MESH,
        )
        copy.start()
        sent.append(copy)
        return copy

    def settle(in_flight=0):
        for copy in sent[len(settled) : len(sent) - in_flight]:
            copy.wait_send()
            settled.append(copy)

    keep = pltpu.make_async_copy(send_a.at[0, z], buf_a.at[0, z], load_sem.at[5])
    keep.start()
    copies = [send(send_a.at[1, z], buf_a.at[1, z], far[0])]
    for d in range(1, 8):
        to = (z + d) % 8
        copies.append(send(send_a.at[1, to], buf_a.at[1, z], far[d]))
        copies.append(send(send_a.at[0, to], buf_a.at[0, z], line[d - 1]))
    load_wigner.start()
    load_twiddle.wait()
    keep.wait()
    for copy in copies:
        copy.wait_recv()
    sign = (1 - 2 * z_hi).astype(F32)
    values = []
    for n in range(8):
        own, mirror = buf_a[0, n], buf_a[1, n]
        even, odd = own + mirror, (own - mirror) * sign
        re = jnp.where(first, even, pltpu.roll(odd, 1, 1))
        im = jnp.where(first, pltpu.roll(even, 127, 1), odd)
        values.append((re, im))
    done = butterfly(values)
    re = jnp.concatenate([value[0] for value in done], axis=0).T
    im = jnp.concatenate([value[1] for value in done], axis=0).T
    factor = twiddle[v]
    cosine, sine = factor[0:1], factor[1:2]
    send_b[:, 0] = (re * cosine - im * sine).reshape(8, 16, 128)
    send_b[:, 1] = (re * sine + im * cosine).reshape(8, 16, 128)

    keep = pltpu.make_async_copy(send_b.at[v], buf_b.at[v], load_sem.at[6])
    keep.start()
    copies = [send(send_b.at[(v + d) % 8], buf_b.at[v], plane[d - 1]) for d in range(1, 8)]
    settle(7)
    load_step.wait()
    load_place.wait()
    keep.wait()
    for copy in copies:
        copy.wait_recv()
    done = butterfly([(buf_b[n, 0], buf_b[n, 1]) for n in range(8)])
    turned = []
    for k2 in range(8):
        re, im = done[k2]
        factor = twiddle[8 + k2]
        cosine, sine = factor[0:1], factor[1:2]
        turned.append(
            jnp.concatenate([re * cosine - im * sine, re * sine + im * cosine], axis=1)
        )
    values = jnp.concatenate(turned[0::2] + turned[1::2], axis=0)
    high = values.astype(BF16)
    low = (values - high.astype(F32)).astype(BF16)
    both = jnp.concatenate([high, low], axis=0)
    main = jnp.dot(both, step[0:256], preferred_element_type=F32)
    rest = jnp.dot(high, step[256:512], preferred_element_type=F32)
    spectrum = main[0:128] + (main[128:256] + rest)
    first_half = lax.broadcasted_iota(jnp.int32, (64, 128), 1) < 64
    for h in range(2):
        a = spectrum[0:64, 128 * h : 128 * h + 128]
        b = spectrum[64:128, 128 * h : 128 * h + 128]
        re = jnp.where(first_half, a, pltpu.roll(b, 64, 1))
        im = jnp.where(first_half, pltpu.roll(a, 64, 1), b)
        send_c[4 * h : 4 * h + 4, 0] = re.astype(BF16).reshape(4, 16, 128)
        send_c[4 * h : 4 * h + 4, 1] = im.astype(BF16).reshape(4, 16, 128)

    keep = pltpu.make_async_copy(send_c.at[v], buf_c.at[v], load_sem.at[7])
    keep.start()
    copies = [send(send_c.at[(v + d) % 8], buf_c.at[v], plane[d - 1]) for d in range(1, 8)]
    settle(7)
    keep.wait()
    for copy in copies:
        copy.wait_recv()
    for part in range(2):
        values = buf_c[:, part].reshape(128, 128).astype(F32).T
        values = [values[64 * e : 64 * e + 64].reshape(8, 8, 128) for e in range(2)]
        send_d[:, part] = jnp.concatenate(values, axis=1).astype(BF16)

    arrivals = [pltpu.make_async_copy(send_d.at[z], buf_d.at[z], load_sem.at[8])]
    arrivals[0].start()
    arrivals += [send(send_d.at[(z + d) % 8], buf_d.at[z], line[d - 1]) for d in range(1, 8)]

    row = lax.broadcasted_iota(jnp.int32, (8, 128), 0)
    lane = lax.broadcasted_iota(jnp.int32, (8, 128), 1)
    fits = [[(lane % 2 == parity) & (row // 4 == low) for low in range(2)] for parity in range(2)]
    second = lax.broadcasted_iota(jnp.int32, (16, 128), 0) // 2 % 2 == 1

    def products(g):
        steps = (2 * g, 2 * g + 1)
        orders = [(z + 8 - d) % 8 for d in steps]
        for d in steps:
            if d == 0:
                arrivals[d].wait()
            else:
                arrivals[d].wait_recv()
        for at, m in enumerate(orders):
            for part in range(2):
                gathered[g, pl.ds(2 * at + part, 16, stride=4)] = buf_d[m, part].astype(F32)
        terms = []
        for i in range(8):
            rows = gathered[g, 8 * i : 8 * i + 8]
            pairs = [
                jnp.concatenate([jnp.where(fit, rows, 0.0) for fit in parity], axis=1)
                for parity in fits
            ]
            weights = [wig[m, 256 * i : 256 * i + 256] for m in orders]
            both = jnp.dot(
                jnp.concatenate(pairs, axis=0).astype(BF16),
                jnp.concatenate(weights, axis=1),
                preferred_element_type=F32,
            )
            terms.append(jnp.where(second, both[:, 128:256], both[:, 0:128]))
        terms = jnp.concatenate(terms, axis=0).T
        own_e[:, g] = terms.reshape(8, 16, 128)
        terms = terms.astype(BF16)
        for owner in range(8):
            send_e[owner % 4, owner // 4, g] = terms[16 * owner : 16 * owner + 16]

    def total_of(owner):
        total = own_e[owner * 4 + x]
        for d in range(3):
            total += buf_e[d, owner].astype(F32)
        return total

    load_wigner.wait()
    for g in range(4):
        products(g)

    copies = [send(send_e.at[(x + d) % 4], buf_e.at[d - 1], ring[d - 1]) for d in range(1, 4)]
    settle(3)
    for copy in copies:
        copy.wait_recv()

    send_f[...] = total_of(1 - z_hi).astype(BF16)
    copy = send(send_f, buf_f, far[0])
    mine = total_of(z_hi)
    settle(1)
    copy.wait_recv()
    total = mine + buf_f[...].astype(F32)
    high = total.astype(BF16)
    left = total - high.astype(F32)
    middle = left.astype(BF16)
    low = (left - middle.astype(F32)).astype(BF16)
    total = jnp.concatenate([high, middle, low], axis=2)
    for g in range(4):
        rows = lax.dot_general(
            place[...], total[g], (((1,), (1,)), ((), ())), preferred_element_type=F32
        )
        for at in range(2):
            for part in range(2):
                row = 64 * at + 32 * part
                out[part, (z + 8 - 2 * g - at) % 8] = rows[row : row + 32]
    settle()


def body(samples, wigner):
    twiddle, step, place = tables()
    anywhere = pl.BlockSpec(memory_space=pl.ANY)
    terms = pl.pallas_call(
        kernel,
        out_shape=jax.ShapeDtypeStruct((2, 8, 32, 16), F32),
        in_specs=[anywhere] * 5,
        out_specs=pl.BlockSpec(memory_space=pltpu.VMEM),
        scratch_shapes=[
            pltpu.VMEM((2, 8, 16, 128), F32),
            pltpu.VMEM((8, 2048, 128), BF16),
            pltpu.VMEM((512, 256), BF16),
            pltpu.VMEM((128, 384), BF16),
            pltpu.VMEM((16, 2, 128), F32),
            pltpu.VMEM((2, 8, 16, 128), F32),
            pltpu.VMEM((2, 8, 16, 128), F32),
            pltpu.VMEM((8, 2, 16, 128), F32),
            pltpu.VMEM((8, 2, 16, 128), F32),
            pltpu.VMEM((8, 2, 16, 128), BF16),
            pltpu.VMEM((8, 2, 16, 128), BF16),
            pltpu.VMEM((8, 2, 16, 128), BF16),
            pltpu.VMEM((8, 2, 16, 128), BF16),
            pltpu.VMEM((4, 64, 128), F32),
            pltpu.VMEM((8, 4, 16, 128), F32),
            pltpu.VMEM((4, 2, 4, 16, 128), BF16),
            pltpu.VMEM((3, 2, 4, 16, 128), BF16),
            pltpu.VMEM((4, 16, 128), BF16),
            pltpu.VMEM((4, 16, 128), BF16),
            pltpu.SemaphoreType.DMA((N_COPIES,)),
            pltpu.SemaphoreType.DMA((N_COPIES,)),
            pltpu.SemaphoreType.DMA((9,)),
        ],
        compiler_params=pltpu.CompilerParams(
            collective_id=0, has_side_effects=True, vmem_limit_bytes=60 * 1024 * 1024
        ),
    )(
        samples,
        wigner.reshape(8, 2048, 128),
        jnp.asarray(step),
        jnp.asarray(place),
        jnp.asarray(twiddle),
    )
    return terms.reshape(2, 8, 16, 2, 16)


def solution(mesh):
    return jax.shard_map(
        body,
        mesh=mesh,
        in_specs=(P(None, None, "wide", "beta"), P(None, "wide", "beta", None, None)),
        out_specs=P(None, None, "wide", None, "beta"),
        check_vma=False,
    )
```

```python
import math

import jax
import jax.numpy as jnp
import ml_dtypes
import numpy as np
from jax import lax
from jax.experimental import pallas as pl
from jax.experimental.pallas import tpu as pltpu
from jax.sharding import PartitionSpec as P

MESH = pl.DeviceIdType.MESH
BF16 = jnp.bfloat16
F32 = jnp.float32
N_COPIES = 40


def tables():
    lane = np.arange(128)
    k1, n3 = lane // 16, lane % 16
    rows = []
    for v in range(8):
        angle = 2 * math.pi * ((16 * v + n3) * k1 % 1024) / 1024
        rows.append(np.stack([np.cos(angle), -np.sin(angle)]) / 32)
    for k2 in range(8):
        angle = 2 * math.pi * (n3 * k2 % 128) / 128
        rows.append(np.stack([np.cos(angle), -np.sin(angle)]))
    twiddle = np.stack(rows).astype(np.float32)

    step = np.zeros((2, 8, 16, 2, 2, 8, 8))
    three = np.arange(16)
    for first in range(8):
        for h in range(2):
            for z in range(8):
                angle = 2 * math.pi * (three * (2 * z + h) % 16) / 16
                cosine, sine = np.cos(angle), np.sin(angle)
                step[0, first, :, h, 0, z, first] = cosine
                step[0, first, :, h, 1, z, first] = -sine
                step[1, first, :, h, 0, z, first] = sine
                step[1, first, :, h, 1, z, first] = cosine
    step = step.reshape(256, 256)
    high = step.astype(ml_dtypes.bfloat16)
    low = (step - high.astype(np.float64)).astype(ml_dtypes.bfloat16)
    step = np.concatenate([high, low])

    place = np.zeros((2, 2, 8, 2, 2, 3, 8, 2, 2, 2, 2))
    for m, part, half, low, parity in np.ndindex(2, 2, 8, 2, 2):
        place[m, part, half, low, parity, :, half, parity, low, m, part] = 1
    return twiddle, step, place.reshape(128, 384).astype(ml_dtypes.bfloat16)


def turn(value, eighths):
    re, im = value
    root = math.sqrt(0.5)
    if eighths == 0:
        return value
    if eighths == 1:
        return (re + im) * root, (im - re) * root
    if eighths == 2:
        return im, -re
    return (im - re) * root, -(re + im) * root


def butterfly(values):
    count = len(values)
    if count == 1:
        return values
    even, odd = butterfly(values[0::2]), butterfly(values[1::2])
    low, high = [], []
    for k in range(count // 2):
        a, b = even[k], turn(odd[k], k * 8 // count)
        low.append((a[0] + b[0], a[1] + b[1]))
        high.append((a[0] - b[0], a[1] - b[1]))
    return low + high


def kernel(
    samples_hbm, wigner, step_hbm, place_hbm, twiddle_hbm, out,
    samples, wig, step, place, twiddle, send_a, buf_a, send_b, buf_b, send_c, buf_c, send_d, buf_d,
    gathered, own_e, send_e, buf_e, send_f, buf_f, send_sem, recv_sem, load_sem, wigner_sem,
):
    wide, beta = lax.axis_index("wide"), lax.axis_index("beta")
    z, v = wide // 8, wide % 8
    z_hi, x = beta // 4, beta % 4
    other = (beta + 4) % 8

    load_samples = pltpu.make_async_copy(samples_hbm, samples, load_sem.at[0])
    load_twiddle = pltpu.make_async_copy(twiddle_hbm, twiddle, load_sem.at[1])
    load_step = pltpu.make_async_copy(step_hbm, step, load_sem.at[2])
    load_place = pltpu.make_async_copy(place_hbm, place, load_sem.at[3])
    load_wigner = [
        pltpu.make_async_copy(wigner.at[m], wig.at[m], wigner_sem.at[m]) for m in range(8)
    ]
    load_samples.start()

    line = [(((z + d) % 8) * 8 + v, beta) for d in range(1, 8)]
    far = [(((z + d) % 8) * 8 + v, other) for d in range(8)]
    plane = [(z * 8 + (v + d) % 8, beta) for d in range(1, 8)]
    ring = [(wide, z_hi * 4 + (x + d) % 4) for d in range(1, 4)]
    peers = far + line + plane + ring
    barrier = pltpu.get_barrier_semaphore()
    for at_wide, at_beta in peers:
        pl.semaphore_signal(
            barrier, inc=1, device_id={"wide": at_wide, "beta": at_beta}, device_id_type=MESH
        )
    for load in (load_twiddle, load_step, load_place, *load_wigner):
        load.start()

    lane = lax.broadcasted_iota(jnp.int32, (16, 128), 1)
    first = lane % 2 == 0
    load_samples.wait()
    for m in range(8):
        for side in range(2):
            cycle = 127 - lane // 2 if side else lane // 2
            re, im = [jnp.take_along_axis(samples[part, m], cycle, axis=1) for part in range(2)]
            send_a[side, m] = jnp.where(first, re, im)
    pl.semaphore_wait(barrier, len(peers))

    sent, settled = [], []

    def send(source, target, to):
        slot = len(sent)
        copy = pltpu.make_async_remote_copy(
            src_ref=source,
            dst_ref=target,
            send_sem=send_sem.at[slot],
            recv_sem=recv_sem.at[slot],
            device_id={"wide": to[0], "beta": to[1]},
            device_id_type=MESH,
        )
        copy.start()
        sent.append(copy)
        return copy

    def settle(in_flight=0):
        for copy in sent[len(settled) : len(sent) - in_flight]:
            copy.wait_send()
            settled.append(copy)

    keep = pltpu.make_async_copy(send_a.at[0, z], buf_a.at[0, z], load_sem.at[5])
    keep.start()
    copies = [send(send_a.at[1, z], buf_a.at[1, z], far[0])]
    for d in range(1, 8):
        to = (z + d) % 8
        copies.append(send(send_a.at[1, to], buf_a.at[1, z], far[d]))
        copies.append(send(send_a.at[0, to], buf_a.at[0, z], line[d - 1]))
    load_twiddle.wait()
    keep.wait()
    for copy in copies:
        copy.wait_recv()
    sign = (1 - 2 * z_hi).astype(F32)
    values = []
    for n in range(8):
        own, mirror = buf_a[0, n], buf_a[1, n]
        even, odd = own + mirror, (own - mirror) * sign
        re = jnp.where(first, even, pltpu.roll(odd, 1, 1))
        im = jnp.where(first, pltpu.roll(even, 127, 1), odd)
        values.append((re, im))
    done = butterfly(values)
    re = jnp.concatenate([value[0] for value in done], axis=0).T
    im = jnp.concatenate([value[1] for value in done], axis=0).T
    factor = twiddle[v]
    cosine, sine = factor[0:1], factor[1:2]
    send_b[:, 0] = (re * cosine - im * sine).reshape(8, 16, 128)
    send_b[:, 1] = (re * sine + im * cosine).reshape(8, 16, 128)

    keep = pltpu.make_async_copy(send_b.at[v], buf_b.at[v], load_sem.at[6])
    keep.start()
    copies = [send(send_b.at[(v + d) % 8], buf_b.at[v], plane[d - 1]) for d in range(1, 8)]
    settle(7)
    load_step.wait()
    load_place.wait()
    keep.wait()
    for copy in copies:
        copy.wait_recv()
    done = butterfly([(buf_b[n, 0], buf_b[n, 1]) for n in range(8)])
    turned = []
    for k2 in range(8):
        re, im = done[k2]
        factor = twiddle[8 + k2]
        cosine, sine = factor[0:1], factor[1:2]
        turned.append(
            jnp.concatenate([re * cosine - im * sine, re * sine + im * cosine], axis=1)
        )
    values = jnp.concatenate(turned[0::2] + turned[1::2], axis=0)
    high = values.astype(BF16)
    low = (values - high.astype(F32)).astype(BF16)
    both = jnp.concatenate([high, low], axis=0)
    main = jnp.dot(both, step[0:256], preferred_element_type=F32)
    rest = jnp.dot(high, step[256:512], preferred_element_type=F32)
    spectrum = main[0:128] + (main[128:256] + rest)
    first_half = lax.broadcasted_iota(jnp.int32, (64, 128), 1) < 64
    for h in range(2):
        a = spectrum[0:64, 128 * h : 128 * h + 128]
        b = spectrum[64:128, 128 * h : 128 * h + 128]
        re = jnp.where(first_half, a, pltpu.roll(b, 64, 1))
        im = jnp.where(first_half, pltpu.roll(a, 64, 1), b)
        send_c[4 * h : 4 * h + 4, 0] = re.astype(BF16).reshape(4, 16, 128)
        send_c[4 * h : 4 * h + 4, 1] = im.astype(BF16).reshape(4, 16, 128)

    keep = pltpu.make_async_copy(send_c.at[v], buf_c.at[v], load_sem.at[7])
    keep.start()
    copies = [send(send_c.at[(v + d) % 8], buf_c.at[v], plane[d - 1]) for d in range(1, 8)]
    settle(7)
    keep.wait()
    for copy in copies:
        copy.wait_recv()
    for part in range(2):
        values = buf_c[:, part].reshape(128, 128).astype(F32).T
        values = [values[64 * e : 64 * e + 64].reshape(8, 8, 128) for e in range(2)]
        send_d[:, part] = jnp.concatenate(values, axis=1).astype(BF16)

    arrivals = [pltpu.make_async_copy(send_d.at[z], buf_d.at[z], load_sem.at[8])]
    arrivals[0].start()
    arrivals += [send(send_d.at[(z + d) % 8], buf_d.at[z], line[d - 1]) for d in range(1, 8)]

    row = lax.broadcasted_iota(jnp.int32, (8, 128), 0)
    lane = lax.broadcasted_iota(jnp.int32, (8, 128), 1)
    fits = [[(lane % 2 == parity) & (row // 4 == low) for low in range(2)] for parity in range(2)]
    second = lax.broadcasted_iota(jnp.int32, (16, 128), 0) // 2 % 2 == 1

    def products(g):
        steps = (2 * g, 2 * g + 1)
        orders = [(z + 8 - d) % 8 for d in steps]
        for d in steps:
            if d == 0:
                arrivals[d].wait()
            else:
                arrivals[d].wait_recv()
        for at, m in enumerate(orders):
            pltpu.make_async_copy(wigner.at[m], wig.at[m], wigner_sem.at[m]).wait()
            for part in range(2):
                gathered[g, pl.ds(2 * at + part, 16, stride=4)] = buf_d[m, part].astype(F32)
        terms = []
        for i in range(8):
            rows = gathered[g, 8 * i : 8 * i + 8]
            pairs = [
                jnp.concatenate([jnp.where(fit, rows, 0.0) for fit in parity], axis=1)
                for parity in fits
            ]
            weights = [wig[m, 256 * i : 256 * i + 256] for m in orders]
            both = jnp.dot(
                jnp.concatenate(pairs, axis=0).astype(BF16),
                jnp.concatenate(weights, axis=1),
                preferred_element_type=F32,
            )
            terms.append(jnp.where(second, both[:, 128:256], both[:, 0:128]))
        terms = jnp.concatenate(terms, axis=0).T
        own_e[:, g] = terms.reshape(8, 16, 128)
        terms = terms.astype(BF16)
        for owner in range(8):
            send_e[owner % 4, owner // 4, g] = terms[16 * owner : 16 * owner + 16]

    def total_of(owner):
        total = own_e[owner * 4 + x]
        for d in range(3):
            total += buf_e[d, owner].astype(F32)
        return total

    for g in range(4):
        products(g)

    copies = [send(send_e.at[(x + d) % 4], buf_e.at[d - 1], ring[d - 1]) for d in range(1, 4)]
    settle(3)
    for copy in copies:
        copy.wait_recv()

    send_f[...] = total_of(1 - z_hi).astype(BF16)
    copy = send(send_f, buf_f, far[0])
    mine = total_of(z_hi)
    settle(1)
    copy.wait_recv()
    total = mine + buf_f[...].astype(F32)
    high = total.astype(BF16)
    left = total - high.astype(F32)
    middle = left.astype(BF16)
    low = (left - middle.astype(F32)).astype(BF16)
    total = jnp.concatenate([high, middle, low], axis=2)
    for g in range(4):
        rows = lax.dot_general(
            place[...], total[g], (((1,), (1,)), ((), ())), preferred_element_type=F32
        )
        for at in range(2):
            for part in range(2):
                row = 64 * at + 32 * part
                out[part, (z + 8 - 2 * g - at) % 8] = rows[row : row + 32]
    settle()


def body(samples, wigner):
    twiddle, step, place = tables()
    anywhere = pl.BlockSpec(memory_space=pl.ANY)
    terms = pl.pallas_call(
        kernel,
        out_shape=jax.ShapeDtypeStruct((2, 8, 32, 16), F32),
        in_specs=[anywhere] * 5,
        out_specs=pl.BlockSpec(memory_space=pltpu.VMEM),
        scratch_shapes=[
            pltpu.VMEM((2, 8, 16, 128), F32),
            pltpu.VMEM((8, 2048, 128), BF16),
            pltpu.VMEM((512, 256), BF16),
            pltpu.VMEM((128, 384), BF16),
            pltpu.VMEM((16, 2, 128), F32),
            pltpu.VMEM((2, 8, 16, 128), F32),
            pltpu.VMEM((2, 8, 16, 128), F32),
            pltpu.VMEM((8, 2, 16, 128), F32),
            pltpu.VMEM((8, 2, 16, 128), F32),
            pltpu.VMEM((8, 2, 16, 128), BF16),
            pltpu.VMEM((8, 2, 16, 128), BF16),
            pltpu.VMEM((8, 2, 16, 128), BF16),
            pltpu.VMEM((8, 2, 16, 128), BF16),
            pltpu.VMEM((4, 64, 128), F32),
            pltpu.VMEM((8, 4, 16, 128), F32),
            pltpu.VMEM((4, 2, 4, 16, 128), BF16),
            pltpu.VMEM((3, 2, 4, 16, 128), BF16),
            pltpu.VMEM((4, 16, 128), BF16),
            pltpu.VMEM((4, 16, 128), BF16),
            pltpu.SemaphoreType.DMA((N_COPIES,)),
            pltpu.SemaphoreType.DMA((N_COPIES,)),
            pltpu.SemaphoreType.DMA((9,)),
            pltpu.SemaphoreType.DMA((8,)),
        ],
        compiler_params=pltpu.CompilerParams(
            collective_id=0, has_side_effects=True, vmem_limit_bytes=60 * 1024 * 1024
        ),
    )(
        samples,
        wigner.reshape(8, 2048, 128),
        jnp.asarray(step),
        jnp.asarray(place),
        jnp.asarray(twiddle),
    )
    return terms.reshape(2, 8, 16, 2, 16)


def solution(mesh):
    return jax.shard_map(
        body,
        mesh=mesh,
        in_specs=(P(None, None, "wide", "beta"), P(None, "wide", "beta", None, None)),
        out_specs=P(None, None, "wide", None, "beta"),
        check_vma=False,
    )
```

```python
import math

import jax
import jax.numpy as jnp
import ml_dtypes
import numpy as np
from jax import lax
from jax.experimental import pallas as pl
from jax.experimental.pallas import tpu as pltpu
from jax.sharding import PartitionSpec as P

MESH = pl.DeviceIdType.MESH
BF16 = jnp.bfloat16
F32 = jnp.float32


def tables():
    lane = np.arange(128)
    k1, n3 = lane // 16, lane % 16
    rows = []
    for v in range(8):
        angle = 2 * math.pi * ((16 * v + n3) * k1 % 1024) / 1024
        rows.append(np.stack([np.cos(angle), -np.sin(angle)]) / 32)
    for k2 in range(8):
        angle = 2 * math.pi * (n3 * k2 % 128) / 128
        rows.append(np.stack([np.cos(angle), -np.sin(angle)]))
    twiddle = np.stack(rows).astype(np.float32)

    step = np.zeros((2, 8, 16, 2, 2, 8, 8))
    three = np.arange(16)
    for first in range(8):
        for h in range(2):
            for z in range(8):
                angle = 2 * math.pi * (three * (2 * z + h) % 16) / 16
                cosine, sine = np.cos(angle), np.sin(angle)
                step[0, first, :, h, 0, z, first] = cosine
                step[0, first, :, h, 1, z, first] = -sine
                step[1, first, :, h, 0, z, first] = sine
                step[1, first, :, h, 1, z, first] = cosine
    step = step.reshape(256, 256)
    high = step.astype(ml_dtypes.bfloat16)
    low = (step - high.astype(np.float64)).astype(ml_dtypes.bfloat16)
    step = np.concatenate([high, low])

    place = np.zeros((2, 2, 8, 2, 2, 3, 8, 2, 2, 2, 2))
    for m, part, half, low, parity in np.ndindex(2, 2, 8, 2, 2):
        place[m, part, half, low, parity, :, half, parity, low, m, part] = 1
    return twiddle, step, place.reshape(128, 384).astype(ml_dtypes.bfloat16)


def turn(value, eighths):
    re, im = value
    root = math.sqrt(0.5)
    if eighths == 0:
        return value
    if eighths == 1:
        return (re + im) * root, (im - re) * root
    if eighths == 2:
        return im, -re
    return (im - re) * root, -(re + im) * root


def butterfly(values):
    count = len(values)
    if count == 1:
        return values
    even, odd = butterfly(values[0::2]), butterfly(values[1::2])
    low, high = [], []
    for k in range(count // 2):
        a, b = even[k], turn(odd[k], k * 8 // count)
        low.append((a[0] + b[0], a[1] + b[1]))
        high.append((a[0] - b[0], a[1] - b[1]))
    return low + high


def kernel(
    samples_hbm, wigner, step_hbm, place_hbm, twiddle_hbm, out,
    samples, wig, step, place, twiddle, send_a, buf_a, send_b, buf_b, send_c, buf_c, send_d, buf_d,
    gathered, own_e, send_e, buf_e, send_f, buf_f, send_sem, recv_sem, recv_d_sem, load_sem, wigner_sem,
):
    wide, beta = lax.axis_index("wide"), lax.axis_index("beta")
    z, v = wide // 8, wide % 8
    z_hi, x = beta // 4, beta % 4
    other = (beta + 4) % 8

    load_samples = pltpu.make_async_copy(samples_hbm, samples, load_sem.at[0])
    load_twiddle = pltpu.make_async_copy(twiddle_hbm, twiddle, load_sem.at[1])
    load_step = pltpu.make_async_copy(step_hbm, step, load_sem.at[2])
    load_place = pltpu.make_async_copy(place_hbm, place, load_sem.at[3])
    load_wigner = [
        pltpu.make_async_copy(wigner.at[m], wig.at[m], wigner_sem.at[m]) for m in range(8)
    ]
    load_samples.start()

    line = [(((z + d) % 8) * 8 + v, beta) for d in range(1, 8)]
    far = [(((z + d) % 8) * 8 + v, other) for d in range(8)]
    plane = [(z * 8 + (v + d) % 8, beta) for d in range(1, 8)]
    ring = [(wide, z_hi * 4 + (x + d) % 4) for d in range(1, 4)]
    peers = far + line + plane + ring
    barrier = pltpu.get_barrier_semaphore()
    for at_wide, at_beta in peers:
        pl.semaphore_signal(
            barrier, inc=1, device_id={"wide": at_wide, "beta": at_beta}, device_id_type=MESH
        )
    for load in (load_twiddle, load_step, load_place, *load_wigner):
        load.start()

    lane = lax.broadcasted_iota(jnp.int32, (16, 128), 1)
    first = lane % 2 == 0
    load_samples.wait()
    for m in range(8):
        for side in range(2):
            cycle = 127 - lane // 2 if side else lane // 2
            re, im = [jnp.take_along_axis(samples[part, m], cycle, axis=1) for part in range(2)]
            send_a[8 * side + m] = jnp.where(first, re, im)
    pl.semaphore_wait(barrier, len(peers))

    def send(source, target, to, sent, arrived):
        pltpu.make_async_remote_copy(
            src_ref=source,
            dst_ref=target,
            send_sem=sent,
            recv_sem=arrived,
            device_id={"wide": to[0], "beta": to[1]},
            device_id_type=MESH,
        ).start()

    def wait(block, semaphore):
        pltpu.make_async_copy(block, block, semaphore).wait()

    pltpu.make_async_copy(send_a.at[z], buf_a.at[z], recv_sem.at[0]).start()
    send(send_a.at[8 + z], buf_a.at[8 + z], far[0], send_sem.at[0], recv_sem.at[0])
    for to_hi in (1, 0):
        side = 1 - z_hi if to_hi else z_hi
        for d in range(1, 8):
            to = (z + d) % 8
            send(
                send_a.at[8 * side + to],
                buf_a.at[8 * side + z],
                (8 * to + v, 4 * to_hi + x),
                send_sem.at[0],
                recv_sem.at[0],
            )
    load_twiddle.wait()
    wait(buf_a, recv_sem.at[0])
    sign = (1 - 2 * z_hi).astype(F32)
    values = []
    for n in range(8):
        own, mirror = buf_a[n], buf_a[8 + n]
        even, odd = own + mirror, (own - mirror) * sign
        re = jnp.where(first, even, pltpu.roll(odd, 1, 1))
        im = jnp.where(first, pltpu.roll(even, 127, 1), odd)
        values.append((re, im))
    done = butterfly(values)
    re = jnp.concatenate([value[0] for value in done], axis=0).T
    im = jnp.concatenate([value[1] for value in done], axis=0).T
    factor = twiddle[v]
    cosine, sine = factor[0:1], factor[1:2]
    send_b[:, 0] = (re * cosine - im * sine).reshape(8, 16, 128)
    send_b[:, 1] = (re * sine + im * cosine).reshape(8, 16, 128)

    pltpu.make_async_copy(send_b.at[v], buf_b.at[v], recv_sem.at[1]).start()
    for d in range(1, 8):
        source, target = send_b.at[(v + d) % 8], buf_b.at[v]
        send(source, target, plane[d - 1], send_sem.at[1], recv_sem.at[1])
    wait(send_a.at[pl.ds(0, 15)], send_sem.at[0])
    load_step.wait()
    load_place.wait()
    wait(buf_b, recv_sem.at[1])
    done = butterfly([(buf_b[n, 0], buf_b[n, 1]) for n in range(8)])
    turned = []
    for k2 in range(8):
        re, im = done[k2]
        factor = twiddle[8 + k2]
        cosine, sine = factor[0:1], factor[1:2]
        turned.append(
            jnp.concatenate([re * cosine - im * sine, re * sine + im * cosine], axis=1)
        )
    values = jnp.concatenate(turned[0::2] + turned[1::2], axis=0)
    high = values.astype(BF16)
    low = (values - high.astype(F32)).astype(BF16)
    both = jnp.concatenate([high, low], axis=0)
    main = jnp.dot(both, step[0:256], preferred_element_type=F32)
    rest = jnp.dot(high, step[256:512], preferred_element_type=F32)
    spectrum = main[0:128] + (main[128:256] + rest)
    first_half = lax.broadcasted_iota(jnp.int32, (64, 128), 1) < 64
    for h in range(2):
        a = spectrum[0:64, 128 * h : 128 * h + 128]
        b = spectrum[64:128, 128 * h : 128 * h + 128]
        re = jnp.where(first_half, a, pltpu.roll(b, 64, 1))
        im = jnp.where(first_half, pltpu.roll(a, 64, 1), b)
        send_c[4 * h : 4 * h + 4, 0] = re.astype(BF16).reshape(4, 16, 128)
        send_c[4 * h : 4 * h + 4, 1] = im.astype(BF16).reshape(4, 16, 128)

    pltpu.make_async_copy(send_c.at[v], buf_c.at[v], recv_sem.at[2]).start()
    for d in range(1, 8):
        source, target = send_c.at[(v + d) % 8], buf_c.at[v]
        send(source, target, plane[d - 1], send_sem.at[2], recv_sem.at[2])
    wait(send_b.at[pl.ds(0, 7)], send_sem.at[1])
    wait(buf_c, recv_sem.at[2])
    for part in range(2):
        values = buf_c[:, part].reshape(128, 128).astype(F32).T
        values = [values[64 * e : 64 * e + 64].reshape(8, 8, 128) for e in range(2)]
        send_d[:, part] = jnp.concatenate(values, axis=1).astype(BF16)

    pltpu.make_async_copy(send_d.at[z], buf_d.at[z], recv_d_sem.at[0]).start()
    for d in range(1, 8):
        source, target = send_d.at[(z + d) % 8], buf_d.at[z]
        send(source, target, line[d - 1], send_sem.at[3], recv_d_sem.at[d])
    wait(send_c.at[pl.ds(0, 7)], send_sem.at[2])

    row = lax.broadcasted_iota(jnp.int32, (8, 128), 0)
    lane = lax.broadcasted_iota(jnp.int32, (8, 128), 1)
    fits = [[(lane % 2 == parity) & (row // 4 == low) for low in range(2)] for parity in range(2)]
    second = lax.broadcasted_iota(jnp.int32, (16, 128), 0) // 2 % 2 == 1

    def products(g):
        steps = (2 * g, 2 * g + 1)
        orders = [(z + 8 - d) % 8 for d in steps]
        for d, m in zip(steps, orders):
            wait(buf_d.at[m], recv_d_sem.at[d])
        for at, m in enumerate(orders):
            pltpu.make_async_copy(wigner.at[m], wig.at[m], wigner_sem.at[m]).wait()
            for part in range(2):
                gathered[g, pl.ds(2 * at + part, 16, stride=4)] = buf_d[m, part].astype(F32)
        terms = []
        for i in range(8):
            rows = gathered[g, 8 * i : 8 * i + 8]
            pairs = [
                jnp.concatenate([jnp.where(fit, rows, 0.0) for fit in parity], axis=1)
                for parity in fits
            ]
            weights = [wig[m, 256 * i : 256 * i + 256] for m in orders]
            both = jnp.dot(
                jnp.concatenate(pairs, axis=0).astype(BF16),
                jnp.concatenate(weights, axis=1),
                preferred_element_type=F32,
            )
            terms.append(jnp.where(second, both[:, 128:256], both[:, 0:128]))
        terms = jnp.concatenate(terms, axis=0).T
        own_e[:, g] = terms.reshape(8, 16, 128)
        terms = terms.astype(BF16)
        for owner in range(8):
            send_e[owner % 4, owner // 4, g] = terms[16 * owner : 16 * owner + 16]

    def total_of(owner):
        total = own_e[owner * 4 + x]
        for d in range(3):
            total += buf_e[d, owner].astype(F32)
        return total

    for g in range(4):
        products(g)

    for d in range(1, 4):
        source, target = send_e.at[(x + d) % 4], buf_e.at[d - 1]
        send(source, target, ring[d - 1], send_sem.at[4], recv_sem.at[3])
    wait(send_d.at[pl.ds(0, 7)], send_sem.at[3])
    wait(buf_e, recv_sem.at[3])

    send_f[...] = total_of(1 - z_hi).astype(BF16)
    send(send_f, buf_f, far[0], send_sem.at[5], recv_sem.at[4])
    mine = total_of(z_hi)
    wait(send_e.at[pl.ds(0, 3)], send_sem.at[4])
    wait(buf_f, recv_sem.at[4])
    total = mine + buf_f[...].astype(F32)
    high = total.astype(BF16)
    left = total - high.astype(F32)
    middle = left.astype(BF16)
    low = (left - middle.astype(F32)).astype(BF16)
    total = jnp.concatenate([high, middle, low], axis=2)
    for g in range(4):
        rows = lax.dot_general(
            place[...], total[g], (((1,), (1,)), ((), ())), preferred_element_type=F32
        )
        for at in range(2):
            for part in range(2):
                row = 64 * at + 32 * part
                out[part, (z + 8 - 2 * g - at) % 8] = rows[row : row + 32]
    wait(send_f, send_sem.at[5])


def body(samples, wigner):
    twiddle, step, place = tables()
    anywhere = pl.BlockSpec(memory_space=pl.ANY)
    terms = pl.pallas_call(
        kernel,
        out_shape=jax.ShapeDtypeStruct((2, 8, 32, 16), F32),
        in_specs=[anywhere] * 5,
        out_specs=pl.BlockSpec(memory_space=pltpu.VMEM),
        scratch_shapes=[
            pltpu.VMEM((2, 8, 16, 128), F32),
            pltpu.VMEM((8, 2048, 128), BF16),
            pltpu.VMEM((512, 256), BF16),
            pltpu.VMEM((128, 384), BF16),
            pltpu.VMEM((16, 2, 128), F32),
            pltpu.VMEM((16, 16, 128), F32),
            pltpu.VMEM((16, 16, 128), F32),
            pltpu.VMEM((8, 2, 16, 128), F32),
            pltpu.VMEM((8, 2, 16, 128), F32),
            pltpu.VMEM((8, 2, 16, 128), BF16),
            pltpu.VMEM((8, 2, 16, 128), BF16),
            pltpu.VMEM((8, 2, 16, 128), BF16),
            pltpu.VMEM((8, 2, 16, 128), BF16),
            pltpu.VMEM((4, 64, 128), F32),
            pltpu.VMEM((8, 4, 16, 128), F32),
            pltpu.VMEM((4, 2, 4, 16, 128), BF16),
            pltpu.VMEM((3, 2, 4, 16, 128), BF16),
            pltpu.VMEM((4, 16, 128), BF16),
            pltpu.VMEM((4, 16, 128), BF16),
            pltpu.SemaphoreType.DMA((6,)),
            pltpu.SemaphoreType.DMA((5,)),
            pltpu.SemaphoreType.DMA((8,)),
            pltpu.SemaphoreType.DMA((4,)),
            pltpu.SemaphoreType.DMA((8,)),
        ],
        compiler_params=pltpu.CompilerParams(
            collective_id=0, has_side_effects=True, vmem_limit_bytes=60 * 1024 * 1024
        ),
    )(
        samples,
        wigner.reshape(8, 2048, 128),
        jnp.asarray(step),
        jnp.asarray(place),
        jnp.asarray(twiddle),
    )
    return terms.reshape(2, 8, 16, 2, 16)


def solution(mesh):
    return jax.shard_map(
        body,
        mesh=mesh,
        in_specs=(P(None, None, "wide", "beta"), P(None, "wide", "beta", None, None)),
        out_specs=P(None, None, "wide", None, "beta"),
        check_vma=False,
    )
```

```python
import math

import jax
import jax.numpy as jnp
import ml_dtypes
import numpy as np
from jax import lax
from jax.experimental import pallas as pl
from jax.experimental.pallas import tpu as pltpu
from jax.sharding import PartitionSpec as P

MESH = pl.DeviceIdType.MESH
BF16 = jnp.bfloat16
F32 = jnp.float32


def tables():
    lane = np.arange(128)
    k1, n3 = lane // 16, lane % 16
    rows = []
    for v in range(8):
        angle = 2 * math.pi * ((16 * v + n3) * k1 % 1024) / 1024
        rows.append(np.stack([np.cos(angle), -np.sin(angle)]) / 32)
    for k2 in range(8):
        angle = 2 * math.pi * (n3 * k2 % 128) / 128
        rows.append(np.stack([np.cos(angle), -np.sin(angle)]))
    twiddle = np.stack(rows).astype(np.float32)

    step = np.zeros((2, 8, 16, 2, 2, 8, 8))
    three = np.arange(16)
    for first in range(8):
        for h in range(2):
            for z in range(8):
                angle = 2 * math.pi * (three * (2 * z + h) % 16) / 16
                cosine, sine = np.cos(angle), np.sin(angle)
                step[0, first, :, h, 0, z, first] = cosine
                step[0, first, :, h, 1, z, first] = -sine
                step[1, first, :, h, 0, z, first] = sine
                step[1, first, :, h, 1, z, first] = cosine
    step = step.reshape(256, 256)
    high = step.astype(ml_dtypes.bfloat16)
    low = (step - high.astype(np.float64)).astype(ml_dtypes.bfloat16)
    step = np.concatenate([high, low])

    place = np.zeros((2, 2, 8, 2, 2, 3, 8, 2, 2, 2, 2))
    for m, part, half, low, parity in np.ndindex(2, 2, 8, 2, 2):
        place[m, part, half, low, parity, :, half, parity, low, m, part] = 1
    return twiddle, step, place.reshape(128, 384).astype(ml_dtypes.bfloat16)


def turn(value, eighths):
    re, im = value
    root = math.sqrt(0.5)
    if eighths == 0:
        return value
    if eighths == 1:
        return (re + im) * root, (im - re) * root
    if eighths == 2:
        return im, -re
    return (im - re) * root, -(re + im) * root


def butterfly(values):
    count = len(values)
    if count == 1:
        return values
    even, odd = butterfly(values[0::2]), butterfly(values[1::2])
    low, high = [], []
    for k in range(count // 2):
        a, b = even[k], turn(odd[k], k * 8 // count)
        low.append((a[0] + b[0], a[1] + b[1]))
        high.append((a[0] - b[0], a[1] - b[1]))
    return low + high


def kernel(
    samples_hbm, wigner, step_hbm, place_hbm, twiddle_hbm, out,
    samples, wig, step, place, twiddle, send_a, buf_a, send_b, buf_b, send_c, buf_c, send_d, buf_d,
    gathered, own_e, send_e, buf_e, send_f, buf_f, send_sem, recv_sem, recv_d_sem, load_sem, wigner_sem,
):
    wide, beta = lax.axis_index("wide"), lax.axis_index("beta")
    z, v = wide // 8, wide % 8
    z_hi, x = beta // 4, beta % 4
    other = (beta + 4) % 8

    load_samples = pltpu.make_async_copy(samples_hbm, samples, load_sem.at[0])
    load_twiddle = pltpu.make_async_copy(twiddle_hbm, twiddle, load_sem.at[1])
    load_step = pltpu.make_async_copy(step_hbm, step, load_sem.at[2])
    load_place = pltpu.make_async_copy(place_hbm, place, load_sem.at[3])
    load_wigner = [
        pltpu.make_async_copy(wigner.at[m], wig.at[m], wigner_sem.at[m]) for m in range(8)
    ]
    load_samples.start()

    line = [(((z + d) % 8) * 8 + v, beta) for d in range(1, 8)]
    far = [(((z + d) % 8) * 8 + v, other) for d in range(8)]
    plane = [(z * 8 + (v + d) % 8, beta) for d in range(1, 8)]
    ring = [(wide, z_hi * 4 + (x + d) % 4) for d in range(1, 4)]
    peers = far + line + plane + ring
    barrier = pltpu.get_barrier_semaphore()
    for at_wide, at_beta in peers:
        pl.semaphore_signal(
            barrier, inc=1, device_id={"wide": at_wide, "beta": at_beta}, device_id_type=MESH
        )
    for load in (load_twiddle, load_step, load_place, *load_wigner):
        load.start()

    lane = lax.broadcasted_iota(jnp.int32, (16, 128), 1)
    first = lane % 2 == 0
    load_samples.wait()
    for m in range(8):
        for side in range(2):
            cycle = 127 - lane // 2 if side else lane // 2
            re, im = [jnp.take_along_axis(samples[part, m], cycle, axis=1) for part in range(2)]
            send_a[8 * side + m] = jnp.where(first, re, im)
    pl.semaphore_wait(barrier, len(peers))

    def send(source, target, to, sent, arrived):
        pltpu.make_async_remote_copy(
            src_ref=source,
            dst_ref=target,
            send_sem=sent,
            recv_sem=arrived,
            device_id={"wide": to[0], "beta": to[1]},
            device_id_type=MESH,
        ).start()

    def wait(block, semaphore):
        pltpu.make_async_copy(block, block, semaphore).wait()

    pltpu.make_async_copy(send_a.at[z], buf_a.at[z], recv_sem.at[0]).start()
    send(send_a.at[8 + z], buf_a.at[8 + z], far[0], send_sem.at[0], recv_sem.at[0])
    for to_hi in (1, 0):
        side = 1 - z_hi if to_hi else z_hi
        for d in range(1, 8):
            to = (z + d) % 8
            send(
                send_a.at[8 * side + to],
                buf_a.at[8 * side + z],
                (8 * to + v, 4 * to_hi + x),
                send_sem.at[0],
                recv_sem.at[0],
            )
    load_twiddle.wait()
    wait(buf_a, recv_sem.at[0])
    sign = (1 - 2 * z_hi).astype(F32)
    values = []
    for n in range(8):
        own, mirror = buf_a[n], buf_a[8 + n]
        even, odd = own + mirror, (own - mirror) * sign
        re = jnp.where(first, even, pltpu.roll(odd, 1, 1))
        im = jnp.where(first, pltpu.roll(even, 127, 1), odd)
        values.append((re, im))
    done = butterfly(values)
    re = jnp.concatenate([value[0] for value in done], axis=0).T
    im = jnp.concatenate([value[1] for value in done], axis=0).T
    factor = twiddle[v]
    cosine, sine = factor[0:1], factor[1:2]
    send_b[:, 0] = (re * cosine - im * sine).reshape(8, 16, 128)
    send_b[:, 1] = (re * sine + im * cosine).reshape(8, 16, 128)

    pltpu.make_async_copy(send_b.at[v], buf_b.at[v], recv_sem.at[1]).start()
    for d in range(1, 8):
        source, target = send_b.at[(v + d) % 8], buf_b.at[v]
        send(source, target, plane[d - 1], send_sem.at[1], recv_sem.at[1])
    wait(send_a.at[pl.ds(0, 15)], send_sem.at[0])
    load_step.wait()
    load_place.wait()
    wait(buf_b, recv_sem.at[1])
    done = butterfly([(buf_b[n, 0], buf_b[n, 1]) for n in range(8)])
    turned = []
    for k2 in range(8):
        re, im = done[k2]
        factor = twiddle[8 + k2]
        cosine, sine = factor[0:1], factor[1:2]
        turned.append(
            jnp.concatenate([re * cosine - im * sine, re * sine + im * cosine], axis=1)
        )
    values = jnp.concatenate(turned[0::2] + turned[1::2], axis=0)
    high = values.astype(BF16)
    low = (values - high.astype(F32)).astype(BF16)
    both = jnp.concatenate([high, low], axis=0)
    main = jnp.dot(both, step[0:256], preferred_element_type=F32)
    rest = jnp.dot(high, step[256:512], preferred_element_type=F32)
    spectrum = main[0:128] + (main[128:256] + rest)
    first_half = lax.broadcasted_iota(jnp.int32, (64, 128), 1) < 64
    for h in range(2):
        a = spectrum[0:64, 128 * h : 128 * h + 128]
        b = spectrum[64:128, 128 * h : 128 * h + 128]
        re = jnp.where(first_half, a, pltpu.roll(b, 64, 1))
        im = jnp.where(first_half, pltpu.roll(a, 64, 1), b)
        send_c[4 * h : 4 * h + 4, 0] = re.astype(BF16).reshape(4, 16, 128)
        send_c[4 * h : 4 * h + 4, 1] = im.astype(BF16).reshape(4, 16, 128)

    pltpu.make_async_copy(send_c.at[v], buf_c.at[v], recv_sem.at[2]).start()
    for d in range(1, 8):
        source, target = send_c.at[(v + d) % 8], buf_c.at[v]
        send(source, target, plane[d - 1], send_sem.at[2], recv_sem.at[2])
    wait(send_b.at[pl.ds(0, 7)], send_sem.at[1])
    wait(buf_c, recv_sem.at[2])
    for part in range(2):
        values = buf_c[:, part].reshape(128, 128).astype(F32).T
        values = [values[64 * e : 64 * e + 64].reshape(8, 8, 128) for e in range(2)]
        send_d[:, part] = jnp.concatenate(values, axis=1).astype(BF16)

    pltpu.make_async_copy(send_d.at[z], buf_d.at[z], recv_d_sem.at[0]).start()
    for d in range(1, 8):
        source, target = send_d.at[(z + d) % 8], buf_d.at[z]
        send(source, target, line[d - 1], send_sem.at[3], recv_d_sem.at[d])
    wait(send_c.at[pl.ds(0, 7)], send_sem.at[2])

    row = lax.broadcasted_iota(jnp.int32, (8, 128), 0)
    lane = lax.broadcasted_iota(jnp.int32, (8, 128), 1)
    fits = [[(lane % 2 == parity) & (row // 4 == low) for low in range(2)] for parity in range(2)]
    second = lax.broadcasted_iota(jnp.int32, (16, 128), 0) // 2 % 2 == 1

    def products(g):
        steps = (2 * g, 2 * g + 1)
        orders = [(z + 8 - d) % 8 for d in steps]
        for d, m in zip(steps, orders):
            wait(buf_d.at[m], recv_d_sem.at[d])
        for at, m in enumerate(orders):
            pltpu.make_async_copy(wigner.at[m], wig.at[m], wigner_sem.at[m]).wait()
            for part in range(2):
                gathered[g, pl.ds(2 * at + part, 16, stride=4)] = buf_d[m, part].astype(F32)
        terms = []
        for i in range(8):
            rows = gathered[g, 8 * i : 8 * i + 8]
            pairs = [
                jnp.concatenate([jnp.where(fit, rows, 0.0) for fit in parity], axis=1)
                for parity in fits
            ]
            weights = [wig[m, 256 * i : 256 * i + 256] for m in orders]
            both = jnp.dot(
                jnp.concatenate(pairs, axis=0).astype(BF16),
                jnp.concatenate(weights, axis=1),
                preferred_element_type=F32,
            )
            terms.append(jnp.where(second, both[:, 128:256], both[:, 0:128]))
        terms = jnp.concatenate(terms, axis=0).T
        own_e[:, g] = terms.reshape(8, 16, 128)
        terms = terms.astype(BF16)
        for owner in range(8):
            send_e[owner // 4, owner % 4, g] = terms[16 * owner : 16 * owner + 16]

    def total_of(owner):
        total = own_e[owner * 4 + x]
        for d in range(3):
            total += buf_e[owner, d].astype(F32)
        return total

    for g in range(4):
        products(g)

    for step, owner in ((4, 1 - z_hi), (5, z_hi)):
        for d in range(1, 4):
            source, target = send_e.at[owner, (x + d) % 4], buf_e.at[owner, d - 1]
            send(source, target, ring[d - 1], send_sem.at[step], recv_sem.at[step - 1])
    wait(send_d.at[pl.ds(0, 7)], send_sem.at[3])
    wait(buf_e.at[0], recv_sem.at[3])

    send_f[...] = total_of(1 - z_hi).astype(BF16)
    send(send_f, buf_f, far[0], send_sem.at[6], recv_sem.at[5])
    wait(buf_e.at[1], recv_sem.at[4])
    mine = total_of(z_hi)
    for step in (4, 5):
        wait(send_e.at[0, pl.ds(0, 3)], send_sem.at[step])
    wait(buf_f, recv_sem.at[5])
    total = mine + buf_f[...].astype(F32)
    high = total.astype(BF16)
    left = total - high.astype(F32)
    middle = left.astype(BF16)
    low = (left - middle.astype(F32)).astype(BF16)
    total = jnp.concatenate([high, middle, low], axis=2)
    row = lax.broadcasted_iota(jnp.int32, (128, 128), 0)
    lane = lax.broadcasted_iota(jnp.int32, (128, 128), 1)
    for g in range(4):
        rows = lax.dot_general(
            place[...],
            jnp.concatenate([total[g]] * 8, axis=0),
            (((1,), (1,)), ((), ())),
            preferred_element_type=F32,
        )
        rows = jnp.where(lane // 16 == row % 8, rows, 0.0).reshape(16, 8, 128).sum(axis=1)
        for at in range(2):
            for part in range(2):
                first_row = 8 * at + 4 * part
                out[part, (z + 8 - 2 * g - at) % 8] = rows[first_row : first_row + 4]
    wait(send_f, send_sem.at[6])


def body(samples, wigner):
    twiddle, step, place = tables()
    anywhere = pl.BlockSpec(memory_space=pl.ANY)
    terms = pl.pallas_call(
        kernel,
        out_shape=jax.ShapeDtypeStruct((2, 8, 4, 128), F32),
        in_specs=[anywhere] * 5,
        out_specs=pl.BlockSpec(memory_space=pltpu.VMEM),
        scratch_shapes=[
            pltpu.VMEM((2, 8, 16, 128), F32),
            pltpu.VMEM((8, 2048, 128), BF16),
            pltpu.VMEM((512, 256), BF16),
            pltpu.VMEM((128, 384), BF16),
            pltpu.VMEM((16, 2, 128), F32),
            pltpu.VMEM((16, 16, 128), F32),
            pltpu.VMEM((16, 16, 128), F32),
            pltpu.VMEM((8, 2, 16, 128), F32),
            pltpu.VMEM((8, 2, 16, 128), F32),
            pltpu.VMEM((8, 2, 16, 128), BF16),
            pltpu.VMEM((8, 2, 16, 128), BF16),
            pltpu.VMEM((8, 2, 16, 128), BF16),
            pltpu.VMEM((8, 2, 16, 128), BF16),
            pltpu.VMEM((4, 64, 128), F32),
            pltpu.VMEM((8, 4, 16, 128), F32),
            pltpu.VMEM((2, 4, 4, 16, 128), BF16),
            pltpu.VMEM((2, 3, 4, 16, 128), BF16),
            pltpu.VMEM((4, 16, 128), BF16),
            pltpu.VMEM((4, 16, 128), BF16),
            pltpu.SemaphoreType.DMA((7,)),
            pltpu.SemaphoreType.DMA((6,)),
            pltpu.SemaphoreType.DMA((8,)),
            pltpu.SemaphoreType.DMA((4,)),
            pltpu.SemaphoreType.DMA((8,)),
        ],
        compiler_params=pltpu.CompilerParams(
            collective_id=0, has_side_effects=True, vmem_limit_bytes=60 * 1024 * 1024
        ),
    )(
        samples,
        wigner.reshape(8, 2048, 128),
        jnp.asarray(step),
        jnp.asarray(place),
        jnp.asarray(twiddle),
    )
    return terms.reshape(2, 8, 16, 2, 16)


def solution(mesh):
    return jax.shard_map(
        body,
        mesh=mesh,
        in_specs=(P(None, None, "wide", "beta"), P(None, "wide", "beta", None, None)),
        out_specs=P(None, None, "wide", None, "beta"),
        check_vma=False,
    )
```

```python
import math

import jax
import jax.numpy as jnp
import ml_dtypes
import numpy as np
from jax import lax
from jax.experimental import pallas as pl
from jax.experimental.pallas import tpu as pltpu
from jax.sharding import PartitionSpec as P

MESH = pl.DeviceIdType.MESH
BF16 = jnp.bfloat16
F32 = jnp.float32


def tables():
    lane = np.arange(128)
    k1, n3 = lane // 16, lane % 16
    rows = []
    for v in range(8):
        angle = 2 * math.pi * ((16 * v + n3) * k1 % 1024) / 1024
        rows.append(np.stack([np.cos(angle), -np.sin(angle)]) / 32)
    for k2 in range(8):
        angle = 2 * math.pi * (n3 * k2 % 128) / 128
        rows.append(np.stack([np.cos(angle), -np.sin(angle)]))
    twiddle = np.stack(rows).astype(np.float32)

    step = np.zeros((2, 8, 16, 2, 2, 8, 8))
    three = np.arange(16)
    for first in range(8):
        for h in range(2):
            for z in range(8):
                angle = 2 * math.pi * (three * (2 * z + h) % 16) / 16
                cosine, sine = np.cos(angle), np.sin(angle)
                step[0, first, :, h, 0, z, first] = cosine
                step[0, first, :, h, 1, z, first] = -sine
                step[1, first, :, h, 0, z, first] = sine
                step[1, first, :, h, 1, z, first] = cosine
    step = step.reshape(256, 256)
    high = step.astype(ml_dtypes.bfloat16)
    low = (step - high.astype(np.float64)).astype(ml_dtypes.bfloat16)
    step = np.concatenate([high, low])

    place = np.zeros((2, 2, 8, 2, 2, 3, 8, 2, 2, 2, 2))
    for m, part, half, low, parity in np.ndindex(2, 2, 8, 2, 2):
        place[m, part, half, low, parity, :, half, parity, low, m, part] = 1
    return twiddle, step, place.reshape(128, 384).astype(ml_dtypes.bfloat16)


def turn(value, eighths):
    re, im = value
    root = math.sqrt(0.5)
    if eighths == 0:
        return value
    if eighths == 1:
        return (re + im) * root, (im - re) * root
    if eighths == 2:
        return im, -re
    return (im - re) * root, -(re + im) * root


def butterfly(values):
    count = len(values)
    if count == 1:
        return values
    even, odd = butterfly(values[0::2]), butterfly(values[1::2])
    low, high = [], []
    for k in range(count // 2):
        a, b = even[k], turn(odd[k], k * 8 // count)
        low.append((a[0] + b[0], a[1] + b[1]))
        high.append((a[0] - b[0], a[1] - b[1]))
    return low + high


def kernel(
    samples_hbm, wigner, step_hbm, place_hbm, twiddle_hbm, out,
    samples, wig, step, place, twiddle, send_a, buf_a, send_b, buf_b, send_c, buf_c, send_d, buf_d,
    gathered, own_e, send_e, buf_e, send_f, buf_f, send_sem, recv_sem, recv_d_sem, load_sem, wigner_sem,
):
    wide, beta = lax.axis_index("wide"), lax.axis_index("beta")
    z, y, core = wide // 8, wide // 2 % 4, wide % 2
    z_hi, x = beta // 4, beta % 4
    other = (beta + 4) % 8

    load_samples = pltpu.make_async_copy(samples_hbm, samples, load_sem.at[0])
    load_twiddle = pltpu.make_async_copy(twiddle_hbm, twiddle, load_sem.at[1])
    load_step = pltpu.make_async_copy(step_hbm, step, load_sem.at[2])
    load_place = pltpu.make_async_copy(place_hbm, place, load_sem.at[3])
    load_wigner = [
        pltpu.make_async_copy(wigner.at[m], wig.at[m], wigner_sem.at[m]) for m in range(8)
    ]
    load_samples.start()

    def chip(d):
        return (z + d) % 8 * 8 + 2 * y

    ring = [(wide, z_hi * 4 + (x + d) % 4) for d in range(1, 4)]
    plane = [(z * 8 + (y + d) % 4 * 2 + 1, beta) for d in range(1, 4)]
    partner = (wide, other)
    barrier = pltpu.get_barrier_semaphore()

    def greet(peers):
        for at_wide, at_beta in peers:
            pl.semaphore_signal(
                barrier, inc=1, device_id={"wide": at_wide, "beta": at_beta}, device_id_type=MESH
            )

    greet([partner])

    @pl.when(core == 1)
    def _():
        greet([(chip(d) + 1, other) for d in range(1, 8)])
        greet([(chip(d), other) for d in range(8)])
        greet([(chip(d) + 1, beta) for d in range(1, 8)])

    greet([(chip(d) + 1 - core, beta) for d in range(8)])

    @pl.when(core == 1)
    def _():
        greet(plane)
        load_twiddle.start()
        load_step.start()

    greet(ring)
    for load in (load_place, *load_wigner):
        load.start()

    lane = lax.broadcasted_iota(jnp.int32, (16, 128), 1)
    first = lane % 2 == 0
    load_samples.wait()
    for m in range(8):
        for side in range(2):
            cycle = 127 - lane // 2 if side else lane // 2
            re, im = [jnp.take_along_axis(samples[part, m], cycle, axis=1) for part in range(2)]
            send_a[8 * side + m] = jnp.where(first, re, im)
    pl.semaphore_wait(barrier, 20 + 9 * core)

    def send(source, target, to, sent, arrived):
        pltpu.make_async_remote_copy(
            src_ref=source,
            dst_ref=target,
            send_sem=sent,
            recv_sem=arrived,
            device_id={"wide": to[0], "beta": to[1]},
            device_id_type=MESH,
        ).start()

    def wait(block, semaphore):
        pltpu.make_async_copy(block, block, semaphore).wait()

    def send_block(side, d, to_hi):
        send(
            send_a.at[8 * side + (z + d) % 8],
            buf_a.at[16 * core + 8 * side + z],
            (chip(d) + 1, 4 * to_hi + x),
            send_sem.at[0],
            recv_sem.at[0],
        )

    send_block(1, 0, 1 - z_hi)

    @pl.when(core == 0)
    def _():
        send_block(0, 0, z_hi)

    for to_hi in (1, 0):
        for d in range(1, 8):
            send_block(1 - z_hi if to_hi else z_hi, d, to_hi)

    @pl.when(core == 0)
    def _():
        wait(send_a, send_sem.at[0])

    @pl.when(core == 1)
    def _():
        pltpu.make_async_copy(send_a.at[z], buf_a.at[16 + z], recv_sem.at[0]).start()
        load_twiddle.wait()
        wait(buf_a, recv_sem.at[0])
        sign = (1 - 2 * z_hi).astype(F32)
        for source in range(2):
            values = []
            for n in range(8):
                own, mirror = buf_a[16 * source + n], buf_a[16 * source + 8 + n]
                even, odd = own + mirror, (own - mirror) * sign
                re = jnp.where(first, even, pltpu.roll(odd, 1, 1))
                im = jnp.where(first, pltpu.roll(even, 127, 1), odd)
                values.append((re, im))
            done = butterfly(values)
            re = jnp.concatenate([value[0] for value in done], axis=0).T
            im = jnp.concatenate([value[1] for value in done], axis=0).T
            factor = twiddle[2 * y + source]
            cosine, sine = factor[0:1], factor[1:2]
            send_b[:, source, 0] = (re * cosine - im * sine).reshape(4, 32, 128)
            send_b[:, source, 1] = (re * sine + im * cosine).reshape(4, 32, 128)

        pltpu.make_async_copy(send_b.at[y], buf_b.at[y], recv_sem.at[1]).start()
        for d in range(1, 4):
            source, target = send_b.at[(y + d) % 4], buf_b.at[y]
            send(source, target, plane[d - 1], send_sem.at[1], recv_sem.at[1])
        wait(send_a.at[pl.ds(0, 15)], send_sem.at[0])
        load_step.wait()
        wait(buf_b, recv_sem.at[1])
        done = butterfly([(buf_b[n // 2, n % 2, 0], buf_b[n // 2, n % 2, 1]) for n in range(8)])
        turned = []
        for k2 in range(8):
            re, im = done[k2]
            factor = twiddle[8 + k2]
            cosine, sine = factor[0:1], factor[1:2]
            turned.append(
                jnp.concatenate([re * cosine - im * sine, re * sine + im * cosine], axis=1)
            )
        values = jnp.concatenate(turned[0::2] + turned[1::2], axis=0)
        high = values.astype(BF16)
        low = (values - high.astype(F32)).astype(BF16)
        both = jnp.concatenate([high, low], axis=0)
        main = jnp.dot(both, step[0:256], preferred_element_type=F32)
        rest = jnp.dot(high, step[256:512], preferred_element_type=F32)
        spectrum = main[0:256] + (main[256:512] + rest)
        first_half = lax.broadcasted_iota(jnp.int32, (128, 128), 1) < 64
        for h in range(2):
            a = spectrum[0:128, 128 * h : 128 * h + 128]
            b = spectrum[128:256, 128 * h : 128 * h + 128]
            re = jnp.where(first_half, a, pltpu.roll(b, 64, 1))
            im = jnp.where(first_half, pltpu.roll(a, 64, 1), b)
            send_c[2 * h : 2 * h + 2, :, 0] = re.astype(BF16).reshape(2, 2, 32, 128)
            send_c[2 * h : 2 * h + 2, :, 1] = im.astype(BF16).reshape(2, 2, 32, 128)

        pltpu.make_async_copy(send_c.at[y], buf_c.at[y], recv_sem.at[2]).start()
        for d in range(1, 4):
            source, target = send_c.at[(y + d) % 4], buf_c.at[y]
            send(source, target, plane[d - 1], send_sem.at[2], recv_sem.at[2])
        wait(send_b.at[pl.ds(0, 3)], send_sem.at[1])
        wait(buf_c, recv_sem.at[2])
        for to_core in range(2):
            for part in range(2):
                values = buf_c[:, to_core, part].reshape(128, 128).astype(F32).T
                values = [values[64 * e : 64 * e + 64].reshape(8, 8, 128) for e in range(2)]
                send_d[8 * to_core : 8 * to_core + 8, part] = jnp.concatenate(values, axis=1).astype(BF16)

            for d in range(8):
                source, target = send_d.at[8 * to_core + (z + d) % 8], buf_d.at[z]
                if to_core and d == 0:
                    pltpu.make_async_copy(source, target, recv_d_sem.at[0]).start()
                else:
                    to = (chip(d) + to_core, beta)
                    send(source, target, to, send_sem.at[3], recv_d_sem.at[d])
        wait(send_c.at[pl.ds(0, 3)], send_sem.at[2])

    load_place.wait()

    row = lax.broadcasted_iota(jnp.int32, (8, 128), 0)
    lane = lax.broadcasted_iota(jnp.int32, (8, 128), 1)
    fits = [[(lane % 2 == parity) & (row // 4 == low) for low in range(2)] for parity in range(2)]
    second = lax.broadcasted_iota(jnp.int32, (16, 128), 0) // 2 % 2 == 1

    def products(g):
        steps = (2 * g, 2 * g + 1)
        orders = [(z + 8 - d) % 8 for d in steps]
        for d, m in zip(steps, orders):
            wait(buf_d.at[m], recv_d_sem.at[d])
        for at, m in enumerate(orders):
            pltpu.make_async_copy(wigner.at[m], wig.at[m], wigner_sem.at[m]).wait()
            for part in range(2):
                gathered[g, pl.ds(2 * at + part, 16, stride=4)] = buf_d[m, part].astype(F32)
        terms = []
        for i in range(8):
            rows = gathered[g, 8 * i : 8 * i + 8]
            pairs = [
                jnp.concatenate([jnp.where(fit, rows, 0.0) for fit in parity], axis=1)
                for parity in fits
            ]
            weights = [wig[m, 256 * i : 256 * i + 256] for m in orders]
            both = jnp.dot(
                jnp.concatenate(pairs, axis=0).astype(BF16),
                jnp.concatenate(weights, axis=1),
                preferred_element_type=F32,
            )
            terms.append(jnp.where(second, both[:, 128:256], both[:, 0:128]))
        terms = jnp.concatenate(terms, axis=0).T
        own_e[:, g] = terms.reshape(8, 16, 128)
        terms = terms.astype(BF16)
        for owner in range(8):
            send_e[owner // 4, owner % 4, g] = terms[16 * owner : 16 * owner + 16]

    def total_of(owner):
        total = own_e[owner * 4 + x]
        for d in range(3):
            total += buf_e[owner, d].astype(F32)
        return total

    for g in range(4):
        products(g)

    for step, owner in ((4, 1 - z_hi), (5, z_hi)):
        for d in range(1, 4):
            source, target = send_e.at[owner, (x + d) % 4], buf_e.at[owner, d - 1]
            send(source, target, ring[d - 1], send_sem.at[step], recv_sem.at[step - 1])

    @pl.when(core == 1)
    def _():
        wait(send_d.at[pl.ds(0, 15)], send_sem.at[3])

    wait(buf_e.at[0], recv_sem.at[3])

    send_f[...] = total_of(1 - z_hi).astype(BF16)
    send(send_f, buf_f, partner, send_sem.at[6], recv_sem.at[5])
    wait(buf_e.at[1], recv_sem.at[4])
    mine = total_of(z_hi)
    for step in (4, 5):
        wait(send_e.at[0, pl.ds(0, 3)], send_sem.at[step])
    wait(buf_f, recv_sem.at[5])
    total = mine + buf_f[...].astype(F32)
    high = total.astype(BF16)
    left = total - high.astype(F32)
    middle = left.astype(BF16)
    low = (left - middle.astype(F32)).astype(BF16)
    total = jnp.concatenate([high, middle, low], axis=2)
    row = lax.broadcasted_iota(jnp.int32, (128, 128), 0)
    lane = lax.broadcasted_iota(jnp.int32, (128, 128), 1)
    for g in range(4):
        rows = lax.dot_general(
            place[...],
            jnp.concatenate([total[g]] * 8, axis=0),
            (((1,), (1,)), ((), ())),
            preferred_element_type=F32,
        )
        rows = jnp.where(lane // 16 == row % 8, rows, 0.0).reshape(16, 8, 128).sum(axis=1)
        for at in range(2):
            for part in range(2):
                first_row = 8 * at + 4 * part
                out[part, (z + 8 - 2 * g - at) % 8] = rows[first_row : first_row + 4]
    wait(send_f, send_sem.at[6])


def body(samples, wigner):
    twiddle, step, place = tables()
    anywhere = pl.BlockSpec(memory_space=pl.ANY)
    terms = pl.pallas_call(
        kernel,
        out_shape=jax.ShapeDtypeStruct((2, 8, 4, 128), F32),
        in_specs=[anywhere] * 5,
        out_specs=pl.BlockSpec(memory_space=pltpu.VMEM),
        scratch_shapes=[
            pltpu.VMEM((2, 8, 16, 128), F32),
            pltpu.VMEM((8, 2048, 128), BF16),
            pltpu.VMEM((512, 256), BF16),
            pltpu.VMEM((128, 384), BF16),
            pltpu.VMEM((16, 2, 128), F32),
            pltpu.VMEM((16, 16, 128), F32),
            pltpu.VMEM((32, 16, 128), F32),
            pltpu.VMEM((4, 2, 2, 32, 128), F32),
            pltpu.VMEM((4, 2, 2, 32, 128), F32),
            pltpu.VMEM((4, 2, 2, 32, 128), BF16),
            pltpu.VMEM((4, 2, 2, 32, 128), BF16),
            pltpu.VMEM((16, 2, 16, 128), BF16),
            pltpu.VMEM((8, 2, 16, 128), BF16),
            pltpu.VMEM((4, 64, 128), F32),
            pltpu.VMEM((8, 4, 16, 128), F32),
            pltpu.VMEM((2, 4, 4, 16, 128), BF16),
            pltpu.VMEM((2, 3, 4, 16, 128), BF16),
            pltpu.VMEM((4, 16, 128), BF16),
            pltpu.VMEM((4, 16, 128), BF16),
            pltpu.SemaphoreType.DMA((7,)),
            pltpu.SemaphoreType.DMA((6,)),
            pltpu.SemaphoreType.DMA((8,)),
            pltpu.SemaphoreType.DMA((4,)),
            pltpu.SemaphoreType.DMA((8,)),
        ],
        compiler_params=pltpu.CompilerParams(
            collective_id=0, has_side_effects=True, vmem_limit_bytes=60 * 1024 * 1024
        ),
    )(
        samples,
        wigner.reshape(8, 2048, 128),
        jnp.asarray(step),
        jnp.asarray(place),
        jnp.asarray(twiddle),
    )
    return terms.reshape(2, 8, 16, 2, 16)


def solution(mesh):
    return jax.shard_map(
        body,
        mesh=mesh,
        in_specs=(P(None, None, "wide", "beta"), P(None, "wide", "beta", None, None)),
        out_specs=P(None, None, "wide", None, "beta"),
        check_vma=False,
    )
```

```python
import math

import jax
import jax.numpy as jnp
import ml_dtypes
import numpy as np
from jax import lax
from jax.experimental import pallas as pl
from jax.experimental.pallas import tpu as pltpu
from jax.sharding import PartitionSpec as P

MESH = pl.DeviceIdType.MESH
BF16 = jnp.bfloat16
F32 = jnp.float32


def tables():
    lane = np.arange(128)
    k1, n3 = lane // 16, lane % 16
    rows = []
    for v in range(8):
        angle = 2 * math.pi * ((16 * v + n3) * k1 % 1024) / 1024
        rows.append(np.stack([np.cos(angle), -np.sin(angle)]) / 32)
    for k2 in range(8):
        angle = 2 * math.pi * (n3 * k2 % 128) / 128
        rows.append(np.stack([np.cos(angle), -np.sin(angle)]))
    twiddle = np.stack(rows).astype(np.float32)

    step = np.zeros((2, 8, 16, 2, 2, 8, 8))
    three = np.arange(16)
    for first in range(8):
        for h in range(2):
            for z in range(8):
                angle = 2 * math.pi * (three * (2 * z + h) % 16) / 16
                cosine, sine = np.cos(angle), np.sin(angle)
                step[0, first, :, h, 0, z, first] = cosine
                step[0, first, :, h, 1, z, first] = -sine
                step[1, first, :, h, 0, z, first] = sine
                step[1, first, :, h, 1, z, first] = cosine
    step = step.reshape(256, 256)
    high = step.astype(ml_dtypes.bfloat16)
    low = (step - high.astype(np.float64)).astype(ml_dtypes.bfloat16)
    step = np.concatenate([high, low])

    place = np.zeros((2, 2, 8, 2, 2, 3, 8, 2, 2, 2, 2))
    for m, part, half, low, parity in np.ndindex(2, 2, 8, 2, 2):
        place[m, part, half, low, parity, :, half, parity, low, m, part] = 1
    return twiddle, step, place.reshape(128, 384).astype(ml_dtypes.bfloat16)


def turn(value, eighths):
    re, im = value
    root = math.sqrt(0.5)
    if eighths == 0:
        return value
    if eighths == 1:
        return (re + im) * root, (im - re) * root
    if eighths == 2:
        return im, -re
    return (im - re) * root, -(re + im) * root


def butterfly(values):
    count = len(values)
    if count == 1:
        return values
    even, odd = butterfly(values[0::2]), butterfly(values[1::2])
    low, high = [], []
    for k in range(count // 2):
        a, b = even[k], turn(odd[k], k * 8 // count)
        low.append((a[0] + b[0], a[1] + b[1]))
        high.append((a[0] - b[0], a[1] - b[1]))
    return low + high


def kernel(
    samples_hbm, wigner, step_hbm, place_hbm, twiddle_hbm, out,
    samples, wig, step, place, twiddle, send_a, buf_a, send_b, buf_b, send_c, buf_c, send_d, buf_d,
    gathered, own_e, send_e, buf_e, send_f, buf_f, send_sem, recv_sem, recv_d_sem, load_sem, wigner_sem,
):
    wide, beta = lax.axis_index("wide"), lax.axis_index("beta")
    z, v = wide // 8, wide % 8
    z_hi, x = beta // 4, beta % 4
    other = (beta + 4) % 8

    load_samples = pltpu.make_async_copy(samples_hbm, samples, load_sem.at[0])
    load_twiddle = pltpu.make_async_copy(twiddle_hbm, twiddle, load_sem.at[1])
    load_step = pltpu.make_async_copy(step_hbm, step, load_sem.at[2])
    load_place = pltpu.make_async_copy(place_hbm, place, load_sem.at[3])
    load_wigner = [
        pltpu.make_async_copy(wigner.at[m], wig.at[m], wigner_sem.at[m]) for m in range(8)
    ]
    load_samples.start()

    line = [(((z + d) % 8) * 8 + v, beta) for d in range(1, 8)]
    far = [(((z + d) % 8) * 8 + v, other) for d in range(8)]
    plane = [(z * 8 + (v + d) % 8, beta) for d in range(1, 8)]
    ring = [(wide, z_hi * 4 + (x + d) % 4) for d in range(1, 4)]
    peers = far + line + plane + ring
    barrier = pltpu.get_barrier_semaphore()
    for at_wide, at_beta in peers:
        pl.semaphore_signal(
            barrier, inc=1, device_id={"wide": at_wide, "beta": at_beta}, device_id_type=MESH
        )
    for load in (load_twiddle, load_step, load_place, *load_wigner):
        load.start()

    lane = lax.broadcasted_iota(jnp.int32, (16, 128), 1)
    first = lane % 2 == 0
    load_samples.wait()
    for m in range(8):
        for side in range(2):
            cycle = 127 - lane // 2 if side else lane // 2
            re, im = [jnp.take_along_axis(samples[part, m], cycle, axis=1) for part in range(2)]
            send_a[8 * side + m] = jnp.where(first, re, im)
    pl.semaphore_wait(barrier, len(peers))

    def send(source, target, to, sent, arrived):
        pltpu.make_async_remote_copy(
            src_ref=source,
            dst_ref=target,
            send_sem=sent,
            recv_sem=arrived,
            device_id={"wide": to[0], "beta": to[1]},
            device_id_type=MESH,
        ).start()

    def wait(block, semaphore):
        pltpu.make_async_copy(block, block, semaphore).wait()

    pltpu.make_async_copy(send_a.at[z], buf_a.at[z], recv_sem.at[0]).start()
    send(send_a.at[8 + z], buf_a.at[8 + z], far[0], send_sem.at[0], recv_sem.at[0])
    for to_hi in (1, 0):
        side = 1 - z_hi if to_hi else z_hi
        for d in range(1, 8):
            to = (z + d) % 8
            send(
                send_a.at[8 * side + to],
                buf_a.at[8 * side + z],
                (8 * to + v, 4 * to_hi + x),
                send_sem.at[0],
                recv_sem.at[0],
            )
    load_twiddle.wait()
    wait(buf_a, recv_sem.at[0])
    sign = (1 - 2 * z_hi).astype(F32)
    values = []
    for n in range(8):
        own, mirror = buf_a[n], buf_a[8 + n]
        even, odd = own + mirror, (own - mirror) * sign
        re = jnp.where(first, even, pltpu.roll(odd, 1, 1))
        im = jnp.where(first, pltpu.roll(even, 127, 1), odd)
        values.append((re, im))
    done = butterfly(values)
    re = jnp.concatenate([value[0] for value in done], axis=0).T
    im = jnp.concatenate([value[1] for value in done], axis=0).T
    factor = twiddle[v]
    cosine, sine = factor[0:1], factor[1:2]
    send_b[:, 0] = (re * cosine - im * sine).reshape(8, 16, 128)
    send_b[:, 1] = (re * sine + im * cosine).reshape(8, 16, 128)

    pltpu.make_async_copy(send_b.at[v], buf_b.at[v], recv_sem.at[1]).start()
    for d in range(1, 8):
        source, target = send_b.at[(v + d) % 8], buf_b.at[v]
        send(source, target, plane[d - 1], send_sem.at[1], recv_sem.at[1])
    wait(send_a.at[pl.ds(0, 15)], send_sem.at[0])
    load_step.wait()
    load_place.wait()
    wait(buf_b, recv_sem.at[1])
    done = butterfly([(buf_b[n, 0], buf_b[n, 1]) for n in range(8)])
    turned = []
    for k2 in range(8):
        re, im = done[k2]
        factor = twiddle[8 + k2]
        cosine, sine = factor[0:1], factor[1:2]
        turned.append(
            jnp.concatenate([re * cosine - im * sine, re * sine + im * cosine], axis=1)
        )
    values = jnp.concatenate(turned[0::2] + turned[1::2], axis=0)
    high = values.astype(BF16)
    low = (values - high.astype(F32)).astype(BF16)
    both = jnp.concatenate([high, low], axis=0)
    main = jnp.dot(both, step[0:256], preferred_element_type=F32)
    rest = jnp.dot(high, step[256:512], preferred_element_type=F32)
    spectrum = main[0:128] + (main[128:256] + rest)
    first_half = lax.broadcasted_iota(jnp.int32, (64, 128), 1) < 64
    for h in range(2):
        a = spectrum[0:64, 128 * h : 128 * h + 128]
        b = spectrum[64:128, 128 * h : 128 * h + 128]
        re = jnp.where(first_half, a, pltpu.roll(b, 64, 1))
        im = jnp.where(first_half, pltpu.roll(a, 64, 1), b)
        send_c[4 * h : 4 * h + 4, 0] = re.astype(BF16).reshape(4, 16, 128)
        send_c[4 * h : 4 * h + 4, 1] = im.astype(BF16).reshape(4, 16, 128)

    pltpu.make_async_copy(send_c.at[v], buf_c.at[v], recv_sem.at[2]).start()
    for d in range(1, 8):
        source, target = send_c.at[(v + d) % 8], buf_c.at[v]
        send(source, target, plane[d - 1], send_sem.at[2], recv_sem.at[2])
    wait(send_b.at[pl.ds(0, 7)], send_sem.at[1])
    wait(buf_c, recv_sem.at[2])
    for part in range(2):
        values = buf_c[:, part].reshape(128, 128).astype(F32).T
        values = [values[64 * e : 64 * e + 64].reshape(8, 8, 128) for e in range(2)]
        send_d[:, part] = jnp.concatenate(values, axis=1).astype(BF16)

    pltpu.make_async_copy(send_d.at[z], buf_d.at[z], recv_d_sem.at[0]).start()
    for d in range(1, 8):
        source, target = send_d.at[(z + d) % 8], buf_d.at[z]
        send(source, target, line[d - 1], send_sem.at[3], recv_d_sem.at[d])
    wait(send_c.at[pl.ds(0, 7)], send_sem.at[2])

    row = lax.broadcasted_iota(jnp.int32, (8, 128), 0)
    lane = lax.broadcasted_iota(jnp.int32, (8, 128), 1)
    fits = [[(lane % 2 == parity) & (row // 4 == low) for low in range(2)] for parity in range(2)]
    second = lax.broadcasted_iota(jnp.int32, (16, 128), 0) // 2 % 2 == 1

    def products(g):
        steps = (2 * g, 2 * g + 1)
        orders = [(z + 8 - d) % 8 for d in steps]
        for d, m in zip(steps, orders):
            wait(buf_d.at[m], recv_d_sem.at[d])
        for at, m in enumerate(orders):
            pltpu.make_async_copy(wigner.at[m], wig.at[m], wigner_sem.at[m]).wait()
            for part in range(2):
                gathered[g, pl.ds(2 * at + part, 16, stride=4)] = buf_d[m, part].astype(F32)
        terms = []
        for i in range(8):
            rows = gathered[g, 8 * i : 8 * i + 8]
            pairs = [
                jnp.concatenate([jnp.where(fit, rows, 0.0) for fit in parity], axis=1)
                for parity in fits
            ]
            weights = [wig[m, 256 * i : 256 * i + 256] for m in orders]
            both = jnp.dot(
                jnp.concatenate(pairs, axis=0).astype(BF16),
                jnp.concatenate(weights, axis=1),
                preferred_element_type=F32,
            )
            terms.append(jnp.where(second, both[:, 128:256], both[:, 0:128]))
        terms = jnp.concatenate(terms, axis=0).T
        own_e[:, g] = terms.reshape(8, 16, 128)
        terms = terms.astype(BF16)
        for owner in range(8):
            send_e[owner // 4, g // 2, owner % 4, g % 2] = terms[16 * owner : 16 * owner + 16]

    def total_of(owner, half):
        total = own_e[owner * 4 + x, 2 * half : 2 * half + 2]
        for d in range(3):
            total += buf_e[owner, half, d].astype(F32)
        return total

    for half in range(2):
        products(2 * half)
        products(2 * half + 1)
        for d in range(1, 4):
            send(
                send_e.at[1 - z_hi, half, (x + d) % 4],
                buf_e.at[1 - z_hi, half, d - 1],
                ring[d - 1],
                send_sem.at[4 + half],
                recv_sem.at[3 + half],
            )
    for d in range(1, 4):
        source, target = send_e.at[z_hi, :, (x + d) % 4], buf_e.at[z_hi, :, d - 1]
        send(source, target, ring[d - 1], send_sem.at[6], recv_sem.at[5])
    wait(send_d.at[pl.ds(0, 7)], send_sem.at[3])

    for half in range(2):
        wait(buf_e.at[0, half], recv_sem.at[3 + half])
        pair = pl.ds(2 * half, 2)
        send_f[2 * half : 2 * half + 2] = total_of(1 - z_hi, half).astype(BF16)
        send(
            send_f.at[pair], buf_f.at[pair], far[0], send_sem.at[7 + half], recv_sem.at[6 + half]
        )
    wait(buf_e.at[0], recv_sem.at[5])
    mine = jnp.concatenate([total_of(z_hi, half) for half in range(2)], axis=0)
    for half in range(2):
        wait(send_e.at[0, 0, pl.ds(0, 3)], send_sem.at[4 + half])
    wait(buf_e.at[0], send_sem.at[6])
    for half in range(2):
        wait(buf_f.at[pl.ds(2 * half, 2)], recv_sem.at[6 + half])
    total = mine + buf_f[...].astype(F32)
    high = total.astype(BF16)
    left = total - high.astype(F32)
    middle = left.astype(BF16)
    low = (left - middle.astype(F32)).astype(BF16)
    total = jnp.concatenate([high, middle, low], axis=2)
    row = lax.broadcasted_iota(jnp.int32, (128, 128), 0)
    lane = lax.broadcasted_iota(jnp.int32, (128, 128), 1)
    for g in range(4):
        rows = lax.dot_general(
            place[...],
            jnp.concatenate([total[g]] * 8, axis=0),
            (((1,), (1,)), ((), ())),
            preferred_element_type=F32,
        )
        rows = jnp.where(lane // 16 == row % 8, rows, 0.0).reshape(16, 8, 128).sum(axis=1)
        for at in range(2):
            for part in range(2):
                first_row = 8 * at + 4 * part
                out[part, (z + 8 - 2 * g - at) % 8] = rows[first_row : first_row + 4]
    for half in range(2):
        wait(send_f.at[pl.ds(2 * half, 2)], send_sem.at[7 + half])


def body(samples, wigner):
    twiddle, step, place = tables()
    anywhere = pl.BlockSpec(memory_space=pl.ANY)
    terms = pl.pallas_call(
        kernel,
        out_shape=jax.ShapeDtypeStruct((2, 8, 4, 128), F32),
        in_specs=[anywhere] * 5,
        out_specs=pl.BlockSpec(memory_space=pltpu.VMEM),
        scratch_shapes=[
            pltpu.VMEM((2, 8, 16, 128), F32),
            pltpu.VMEM((8, 2048, 128), BF16),
            pltpu.VMEM((512, 256), BF16),
            pltpu.VMEM((128, 384), BF16),
            pltpu.VMEM((16, 2, 128), F32),
            pltpu.VMEM((16, 16, 128), F32),
            pltpu.VMEM((16, 16, 128), F32),
            pltpu.VMEM((8, 2, 16, 128), F32),
            pltpu.VMEM((8, 2, 16, 128), F32),
            pltpu.VMEM((8, 2, 16, 128), BF16),
            pltpu.VMEM((8, 2, 16, 128), BF16),
            pltpu.VMEM((8, 2, 16, 128), BF16),
            pltpu.VMEM((8, 2, 16, 128), BF16),
            pltpu.VMEM((4, 64, 128), F32),
            pltpu.VMEM((8, 4, 16, 128), F32),
            pltpu.VMEM((2, 2, 4, 2, 16, 128), BF16),
            pltpu.VMEM((2, 2, 3, 2, 16, 128), BF16),
            pltpu.VMEM((4, 16, 128), BF16),
            pltpu.VMEM((4, 16, 128), BF16),
            pltpu.SemaphoreType.DMA((9,)),
            pltpu.SemaphoreType.DMA((8,)),
            pltpu.SemaphoreType.DMA((8,)),
            pltpu.SemaphoreType.DMA((4,)),
            pltpu.SemaphoreType.DMA((8,)),
        ],
        compiler_params=pltpu.CompilerParams(
            collective_id=0, has_side_effects=True, vmem_limit_bytes=60 * 1024 * 1024
        ),
    )(
        samples,
        wigner.reshape(8, 2048, 128),
        jnp.asarray(step),
        jnp.asarray(place),
        jnp.asarray(twiddle),
    )
    return terms.reshape(2, 8, 16, 2, 16)


def solution(mesh):
    return jax.shard_map(
        body,
        mesh=mesh,
        in_specs=(P(None, None, "wide", "beta"), P(None, "wide", "beta", None, None)),
        out_specs=P(None, None, "wide", None, "beta"),
        check_vma=False,
    )
```

```python
import math

import jax
import jax.numpy as jnp
import ml_dtypes
import numpy as np
from jax import lax
from jax.experimental import pallas as pl
from jax.experimental.pallas import tpu as pltpu
from jax.sharding import PartitionSpec as P

MESH = pl.DeviceIdType.MESH
BF16 = jnp.bfloat16
F32 = jnp.float32


def tables():
    lane = np.arange(128)
    k1, n3 = lane // 16, lane % 16
    rows = []
    for v in range(8):
        angle = 2 * math.pi * ((16 * v + n3) * k1 % 1024) / 1024
        rows.append(np.stack([np.cos(angle), -np.sin(angle)]) / 32)
    for k2 in range(8):
        angle = 2 * math.pi * (n3 * k2 % 128) / 128
        rows.append(np.stack([np.cos(angle), -np.sin(angle)]))
    twiddle = np.stack(rows).astype(np.float32)

    step = np.zeros((2, 8, 16, 2, 2, 8, 8))
    three = np.arange(16)
    for first in range(8):
        for h in range(2):
            for z in range(8):
                angle = 2 * math.pi * (three * (2 * z + h) % 16) / 16
                cosine, sine = np.cos(angle), np.sin(angle)
                step[0, first, :, h, 0, z, first] = cosine
                step[0, first, :, h, 1, z, first] = -sine
                step[1, first, :, h, 0, z, first] = sine
                step[1, first, :, h, 1, z, first] = cosine
    step = step.reshape(256, 256)
    high = step.astype(ml_dtypes.bfloat16)
    low = (step - high.astype(np.float64)).astype(ml_dtypes.bfloat16)
    step = np.concatenate([high, low])

    place = np.zeros((2, 2, 8, 2, 2, 3, 8, 2, 2, 2, 2))
    for m, part, half, low, parity in np.ndindex(2, 2, 8, 2, 2):
        place[m, part, half, low, parity, :, half, parity, low, m, part] = 1
    return twiddle, step, place.reshape(128, 384).astype(ml_dtypes.bfloat16)


def turn(value, eighths):
    re, im = value
    root = math.sqrt(0.5)
    if eighths == 0:
        return value
    if eighths == 1:
        return (re + im) * root, (im - re) * root
    if eighths == 2:
        return im, -re
    return (im - re) * root, -(re + im) * root


def butterfly(values):
    count = len(values)
    if count == 1:
        return values
    even, odd = butterfly(values[0::2]), butterfly(values[1::2])
    low, high = [], []
    for k in range(count // 2):
        a, b = even[k], turn(odd[k], k * 8 // count)
        low.append((a[0] + b[0], a[1] + b[1]))
        high.append((a[0] - b[0], a[1] - b[1]))
    return low + high


def kernel(
    samples_hbm, wigner, step_hbm, place_hbm, twiddle_hbm, out,
    samples, wig, step, place, twiddle, send_a, buf_a, send_b, buf_b, send_c, buf_c, send_d, buf_d,
    gathered, own_e, send_e, buf_e, send_f, buf_f, send_sem, recv_sem, recv_d_sem, load_sem, wigner_sem,
):
    wide, beta = lax.axis_index("wide"), lax.axis_index("beta")
    z, v = wide // 8, wide % 8
    z_hi, x = beta // 4, beta % 4
    other = (beta + 4) % 8

    load_samples = pltpu.make_async_copy(samples_hbm, samples, load_sem.at[0])
    load_twiddle = pltpu.make_async_copy(twiddle_hbm, twiddle, load_sem.at[1])
    load_step = pltpu.make_async_copy(step_hbm, step, load_sem.at[2])
    load_place = pltpu.make_async_copy(place_hbm, place, load_sem.at[3])
    load_wigner = [
        pltpu.make_async_copy(wigner.at[m], wig.at[m], wigner_sem.at[m]) for m in range(8)
    ]
    load_samples.start()

    def across(d):
        return sum((z // bit + d // bit) % 2 * bit for bit in (1, 2, 4))

    line = [(across(d) * 8 + v, beta) for d in range(1, 8)]
    far = [(across(d) * 8 + v, other) for d in range(8)]
    plane = [(z * 8 + (v + d) % 8, beta) for d in range(1, 8)]
    ring = [(wide, z_hi * 4 + (x + d) % 4) for d in range(1, 4)]
    peers = far + line[::-1] + plane + ring
    barrier = pltpu.get_barrier_semaphore()
    for at_wide, at_beta in peers:
        pl.semaphore_signal(
            barrier, inc=1, device_id={"wide": at_wide, "beta": at_beta}, device_id_type=MESH
        )
    for load in (load_twiddle, load_step, load_place, *load_wigner):
        load.start()

    lane = lax.broadcasted_iota(jnp.int32, (16, 128), 1)
    first = lane % 2 == 0
    load_samples.wait()
    for m in range(8):
        for side in range(2):
            cycle = 127 - lane // 2 if side else lane // 2
            re, im = [jnp.take_along_axis(samples[part, m], cycle, axis=1) for part in range(2)]
            send_a[8 * side + m] = jnp.where(first, re, im)
    pl.semaphore_wait(barrier, len(peers))

    def send(source, target, to, sent, arrived):
        pltpu.make_async_remote_copy(
            src_ref=source,
            dst_ref=target,
            send_sem=sent,
            recv_sem=arrived,
            device_id={"wide": to[0], "beta": to[1]},
            device_id_type=MESH,
        ).start()

    def wait(block, semaphore):
        pltpu.make_async_copy(block, block, semaphore).wait()

    pltpu.make_async_copy(send_a.at[z], buf_a.at[z], recv_sem.at[0]).start()
    send(send_a.at[8 + z], buf_a.at[8 + z], far[0], send_sem.at[0], recv_sem.at[0])
    for to_hi in (1, 0):
        side = 1 - z_hi if to_hi else z_hi
        for k in range(1, 8):
            to = across(8 - k + side * (2 * k - 8))
            send(
                send_a.at[8 * side + to],
                buf_a.at[8 * side + z],
                (8 * to + v, 4 * to_hi + x),
                send_sem.at[0],
                recv_sem.at[0],
            )
    load_twiddle.wait()
    wait(buf_a, recv_sem.at[0])
    sign = (1 - 2 * z_hi).astype(F32)
    values = []
    for n in range(8):
        own, mirror = buf_a[n], buf_a[8 + n]
        even, odd = own + mirror, (own - mirror) * sign
        re = jnp.where(first, even, pltpu.roll(odd, 1, 1))
        im = jnp.where(first, pltpu.roll(even, 127, 1), odd)
        values.append((re, im))
    done = butterfly(values)
    re = jnp.concatenate([value[0] for value in done], axis=0).T
    im = jnp.concatenate([value[1] for value in done], axis=0).T
    factor = twiddle[v]
    cosine, sine = factor[0:1], factor[1:2]
    send_b[:, 0] = (re * cosine - im * sine).reshape(8, 16, 128)
    send_b[:, 1] = (re * sine + im * cosine).reshape(8, 16, 128)

    pltpu.make_async_copy(send_b.at[v], buf_b.at[v], recv_sem.at[1]).start()
    for d in (4, 3, 5, 2, 6, 1, 7):
        source, target = send_b.at[(v + d) % 8], buf_b.at[v]
        send(source, target, plane[d - 1], send_sem.at[1], recv_sem.at[1])
    wait(send_a.at[pl.ds(0, 15)], send_sem.at[0])
    load_step.wait()
    load_place.wait()
    wait(buf_b, recv_sem.at[1])
    done = butterfly([(buf_b[n, 0], buf_b[n, 1]) for n in range(8)])
    turned = []
    for k2 in range(8):
        re, im = done[k2]
        factor = twiddle[8 + k2]
        cosine, sine = factor[0:1], factor[1:2]
        turned.append(
            jnp.concatenate([re * cosine - im * sine, re * sine + im * cosine], axis=1)
        )
    values = jnp.concatenate(turned[0::2] + turned[1::2], axis=0)
    high = values.astype(BF16)
    low = (values - high.astype(F32)).astype(BF16)
    both = jnp.concatenate([high, low], axis=0)
    main = jnp.dot(both, step[0:256], preferred_element_type=F32)
    rest = jnp.dot(high, step[256:512], preferred_element_type=F32)
    spectrum = main[0:128] + (main[128:256] + rest)
    first_half = lax.broadcasted_iota(jnp.int32, (64, 128), 1) < 64
    for h in range(2):
        a = spectrum[0:64, 128 * h : 128 * h + 128]
        b = spectrum[64:128, 128 * h : 128 * h + 128]
        re = jnp.where(first_half, a, pltpu.roll(b, 64, 1))
        im = jnp.where(first_half, pltpu.roll(a, 64, 1), b)
        send_c[4 * h : 4 * h + 4, 0] = re.astype(BF16).reshape(4, 16, 128)
        send_c[4 * h : 4 * h + 4, 1] = im.astype(BF16).reshape(4, 16, 128)

    pltpu.make_async_copy(send_c.at[v], buf_c.at[v], recv_sem.at[2]).start()
    for d in (4, 3, 5, 2, 6, 1, 7):
        source, target = send_c.at[(v + d) % 8], buf_c.at[v]
        send(source, target, plane[d - 1], send_sem.at[2], recv_sem.at[2])
    wait(send_b.at[pl.ds(0, 7)], send_sem.at[1])
    wait(buf_c, recv_sem.at[2])
    for part in range(2):
        values = buf_c[:, part].reshape(128, 128).astype(F32).T
        values = [values[64 * e : 64 * e + 64].reshape(8, 8, 128) for e in range(2)]
        send_d[:, part] = jnp.concatenate(values, axis=1).astype(BF16)

    pltpu.make_async_copy(send_d.at[z], buf_d.at[z], recv_d_sem.at[0]).start()
    for d in range(7, 0, -1):
        source, target = send_d.at[across(d)], buf_d.at[z]
        send(source, target, line[d - 1], send_sem.at[3], recv_d_sem.at[d])
    wait(send_c.at[pl.ds(0, 7)], send_sem.at[2])

    row = lax.broadcasted_iota(jnp.int32, (8, 128), 0)
    lane = lax.broadcasted_iota(jnp.int32, (8, 128), 1)
    fits = [[(lane % 2 == parity) & (row // 4 == low) for low in range(2)] for parity in range(2)]
    second = lax.broadcasted_iota(jnp.int32, (16, 128), 0) // 2 % 2 == 1

    def products(g):
        steps = (2 * g, 2 * g + 1)
        orders = [across(d) for d in steps]
        for d, m in zip(steps, orders):
            wait(buf_d.at[m], recv_d_sem.at[d])
        for at, m in enumerate(orders):
            pltpu.make_async_copy(wigner.at[m], wig.at[m], wigner_sem.at[m]).wait()
            for part in range(2):
                gathered[g, pl.ds(2 * at + part, 16, stride=4)] = buf_d[m, part].astype(F32)
        terms = []
        for i in range(8):
            rows = gathered[g, 8 * i : 8 * i + 8]
            pairs = [
                jnp.concatenate([jnp.where(fit, rows, 0.0) for fit in parity], axis=1)
                for parity in fits
            ]
            weights = [wig[m, 256 * i : 256 * i + 256] for m in orders]
            both = jnp.dot(
                jnp.concatenate(pairs, axis=0).astype(BF16),
                jnp.concatenate(weights, axis=1),
                preferred_element_type=F32,
            )
            terms.append(jnp.where(second, both[:, 128:256], both[:, 0:128]))
        terms = jnp.concatenate(terms, axis=0).T
        own_e[:, g] = terms.reshape(8, 16, 128)
        terms = terms.astype(BF16)
        for owner in range(8):
            send_e[owner // 4, owner % 4, g] = terms[16 * owner : 16 * owner + 16]

    def total_of(owner):
        total = own_e[owner * 4 + x]
        for d in range(3):
            total += buf_e[owner, d].astype(F32)
        return total

    for g in range(4):
        products(g)

    for step, owner in ((4, 1 - z_hi), (5, z_hi)):
        for d in (2, 1, 3):
            source, target = send_e.at[owner, (x + d) % 4], buf_e.at[owner, d - 1]
            send(source, target, ring[d - 1], send_sem.at[step], recv_sem.at[step - 1])
    wait(send_d.at[pl.ds(0, 7)], send_sem.at[3])
    wait(buf_e.at[0], recv_sem.at[3])

    send_f[...] = total_of(1 - z_hi).astype(BF16)
    send(send_f, buf_f, far[0], send_sem.at[6], recv_sem.at[5])
    wait(buf_e.at[1], recv_sem.at[4])
    mine = total_of(z_hi)
    for step in (4, 5):
        wait(send_e.at[0, pl.ds(0, 3)], send_sem.at[step])
    wait(buf_f, recv_sem.at[5])
    total = mine + buf_f[...].astype(F32)
    high = total.astype(BF16)
    left = total - high.astype(F32)
    middle = left.astype(BF16)
    low = (left - middle.astype(F32)).astype(BF16)
    total = jnp.concatenate([high, middle, low], axis=2)
    row = lax.broadcasted_iota(jnp.int32, (128, 128), 0)
    lane = lax.broadcasted_iota(jnp.int32, (128, 128), 1)
    for g in range(4):
        rows = lax.dot_general(
            place[...],
            jnp.concatenate([total[g]] * 8, axis=0),
            (((1,), (1,)), ((), ())),
            preferred_element_type=F32,
        )
        rows = jnp.where(lane // 16 == row % 8, rows, 0.0).reshape(16, 8, 128).sum(axis=1)
        for at in range(2):
            for part in range(2):
                first_row = 8 * at + 4 * part
                out[part, across(2 * g + at)] = rows[first_row : first_row + 4]
    wait(send_f, send_sem.at[6])


def body(samples, wigner):
    twiddle, step, place = tables()
    anywhere = pl.BlockSpec(memory_space=pl.ANY)
    terms = pl.pallas_call(
        kernel,
        out_shape=jax.ShapeDtypeStruct((2, 8, 4, 128), F32),
        in_specs=[anywhere] * 5,
        out_specs=pl.BlockSpec(memory_space=pltpu.VMEM),
        scratch_shapes=[
            pltpu.VMEM((2, 8, 16, 128), F32),
            pltpu.VMEM((8, 2048, 128), BF16),
            pltpu.VMEM((512, 256), BF16),
            pltpu.VMEM((128, 384), BF16),
            pltpu.VMEM((16, 2, 128), F32),
            pltpu.VMEM((16, 16, 128), F32),
            pltpu.VMEM((16, 16, 128), F32),
            pltpu.VMEM((8, 2, 16, 128), F32),
            pltpu.VMEM((8, 2, 16, 128), F32),
            pltpu.VMEM((8, 2, 16, 128), BF16),
            pltpu.VMEM((8, 2, 16, 128), BF16),
            pltpu.VMEM((8, 2, 16, 128), BF16),
            pltpu.VMEM((8, 2, 16, 128), BF16),
            pltpu.VMEM((4, 64, 128), F32),
            pltpu.VMEM((8, 4, 16, 128), F32),
            pltpu.VMEM((2, 4, 4, 16, 128), BF16),
            pltpu.VMEM((2, 3, 4, 16, 128), BF16),
            pltpu.VMEM((4, 16, 128), BF16),
            pltpu.VMEM((4, 16, 128), BF16),
            pltpu.SemaphoreType.DMA((7,)),
            pltpu.SemaphoreType.DMA((6,)),
            pltpu.SemaphoreType.DMA((8,)),
            pltpu.SemaphoreType.DMA((4,)),
            pltpu.SemaphoreType.DMA((8,)),
        ],
        compiler_params=pltpu.CompilerParams(
            collective_id=0, has_side_effects=True, vmem_limit_bytes=60 * 1024 * 1024
        ),
    )(
        samples,
        wigner.reshape(8, 2048, 128),
        jnp.asarray(step),
        jnp.asarray(place),
        jnp.asarray(twiddle),
    )
    return terms.reshape(2, 8, 16, 2, 16)


def solution(mesh):
    return jax.shard_map(
        body,
        mesh=mesh,
        in_specs=(P(None, None, "wide", "beta"), P(None, "wide", "beta", None, None)),
        out_specs=P(None, None, "wide", None, "beta"),
        check_vma=False,
    )
```

```python
import math

import jax
import jax.numpy as jnp
import ml_dtypes
import numpy as np
from jax import lax
from jax.experimental import pallas as pl
from jax.experimental.pallas import tpu as pltpu
from jax.sharding import PartitionSpec as P

MESH = pl.DeviceIdType.MESH
BF16 = jnp.bfloat16
F32 = jnp.float32


def tables():
    lane = np.arange(128)
    k1, n3 = lane // 16, lane % 16
    rows = []
    for v in range(8):
        angle = 2 * math.pi * ((16 * v + n3) * k1 % 1024) / 1024
        rows.append(np.stack([np.cos(angle), -np.sin(angle)]) / 32)
    for k2 in range(8):
        angle = 2 * math.pi * (n3 * k2 % 128) / 128
        rows.append(np.stack([np.cos(angle), -np.sin(angle)]))
    twiddle = np.stack(rows).astype(np.float32)

    step = np.zeros((2, 8, 16, 2, 2, 8, 8))
    three = np.arange(16)
    for first in range(8):
        for h in range(2):
            for z in range(8):
                angle = 2 * math.pi * (three * (2 * z + h) % 16) / 16
                cosine, sine = np.cos(angle), np.sin(angle)
                step[0, first, :, h, 0, z, first] = cosine
                step[0, first, :, h, 1, z, first] = -sine
                step[1, first, :, h, 0, z, first] = sine
                step[1, first, :, h, 1, z, first] = cosine
    step = step.reshape(256, 256)
    high = step.astype(ml_dtypes.bfloat16)
    low = (step - high.astype(np.float64)).astype(ml_dtypes.bfloat16)
    step = np.concatenate([high, high, low])

    place = np.zeros((2, 2, 8, 2, 2, 3, 8, 2, 2, 2, 2))
    for m, part, half, low, parity in np.ndindex(2, 2, 8, 2, 2):
        place[m, part, half, low, parity, :, half, parity, low, m, part] = 1
    return twiddle, step, place.reshape(128, 384).astype(ml_dtypes.bfloat16)


def turn(value, eighths):
    re, im = value
    root = math.sqrt(0.5)
    if eighths == 0:
        return value
    if eighths == 1:
        return (re + im) * root, (im - re) * root
    if eighths == 2:
        return im, -re
    return (im - re) * root, -(re + im) * root


def butterfly(values):
    count = len(values)
    if count == 1:
        return values
    even, odd = butterfly(values[0::2]), butterfly(values[1::2])
    low, high = [], []
    for k in range(count // 2):
        a, b = even[k], turn(odd[k], k * 8 // count)
        low.append((a[0] + b[0], a[1] + b[1]))
        high.append((a[0] - b[0], a[1] - b[1]))
    return low + high


def kernel(
    samples_hbm, wigner, step_hbm, place_hbm, twiddle_hbm, out,
    samples, wig, step, place, twiddle, send_a, buf_a, send_b, buf_b, send_c, buf_c, send_d, buf_d,
    gathered, own_e, send_e, buf_e, send_f, buf_f, send_sem, recv_sem, recv_d_sem, load_sem, wigner_sem,
):
    wide, beta = lax.axis_index("wide"), lax.axis_index("beta")
    z, v = wide // 8, wide % 8
    z_hi, x = beta // 4, beta % 4
    other = (beta + 4) % 8

    load_samples = pltpu.make_async_copy(samples_hbm, samples, load_sem.at[0])
    load_twiddle = pltpu.make_async_copy(twiddle_hbm, twiddle, load_sem.at[1])
    load_step = pltpu.make_async_copy(step_hbm, step, load_sem.at[2])
    load_place = pltpu.make_async_copy(place_hbm, place, load_sem.at[3])
    load_wigner = [
        pltpu.make_async_copy(wigner.at[m], wig.at[m], wigner_sem.at[m]) for m in range(8)
    ]
    load_samples.start()

    def across(d):
        return sum((z // bit + d // bit) % 2 * bit for bit in (1, 2, 4))

    line = [(across(d) * 8 + v, beta) for d in range(1, 8)]
    far = [(across(d) * 8 + v, other) for d in range(8)]
    plane = [(z * 8 + (v + d) % 8, beta) for d in range(1, 8)]
    ring = [(wide, z_hi * 4 + (x + d) % 4) for d in range(1, 4)]
    peers = far + line[::-1] + plane + ring
    barrier = pltpu.get_barrier_semaphore()
    for at_wide, at_beta in peers:
        pl.semaphore_signal(
            barrier, inc=1, device_id={"wide": at_wide, "beta": at_beta}, device_id_type=MESH
        )
    for load in (load_twiddle, load_step, load_place, *load_wigner):
        load.start()

    lane = lax.broadcasted_iota(jnp.int32, (16, 128), 1)
    first = lane % 2 == 0
    load_samples.wait()
    for m in range(8):
        for side in range(2):
            cycle = 127 - lane // 2 if side else lane // 2
            re, im = [jnp.take_along_axis(samples[part, m], cycle, axis=1) for part in range(2)]
            send_a[8 * side + m] = jnp.where(first, re, im)
    pl.semaphore_wait(barrier, len(peers))

    def send(source, target, to, sent, arrived):
        pltpu.make_async_remote_copy(
            src_ref=source,
            dst_ref=target,
            send_sem=sent,
            recv_sem=arrived,
            device_id={"wide": to[0], "beta": to[1]},
            device_id_type=MESH,
        ).start()

    def wait(block, semaphore):
        pltpu.make_async_copy(block, block, semaphore).wait()

    send(send_a.at[8 + z], buf_a.at[8 + z], far[0], send_sem.at[0], recv_sem.at[0])
    for to_hi in (1, 0):
        side = 1 - z_hi if to_hi else z_hi
        for k in range(1, 8):
            to = across(8 - k + side * (2 * k - 8))
            send(
                send_a.at[8 * side + to],
                buf_a.at[8 * side + z],
                (8 * to + v, 4 * to_hi + x),
                send_sem.at[0],
                recv_sem.at[0],
            )
    pltpu.make_async_copy(send_a.at[z], buf_a.at[z], recv_sem.at[0]).start()
    load_twiddle.wait()
    wait(buf_a, recv_sem.at[0])
    sign = (1 - 2 * z_hi).astype(F32)
    values = []
    for n in range(8):
        own, mirror = buf_a[n], buf_a[8 + n]
        even, odd = own + mirror, (own - mirror) * sign
        re = jnp.where(first, even, pltpu.roll(odd, 1, 1))
        im = jnp.where(first, pltpu.roll(even, 127, 1), odd)
        values.append((re, im))
    done = butterfly(values)
    re = jnp.concatenate([value[0] for value in done], axis=0).T
    im = jnp.concatenate([value[1] for value in done], axis=0).T
    factor = twiddle[v]
    cosine, sine = factor[0:1], factor[1:2]
    send_b[:, 0] = (re * cosine - im * sine).reshape(8, 16, 128)
    send_b[:, 1] = (re * sine + im * cosine).reshape(8, 16, 128)

    for d in (4, 3, 5, 2, 6, 1, 7):
        source, target = send_b.at[(v + d) % 8], buf_b.at[v]
        send(source, target, plane[d - 1], send_sem.at[1], recv_sem.at[1])
    pltpu.make_async_copy(send_b.at[v], buf_b.at[v], recv_sem.at[1]).start()
    wait(send_a.at[pl.ds(0, 15)], send_sem.at[0])
    load_step.wait()
    load_place.wait()
    wait(buf_b, recv_sem.at[1])
    done = butterfly([(buf_b[n, 0], buf_b[n, 1]) for n in range(8)])
    turned = []
    for k2 in range(8):
        re, im = done[k2]
        factor = twiddle[8 + k2]
        cosine, sine = factor[0:1], factor[1:2]
        turned.append(
            jnp.concatenate([re * cosine - im * sine, re * sine + im * cosine], axis=1)
        )
    values = jnp.concatenate(turned[0::2] + turned[1::2], axis=0)
    high = values.astype(BF16)
    low = (values - high.astype(F32)).astype(BF16)
    values = jnp.concatenate([high, low, high], axis=1)
    spectrum = jnp.dot(values, step[...], preferred_element_type=F32)
    first_half = lax.broadcasted_iota(jnp.int32, (64, 128), 1) < 64
    for h in range(2):
        a = spectrum[0:64, 128 * h : 128 * h + 128]
        b = spectrum[64:128, 128 * h : 128 * h + 128]
        re = jnp.where(first_half, a, pltpu.roll(b, 64, 1))
        im = jnp.where(first_half, pltpu.roll(a, 64, 1), b)
        send_c[4 * h : 4 * h + 4, 0] = re.astype(BF16).reshape(4, 16, 128)
        send_c[4 * h : 4 * h + 4, 1] = im.astype(BF16).reshape(4, 16, 128)

    for d in (4, 3, 5, 2, 6, 1, 7):
        source, target = send_c.at[(v + d) % 8], buf_c.at[v]
        send(source, target, plane[d - 1], send_sem.at[2], recv_sem.at[2])
    pltpu.make_async_copy(send_c.at[v], buf_c.at[v], recv_sem.at[2]).start()
    wait(send_b.at[pl.ds(0, 7)], send_sem.at[1])
    wait(buf_c, recv_sem.at[2])
    for part in range(2):
        values = buf_c[:, part].reshape(128, 128).astype(F32).T
        values = [values[64 * e : 64 * e + 64].reshape(8, 8, 128) for e in range(2)]
        send_d[:, part] = jnp.concatenate(values, axis=1).astype(BF16)

    for d in range(7, 0, -1):
        source, target = send_d.at[across(d)], buf_d.at[z]
        send(source, target, line[d - 1], send_sem.at[3], recv_d_sem.at[d])
    pltpu.make_async_copy(send_d.at[z], buf_d.at[z], recv_d_sem.at[0]).start()
    wait(send_c.at[pl.ds(0, 7)], send_sem.at[2])

    row = lax.broadcasted_iota(jnp.int32, (8, 128), 0)
    lane = lax.broadcasted_iota(jnp.int32, (8, 128), 1)
    fits = [[(lane % 2 == parity) & (row // 4 == low) for low in range(2)] for parity in range(2)]
    second = lax.broadcasted_iota(jnp.int32, (16, 128), 0) // 2 % 2 == 1

    def products(g):
        steps = (2 * g, 2 * g + 1)
        orders = [across(d) for d in steps]
        for d, m in zip(steps, orders):
            wait(buf_d.at[m], recv_d_sem.at[d])
        for at, m in enumerate(orders):
            pltpu.make_async_copy(wigner.at[m], wig.at[m], wigner_sem.at[m]).wait()
            for part in range(2):
                gathered[g, pl.ds(2 * at + part, 16, stride=4)] = buf_d[m, part].astype(F32)
        terms = []
        for i in range(8):
            rows = gathered[g, 8 * i : 8 * i + 8]
            pairs = [
                jnp.concatenate([jnp.where(fit, rows, 0.0) for fit in parity], axis=1)
                for parity in fits
            ]
            weights = [wig[m, 256 * i : 256 * i + 256] for m in orders]
            both = jnp.dot(
                jnp.concatenate(pairs, axis=0).astype(BF16),
                jnp.concatenate(weights, axis=1),
                preferred_element_type=F32,
            )
            terms.append(jnp.where(second, both[:, 128:256], both[:, 0:128]))
        terms = jnp.concatenate(terms, axis=0).T
        own_e[:, g] = terms.reshape(8, 16, 128)
        terms = terms.astype(BF16)
        for owner in range(8):
            send_e[owner // 4, owner % 4, g] = terms[16 * owner : 16 * owner + 16]

    def total_of(owner):
        total = own_e[owner * 4 + x]
        for d in range(3):
            total += buf_e[owner, d].astype(F32)
        return total

    for g in range(4):
        products(g)

    for step, owner in ((4, 1 - z_hi), (5, z_hi)):
        for d in (2, 1, 3):
            source, target = send_e.at[owner, (x + d) % 4], buf_e.at[owner, d - 1]
            send(source, target, ring[d - 1], send_sem.at[step], recv_sem.at[step - 1])
    wait(send_d.at[pl.ds(0, 7)], send_sem.at[3])
    wait(buf_e.at[0], recv_sem.at[3])

    send_f[...] = total_of(1 - z_hi).astype(BF16)
    send(send_f, buf_f, far[0], send_sem.at[6], recv_sem.at[5])
    wait(buf_e.at[1], recv_sem.at[4])
    mine = total_of(z_hi)
    for step in (4, 5):
        wait(send_e.at[0, pl.ds(0, 3)], send_sem.at[step])
    row = lax.broadcasted_iota(jnp.int32, (128, 128), 0)
    lane = lax.broadcasted_iota(jnp.int32, (128, 128), 1)

    def placed(values):
        rows = lax.dot_general(
            place[:, 0 : values.shape[1]],
            jnp.concatenate([values] * 8, axis=0),
            (((1,), (1,)), ((), ())),
            preferred_element_type=F32,
        )
        return jnp.where(lane // 16 == row % 8, rows, 0.0).reshape(16, 8, 128).sum(axis=1)

    high = mine.astype(BF16)
    left = mine - high.astype(F32)
    middle = left.astype(BF16)
    low = (left - middle.astype(F32)).astype(BF16)
    mine = jnp.concatenate([high, middle, low], axis=2)
    mine = [placed(mine[g]) for g in range(4)]
    wait(buf_f, recv_sem.at[5])
    for g in range(4):
        rows = mine[g] + placed(buf_f[g])
        for at in range(2):
            for part in range(2):
                first_row = 8 * at + 4 * part
                out[part, across(2 * g + at)] = rows[first_row : first_row + 4]
    wait(send_f, send_sem.at[6])


def body(samples, wigner):
    twiddle, step, place = tables()
    anywhere = pl.BlockSpec(memory_space=pl.ANY)
    terms = pl.pallas_call(
        kernel,
        out_shape=jax.ShapeDtypeStruct((2, 8, 4, 128), F32),
        in_specs=[anywhere] * 5,
        out_specs=pl.BlockSpec(memory_space=pltpu.VMEM),
        scratch_shapes=[
            pltpu.VMEM((2, 8, 16, 128), F32),
            pltpu.VMEM((8, 2048, 128), BF16),
            pltpu.VMEM((768, 256), BF16),
            pltpu.VMEM((128, 384), BF16),
            pltpu.VMEM((16, 2, 128), F32),
            pltpu.VMEM((16, 16, 128), F32),
            pltpu.VMEM((16, 16, 128), F32),
            pltpu.VMEM((8, 2, 16, 128), F32),
            pltpu.VMEM((8, 2, 16, 128), F32),
            pltpu.VMEM((8, 2, 16, 128), BF16),
            pltpu.VMEM((8, 2, 16, 128), BF16),
            pltpu.VMEM((8, 2, 16, 128), BF16),
            pltpu.VMEM((8, 2, 16, 128), BF16),
            pltpu.VMEM((4, 64, 128), F32),
            pltpu.VMEM((8, 4, 16, 128), F32),
            pltpu.VMEM((2, 4, 4, 16, 128), BF16),
            pltpu.VMEM((2, 3, 4, 16, 128), BF16),
            pltpu.VMEM((4, 16, 128), BF16),
            pltpu.VMEM((4, 16, 128), BF16),
            pltpu.SemaphoreType.DMA((7,)),
            pltpu.SemaphoreType.DMA((6,)),
            pltpu.SemaphoreType.DMA((8,)),
            pltpu.SemaphoreType.DMA((4,)),
            pltpu.SemaphoreType.DMA((8,)),
        ],
        compiler_params=pltpu.CompilerParams(
            collective_id=0, has_side_effects=True, vmem_limit_bytes=60 * 1024 * 1024
        ),
    )(
        samples,
        wigner.reshape(8, 2048, 128),
        jnp.asarray(step),
        jnp.asarray(place),
        jnp.asarray(twiddle),
    )
    return terms.reshape(2, 8, 16, 2, 16)


def solution(mesh):
    return jax.shard_map(
        body,
        mesh=mesh,
        in_specs=(P(None, None, "wide", "beta"), P(None, "wide", "beta", None, None)),
        out_specs=P(None, None, "wide", None, "beta"),
        check_vma=False,
    )
```

```python
import math

import jax
import jax.numpy as jnp
import ml_dtypes
import numpy as np
from jax import lax
from jax.experimental import pallas as pl
from jax.experimental.pallas import tpu as pltpu
from jax.sharding import PartitionSpec as P

MESH = pl.DeviceIdType.MESH
BF16 = jnp.bfloat16
F32 = jnp.float32


def tables():
    lane = np.arange(128)
    k1, n3 = lane // 16, lane % 16
    rows = []
    for v in range(8):
        angle = 2 * math.pi * ((16 * v + n3) * k1 % 1024) / 1024
        rows.append(np.stack([np.cos(angle), -np.sin(angle)]) / 32)
    for k2 in range(8):
        angle = 2 * math.pi * (n3 * k2 % 128) / 128
        rows.append(np.stack([np.cos(angle), -np.sin(angle)]))
    twiddle = np.stack(rows).astype(np.float32)

    step = np.zeros((2, 8, 16, 2, 2, 8, 8))
    three = np.arange(16)
    for first in range(8):
        for h in range(2):
            for z in range(8):
                angle = 2 * math.pi * (three * (2 * z + h) % 16) / 16
                cosine, sine = np.cos(angle), np.sin(angle)
                step[0, first, :, h, 0, z, first] = cosine
                step[0, first, :, h, 1, z, first] = -sine
                step[1, first, :, h, 0, z, first] = sine
                step[1, first, :, h, 1, z, first] = cosine
    step = step.reshape(256, 256)
    high = step.astype(ml_dtypes.bfloat16)
    low = (step - high.astype(np.float64)).astype(ml_dtypes.bfloat16)
    step = np.concatenate([high, low])

    place = np.zeros((2, 2, 8, 2, 2, 3, 8, 2, 2, 2, 2))
    for m, part, half, low, parity in np.ndindex(2, 2, 8, 2, 2):
        place[m, part, half, low, parity, :, half, parity, low, m, part] = 1
    return twiddle, step, place.reshape(128, 384).astype(ml_dtypes.bfloat16)


def turn(value, eighths):
    re, im = value
    root = math.sqrt(0.5)
    if eighths == 0:
        return value
    if eighths == 1:
        return (re + im) * root, (im - re) * root
    if eighths == 2:
        return im, -re
    return (im - re) * root, -(re + im) * root


def butterfly(values):
    count = len(values)
    if count == 1:
        return values
    even, odd = butterfly(values[0::2]), butterfly(values[1::2])
    low, high = [], []
    for k in range(count // 2):
        a, b = even[k], turn(odd[k], k * 8 // count)
        low.append((a[0] + b[0], a[1] + b[1]))
        high.append((a[0] - b[0], a[1] - b[1]))
    return low + high


def kernel(
    samples_hbm, wigner, step_hbm, place_hbm, twiddle_hbm, out,
    samples, wig, step, place, twiddle, send_a, buf_a, send_m, buf_m, send_b, buf_b, send_c, buf_c, send_d, buf_d,
    gathered, own_e, send_e, buf_e, send_f, buf_f, send_sem, recv_sem, recv_d_sem, load_sem, wigner_sem,
):
    wide, beta = lax.axis_index("wide"), lax.axis_index("beta")
    z, v = wide // 8, wide % 8
    z_hi, x = beta // 4, beta % 4
    other = (beta + 4) % 8

    load_samples = pltpu.make_async_copy(samples_hbm, samples, load_sem.at[0])
    load_twiddle = pltpu.make_async_copy(twiddle_hbm, twiddle, load_sem.at[1])
    load_step = pltpu.make_async_copy(step_hbm, step, load_sem.at[2])
    load_place = pltpu.make_async_copy(place_hbm, place, load_sem.at[3])
    load_wigner = [
        pltpu.make_async_copy(wigner.at[m], wig.at[m], wigner_sem.at[m]) for m in range(8)
    ]
    load_samples.start()

    def across(d):
        return sum((z // bit + d // bit) % 2 * bit for bit in (1, 2, 4))

    line = [(across(d) * 8 + v, beta) for d in range(1, 8)]
    far = [(across(d) * 8 + v, other) for d in range(8)]
    plane = [(z * 8 + (v + d) % 8, beta) for d in range(1, 8)]
    ring = [(wide, z_hi * 4 + (x + d) % 4) for d in range(1, 4)]
    peers = far + line[::-1] + plane + ring
    barrier = pltpu.get_barrier_semaphore()
    for at_wide, at_beta in peers:
        pl.semaphore_signal(
            barrier, inc=1, device_id={"wide": at_wide, "beta": at_beta}, device_id_type=MESH
        )
    for load in (load_twiddle, load_step, load_place, *load_wigner):
        load.start()

    lane = lax.broadcasted_iota(jnp.int32, (16, 128), 1)
    first = lane % 2 == 0
    load_samples.wait()
    for m in range(8):
        for side in range(2):
            cycle = 127 - lane // 2 if side else lane // 2
            re, im = [jnp.take_along_axis(samples[part, m], cycle, axis=1) for part in range(2)]
            send_a[8 * side + m] = jnp.where(first, re, im)
            if side:
                send_m[m] = jnp.where(first, re, im).astype(BF16)
    pl.semaphore_wait(barrier, len(peers))

    def send(source, target, to, sent, arrived):
        pltpu.make_async_remote_copy(
            src_ref=source,
            dst_ref=target,
            send_sem=sent,
            recv_sem=arrived,
            device_id={"wide": to[0], "beta": to[1]},
            device_id_type=MESH,
        ).start()

    def wait(block, semaphore):
        pltpu.make_async_copy(block, block, semaphore).wait()

    pltpu.make_async_copy(send_a.at[z], buf_a.at[z], recv_sem.at[0]).start()

    def send_own():
        for d in range(7, 0, -1):
            source, target = send_a.at[across(d)], buf_a.at[z]
            send(source, target, line[d - 1], send_sem.at[0], recv_sem.at[0])

    @pl.when(z_hi == 0)
    def _():
        for d in range(8):
            source, target = send_m.at[across(d)], buf_m.at[z]
            send(source, target, far[d], send_sem.at[7], recv_sem.at[6])
        send_own()

    @pl.when(z_hi == 1)
    def _():
        send_own()
        for d in range(8):
            source, target = send_a.at[8 + across(d)], buf_a.at[8 + z]
            send(source, target, far[d], send_sem.at[7], recv_sem.at[6])

    load_twiddle.wait()
    wait(buf_a.at[pl.ds(0, 8)], recv_sem.at[0])

    @pl.when(z_hi == 0)
    def _():
        wait(buf_a.at[pl.ds(8, 8)], recv_sem.at[6])

    @pl.when(z_hi == 1)
    def _():
        wait(buf_m, recv_sem.at[6])
        for n in range(8):
            buf_a[8 + n] = buf_m[n].astype(F32)

    sign = (1 - 2 * z_hi).astype(F32)
    values = []
    for n in range(8):
        own, mirror = buf_a[n], buf_a[8 + n]
        even, odd = own + mirror, (own - mirror) * sign
        re = jnp.where(first, even, pltpu.roll(odd, 1, 1))
        im = jnp.where(first, pltpu.roll(even, 127, 1), odd)
        values.append((re, im))
    done = butterfly(values)
    re = jnp.concatenate([value[0] for value in done], axis=0).T
    im = jnp.concatenate([value[1] for value in done], axis=0).T
    factor = twiddle[v]
    cosine, sine = factor[0:1], factor[1:2]
    send_b[:, 0] = (re * cosine - im * sine).reshape(8, 16, 128)
    send_b[:, 1] = (re * sine + im * cosine).reshape(8, 16, 128)

    pltpu.make_async_copy(send_b.at[v], buf_b.at[v], recv_sem.at[1]).start()
    for d in (4, 3, 5, 2, 6, 1, 7):
        source, target = send_b.at[(v + d) % 8], buf_b.at[v]
        send(source, target, plane[d - 1], send_sem.at[1], recv_sem.at[1])
    wait(send_a.at[pl.ds(0, 7)], send_sem.at[0])

    @pl.when(z_hi == 0)
    def _():
        wait(send_m, send_sem.at[7])

    @pl.when(z_hi == 1)
    def _():
        wait(send_a.at[pl.ds(8, 8)], send_sem.at[7])

    load_step.wait()
    load_place.wait()
    wait(buf_b, recv_sem.at[1])
    done = butterfly([(buf_b[n, 0], buf_b[n, 1]) for n in range(8)])
    turned = []
    for k2 in range(8):
        re, im = done[k2]
        factor = twiddle[8 + k2]
        cosine, sine = factor[0:1], factor[1:2]
        turned.append(
            jnp.concatenate([re * cosine - im * sine, re * sine + im * cosine], axis=1)
        )
    values = jnp.concatenate(turned[0::2] + turned[1::2], axis=0)
    high = values.astype(BF16)
    low = (values - high.astype(F32)).astype(BF16)
    both = jnp.concatenate([high, low], axis=0)
    main = jnp.dot(both, step[0:256], preferred_element_type=F32)
    rest = jnp.dot(high, step[256:512], preferred_element_type=F32)
    spectrum = main[0:128] + (main[128:256] + rest)
    first_half = lax.broadcasted_iota(jnp.int32, (64, 128), 1) < 64
    for h in range(2):
        a = spectrum[0:64, 128 * h : 128 * h + 128]
        b = spectrum[64:128, 128 * h : 128 * h + 128]
        re = jnp.where(first_half, a, pltpu.roll(b, 64, 1))
        im = jnp.where(first_half, pltpu.roll(a, 64, 1), b)
        send_c[4 * h : 4 * h + 4, 0] = re.astype(BF16).reshape(4, 16, 128)
        send_c[4 * h : 4 * h + 4, 1] = im.astype(BF16).reshape(4, 16, 128)

    pltpu.make_async_copy(send_c.at[v], buf_c.at[v], recv_sem.at[2]).start()
    for d in (4, 3, 5, 2, 6, 1, 7):
        source, target = send_c.at[(v + d) % 8], buf_c.at[v]
        send(source, target, plane[d - 1], send_sem.at[2], recv_sem.at[2])
    wait(send_b.at[pl.ds(0, 7)], send_sem.at[1])
    wait(buf_c, recv_sem.at[2])
    for part in range(2):
        values = buf_c[:, part].reshape(128, 128).astype(F32).T
        values = [values[64 * e : 64 * e + 64].reshape(8, 8, 128) for e in range(2)]
        send_d[:, part] = jnp.concatenate(values, axis=1).astype(BF16)

    pltpu.make_async_copy(send_d.at[z], buf_d.at[z], recv_d_sem.at[0]).start()
    for d in range(7, 0, -1):
        source, target = send_d.at[across(d)], buf_d.at[z]
        send(source, target, line[d - 1], send_sem.at[3], recv_d_sem.at[d])
    wait(send_c.at[pl.ds(0, 7)], send_sem.at[2])

    row = lax.broadcasted_iota(jnp.int32, (8, 128), 0)
    lane = lax.broadcasted_iota(jnp.int32, (8, 128), 1)
    fits = [[(lane % 2 == parity) & (row // 4 == low) for low in range(2)] for parity in range(2)]
    second = lax.broadcasted_iota(jnp.int32, (16, 128), 0) // 2 % 2 == 1

    def products(g):
        steps = (2 * g, 2 * g + 1)
        orders = [across(d) for d in steps]
        for d, m in zip(steps, orders):
            wait(buf_d.at[m], recv_d_sem.at[d])
        for at, m in enumerate(orders):
            pltpu.make_async_copy(wigner.at[m], wig.at[m], wigner_sem.at[m]).wait()
            for part in range(2):
                gathered[g, pl.ds(2 * at + part, 16, stride=4)] = buf_d[m, part].astype(F32)
        terms = []
        for i in range(8):
            rows = gathered[g, 8 * i : 8 * i + 8]
            pairs = [
                jnp.concatenate([jnp.where(fit, rows, 0.0) for fit in parity], axis=1)
                for parity in fits
            ]
            weights = [wig[m, 256 * i : 256 * i + 256] for m in orders]
            both = jnp.dot(
                jnp.concatenate(pairs, axis=0).astype(BF16),
                jnp.concatenate(weights, axis=1),
                preferred_element_type=F32,
            )
            terms.append(jnp.where(second, both[:, 128:256], both[:, 0:128]))
        terms = jnp.concatenate(terms, axis=0).T
        own_e[:, g] = terms.reshape(8, 16, 128)
        terms = terms.astype(BF16)
        for owner in range(8):
            send_e[owner // 4, owner % 4, g] = terms[16 * owner : 16 * owner + 16]

    def total_of(owner):
        total = own_e[owner * 4 + x]
        for d in range(3):
            total += buf_e[owner, d].astype(F32)
        return total

    for g in range(4):
        products(g)

    for step, owner in ((4, 1 - z_hi), (5, z_hi)):
        for d in (2, 1, 3):
            source, target = send_e.at[owner, (x + d) % 4], buf_e.at[owner, d - 1]
            send(source, target, ring[d - 1], send_sem.at[step], recv_sem.at[step - 1])
    wait(send_d.at[pl.ds(0, 7)], send_sem.at[3])
    wait(buf_e.at[0], recv_sem.at[3])

    send_f[...] = total_of(1 - z_hi).astype(BF16)
    send(send_f, buf_f, far[0], send_sem.at[6], recv_sem.at[5])
    wait(buf_e.at[1], recv_sem.at[4])
    mine = total_of(z_hi)
    for step in (4, 5):
        wait(send_e.at[0, pl.ds(0, 3)], send_sem.at[step])
    wait(buf_f, recv_sem.at[5])
    total = mine + buf_f[...].astype(F32)
    high = total.astype(BF16)
    left = total - high.astype(F32)
    middle = left.astype(BF16)
    low = (left - middle.astype(F32)).astype(BF16)
    total = jnp.concatenate([high, middle, low], axis=2)
    row = lax.broadcasted_iota(jnp.int32, (128, 128), 0)
    lane = lax.broadcasted_iota(jnp.int32, (128, 128), 1)
    for g in range(4):
        rows = lax.dot_general(
            place[...],
            jnp.concatenate([total[g]] * 8, axis=0),
            (((1,), (1,)), ((), ())),
            preferred_element_type=F32,
        )
        rows = jnp.where(lane // 16 == row % 8, rows, 0.0).reshape(16, 8, 128).sum(axis=1)
        for at in range(2):
            for part in range(2):
                first_row = 8 * at + 4 * part
                out[part, across(2 * g + at)] = rows[first_row : first_row + 4]
    wait(send_f, send_sem.at[6])


def body(samples, wigner):
    twiddle, step, place = tables()
    anywhere = pl.BlockSpec(memory_space=pl.ANY)
    terms = pl.pallas_call(
        kernel,
        out_shape=jax.ShapeDtypeStruct((2, 8, 4, 128), F32),
        in_specs=[anywhere] * 5,
        out_specs=pl.BlockSpec(memory_space=pltpu.VMEM),
        scratch_shapes=[
            pltpu.VMEM((2, 8, 16, 128), F32),
            pltpu.VMEM((8, 2048, 128), BF16),
            pltpu.VMEM((512, 256), BF16),
            pltpu.VMEM((128, 384), BF16),
            pltpu.VMEM((16, 2, 128), F32),
            pltpu.VMEM((16, 16, 128), F32),
            pltpu.VMEM((16, 16, 128), F32),
            pltpu.VMEM((8, 16, 128), BF16),
            pltpu.VMEM((8, 16, 128), BF16),
            pltpu.VMEM((8, 2, 16, 128), F32),
            pltpu.VMEM((8, 2, 16, 128), F32),
            pltpu.VMEM((8, 2, 16, 128), BF16),
            pltpu.VMEM((8, 2, 16, 128), BF16),
            pltpu.VMEM((8, 2, 16, 128), BF16),
            pltpu.VMEM((8, 2, 16, 128), BF16),
            pltpu.VMEM((4, 64, 128), F32),
            pltpu.VMEM((8, 4, 16, 128), F32),
            pltpu.VMEM((2, 4, 4, 16, 128), BF16),
            pltpu.VMEM((2, 3, 4, 16, 128), BF16),
            pltpu.VMEM((4, 16, 128), BF16),
            pltpu.VMEM((4, 16, 128), BF16),
            pltpu.SemaphoreType.DMA((8,)),
            pltpu.SemaphoreType.DMA((7,)),
            pltpu.SemaphoreType.DMA((8,)),
            pltpu.SemaphoreType.DMA((4,)),
            pltpu.SemaphoreType.DMA((8,)),
        ],
        compiler_params=pltpu.CompilerParams(
            collective_id=0, has_side_effects=True, vmem_limit_bytes=60 * 1024 * 1024
        ),
    )(
        samples,
        wigner.reshape(8, 2048, 128),
        jnp.asarray(step),
        jnp.asarray(place),
        jnp.asarray(twiddle),
    )
    return terms.reshape(2, 8, 16, 2, 16)


def solution(mesh):
    return jax.shard_map(
        body,
        mesh=mesh,
        in_specs=(P(None, None, "wide", "beta"), P(None, "wide", "beta", None, None)),
        out_specs=P(None, None, "wide", None, "beta"),
        check_vma=False,
    )
```

```python
import math

import jax
import jax.numpy as jnp
import ml_dtypes
import numpy as np
from jax import lax
from jax.experimental import pallas as pl
from jax.experimental.pallas import tpu as pltpu
from jax.sharding import PartitionSpec as P

MESH = pl.DeviceIdType.MESH
BF16 = jnp.bfloat16
F32 = jnp.float32


def tables():
    lane = np.arange(128)
    k1, n3 = lane // 16, lane % 16
    rows = []
    for v in range(8):
        angle = 2 * math.pi * ((16 * v + n3) * k1 % 1024) / 1024
        rows.append(np.stack([np.cos(angle), -np.sin(angle)]) / 32)
    for k2 in range(8):
        angle = 2 * math.pi * (n3 * k2 % 128) / 128
        rows.append(np.stack([np.cos(angle), -np.sin(angle)]))
    twiddle = np.stack(rows).astype(np.float32)

    step = np.zeros((2, 8, 16, 2, 2, 8, 8))
    three = np.arange(16)
    for first in range(8):
        for h in range(2):
            for z in range(8):
                angle = 2 * math.pi * (three * (2 * z + h) % 16) / 16
                cosine, sine = np.cos(angle), np.sin(angle)
                step[0, first, :, h, 0, z, first] = cosine
                step[0, first, :, h, 1, z, first] = -sine
                step[1, first, :, h, 0, z, first] = sine
                step[1, first, :, h, 1, z, first] = cosine
    step = step.reshape(256, 256)
    high = step.astype(ml_dtypes.bfloat16)
    low = (step - high.astype(np.float64)).astype(ml_dtypes.bfloat16)
    step = np.concatenate([high, low])

    place = np.zeros((2, 2, 8, 2, 2, 3, 8, 2, 2, 2, 2))
    for m, part, half, low, parity in np.ndindex(2, 2, 8, 2, 2):
        place[m, part, half, low, parity, :, half, parity, low, m, part] = 1
    return twiddle, step, place.reshape(128, 384).astype(ml_dtypes.bfloat16)


def turn(value, eighths):
    re, im = value
    root = math.sqrt(0.5)
    if eighths == 0:
        return value
    if eighths == 1:
        return (re + im) * root, (im - re) * root
    if eighths == 2:
        return im, -re
    return (im - re) * root, -(re + im) * root


def butterfly(values):
    count = len(values)
    if count == 1:
        return values
    even, odd = butterfly(values[0::2]), butterfly(values[1::2])
    low, high = [], []
    for k in range(count // 2):
        a, b = even[k], turn(odd[k], k * 8 // count)
        low.append((a[0] + b[0], a[1] + b[1]))
        high.append((a[0] - b[0], a[1] - b[1]))
    return low + high


def kernel(
    samples_hbm, wigner, step_hbm, place_hbm, twiddle_hbm, out,
    samples, wig, step, place, twiddle, send_a, buf_a, send_m, buf_m, send_b, buf_b, send_c, buf_c, send_d, buf_d,
    gathered, own_e, send_e, buf_e, send_f, buf_f, send_sem, recv_sem, recv_d_sem, load_sem, wigner_sem,
):
    wide, beta = lax.axis_index("wide"), lax.axis_index("beta")
    z, v = wide // 8, wide % 8
    z_hi, x = beta // 4, beta % 4
    other = (beta + 4) % 8

    load_samples = pltpu.make_async_copy(samples_hbm, samples, load_sem.at[0])
    load_twiddle = pltpu.make_async_copy(twiddle_hbm, twiddle, load_sem.at[1])
    load_step = pltpu.make_async_copy(step_hbm, step, load_sem.at[2])
    load_place = pltpu.make_async_copy(place_hbm, place, load_sem.at[3])
    load_wigner = [
        pltpu.make_async_copy(wigner.at[m], wig.at[m], wigner_sem.at[m]) for m in range(8)
    ]
    load_samples.start()

    def across(d):
        return sum((z // bit + d // bit) % 2 * bit for bit in (1, 2, 4))

    line = [(across(d) * 8 + v, beta) for d in range(1, 8)]
    far = [(across(d) * 8 + v, other) for d in range(8)]
    plane = [(z * 8 + (v + d) % 8, beta) for d in range(1, 8)]
    ring = [(wide, z_hi * 4 + (x + d) % 4) for d in range(1, 4)]
    peers = far + line[::-1] + plane + ring
    barrier = pltpu.get_barrier_semaphore()
    for at_wide, at_beta in peers:
        pl.semaphore_signal(
            barrier, inc=1, device_id={"wide": at_wide, "beta": at_beta}, device_id_type=MESH
        )
    for load in (load_twiddle, load_step, load_place, *load_wigner):
        load.start()

    lane = lax.broadcasted_iota(jnp.int32, (16, 128), 1)
    first = lane % 2 == 0
    load_samples.wait()
    for m in range(8):
        for side in range(2):
            cycle = 127 - lane // 2 if side else lane // 2
            re, im = [jnp.take_along_axis(samples[part, m], cycle, axis=1) for part in range(2)]
            send_a[8 * side + m] = jnp.where(first, re, im)
            send_m[8 * side + m] = jnp.where(first, re, im).astype(BF16)
    pl.semaphore_wait(barrier, len(peers))

    def send(source, target, to, sent, arrived):
        pltpu.make_async_remote_copy(
            src_ref=source,
            dst_ref=target,
            send_sem=sent,
            recv_sem=arrived,
            device_id={"wide": to[0], "beta": to[1]},
            device_id_type=MESH,
        ).start()

    def wait(block, semaphore):
        pltpu.make_async_copy(block, block, semaphore).wait()

    def send_own(sources, targets):
        pltpu.make_async_copy(sources.at[z], targets.at[z], recv_sem.at[0]).start()
        for d in range(7, 0, -1):
            source, target = sources.at[across(d)], targets.at[z]
            send(source, target, line[d - 1], send_sem.at[0], recv_sem.at[0])

    def send_mirror(sources, targets):
        for d in range(8):
            source, target = sources.at[8 + across(d)], targets.at[8 + z]
            send(source, target, far[d], send_sem.at[7], recv_sem.at[6])

    @pl.when(z_hi == 0)
    def _():
        send_mirror(send_m, buf_m)
        send_own(send_a, buf_a)

    @pl.when(z_hi == 1)
    def _():
        send_own(send_m, buf_m)
        send_mirror(send_a, buf_a)

    load_twiddle.wait()

    @pl.when(z_hi == 0)
    def _():
        wait(buf_a.at[pl.ds(0, 8)], recv_sem.at[0])
        wait(buf_a.at[pl.ds(8, 8)], recv_sem.at[6])

    @pl.when(z_hi == 1)
    def _():
        wait(buf_m.at[pl.ds(0, 8)], recv_sem.at[0])
        wait(buf_m.at[pl.ds(8, 8)], recv_sem.at[6])
        for n in range(16):
            buf_a[n] = buf_m[n].astype(F32)

    sign = (1 - 2 * z_hi).astype(F32)
    values = []
    for n in range(8):
        own, mirror = buf_a[n], buf_a[8 + n]
        even, odd = own + mirror, (own - mirror) * sign
        re = jnp.where(first, even, pltpu.roll(odd, 1, 1))
        im = jnp.where(first, pltpu.roll(even, 127, 1), odd)
        values.append((re, im))
    done = butterfly(values)
    re = jnp.concatenate([value[0] for value in done], axis=0).T
    im = jnp.concatenate([value[1] for value in done], axis=0).T
    factor = twiddle[v]
    cosine, sine = factor[0:1], factor[1:2]
    send_b[:, 0] = (re * cosine - im * sine).reshape(8, 16, 128)
    send_b[:, 1] = (re * sine + im * cosine).reshape(8, 16, 128)

    pltpu.make_async_copy(send_b.at[v], buf_b.at[v], recv_sem.at[1]).start()
    for d in (4, 3, 5, 2, 6, 1, 7):
        source, target = send_b.at[(v + d) % 8], buf_b.at[v]
        send(source, target, plane[d - 1], send_sem.at[1], recv_sem.at[1])

    @pl.when(z_hi == 0)
    def _():
        wait(send_a.at[pl.ds(0, 7)], send_sem.at[0])
        wait(send_m.at[pl.ds(8, 8)], send_sem.at[7])

    @pl.when(z_hi == 1)
    def _():
        wait(send_m.at[pl.ds(0, 7)], send_sem.at[0])
        wait(send_a.at[pl.ds(8, 8)], send_sem.at[7])

    load_step.wait()
    load_place.wait()
    wait(buf_b, recv_sem.at[1])
    done = butterfly([(buf_b[n, 0], buf_b[n, 1]) for n in range(8)])
    turned = []
    for k2 in range(8):
        re, im = done[k2]
        factor = twiddle[8 + k2]
        cosine, sine = factor[0:1], factor[1:2]
        turned.append(
            jnp.concatenate([re * cosine - im * sine, re * sine + im * cosine], axis=1)
        )
    values = jnp.concatenate(turned[0::2] + turned[1::2], axis=0)
    high = values.astype(BF16)
    low = (values - high.astype(F32)).astype(BF16)
    both = jnp.concatenate([high, low], axis=0)
    main = jnp.dot(both, step[0:256], preferred_element_type=F32)
    rest = jnp.dot(high, step[256:512], preferred_element_type=F32)
    spectrum = main[0:128] + (main[128:256] + rest)
    first_half = lax.broadcasted_iota(jnp.int32, (64, 128), 1) < 64
    for h in range(2):
        a = spectrum[0:64, 128 * h : 128 * h + 128]
        b = spectrum[64:128, 128 * h : 128 * h + 128]
        re = jnp.where(first_half, a, pltpu.roll(b, 64, 1))
        im = jnp.where(first_half, pltpu.roll(a, 64, 1), b)
        send_c[4 * h : 4 * h + 4, 0] = re.astype(BF16).reshape(4, 16, 128)
        send_c[4 * h : 4 * h + 4, 1] = im.astype(BF16).reshape(4, 16, 128)

    pltpu.make_async_copy(send_c.at[v], buf_c.at[v], recv_sem.at[2]).start()
    for d in (4, 3, 5, 2, 6, 1, 7):
        source, target = send_c.at[(v + d) % 8], buf_c.at[v]
        send(source, target, plane[d - 1], send_sem.at[2], recv_sem.at[2])
    wait(send_b.at[pl.ds(0, 7)], send_sem.at[1])
    wait(buf_c, recv_sem.at[2])
    for part in range(2):
        values = buf_c[:, part].reshape(128, 128).astype(F32).T
        values = [values[64 * e : 64 * e + 64].reshape(8, 8, 128) for e in range(2)]
        send_d[:, part] = jnp.concatenate(values, axis=1).astype(BF16)

    pltpu.make_async_copy(send_d.at[z], buf_d.at[z], recv_d_sem.at[0]).start()
    for d in range(7, 0, -1):
        source, target = send_d.at[across(d)], buf_d.at[z]
        send(source, target, line[d - 1], send_sem.at[3], recv_d_sem.at[d])
    wait(send_c.at[pl.ds(0, 7)], send_sem.at[2])

    row = lax.broadcasted_iota(jnp.int32, (8, 128), 0)
    lane = lax.broadcasted_iota(jnp.int32, (8, 128), 1)
    fits = [[(lane % 2 == parity) & (row // 4 == low) for low in range(2)] for parity in range(2)]
    second = lax.broadcasted_iota(jnp.int32, (16, 128), 0) // 2 % 2 == 1

    def products(g):
        steps = (2 * g, 2 * g + 1)
        orders = [across(d) for d in steps]
        for d, m in zip(steps, orders):
            wait(buf_d.at[m], recv_d_sem.at[d])
        for at, m in enumerate(orders):
            pltpu.make_async_copy(wigner.at[m], wig.at[m], wigner_sem.at[m]).wait()
            for part in range(2):
                gathered[g, pl.ds(2 * at + part, 16, stride=4)] = buf_d[m, part].astype(F32)
        terms = []
        for i in range(8):
            rows = gathered[g, 8 * i : 8 * i + 8]
            pairs = [
                jnp.concatenate([jnp.where(fit, rows, 0.0) for fit in parity], axis=1)
                for parity in fits
            ]
            weights = [wig[m, 256 * i : 256 * i + 256] for m in orders]
            both = jnp.dot(
                jnp.concatenate(pairs, axis=0).astype(BF16),
                jnp.concatenate(weights, axis=1),
                preferred_element_type=F32,
            )
            terms.append(jnp.where(second, both[:, 128:256], both[:, 0:128]))
        terms = jnp.concatenate(terms, axis=0).T
        own_e[:, g] = terms.reshape(8, 16, 128)
        terms = terms.astype(BF16)
        for owner in range(8):
            send_e[owner // 4, owner % 4, g] = terms[16 * owner : 16 * owner + 16]

    def total_of(owner):
        total = own_e[owner * 4 + x]
        for d in range(3):
            total += buf_e[owner, d].astype(F32)
        return total

    for g in range(4):
        products(g)

    for step, owner in ((4, 1 - z_hi), (5, z_hi)):
        for d in (2, 1, 3):
            source, target = send_e.at[owner, (x + d) % 4], buf_e.at[owner, d - 1]
            send(source, target, ring[d - 1], send_sem.at[step], recv_sem.at[step - 1])
    wait(send_d.at[pl.ds(0, 7)], send_sem.at[3])
    wait(buf_e.at[0], recv_sem.at[3])

    send_f[...] = total_of(1 - z_hi).astype(BF16)
    send(send_f, buf_f, far[0], send_sem.at[6], recv_sem.at[5])
    wait(buf_e.at[1], recv_sem.at[4])
    mine = total_of(z_hi)
    for step in (4, 5):
        wait(send_e.at[0, pl.ds(0, 3)], send_sem.at[step])
    wait(buf_f, recv_sem.at[5])
    total = mine + buf_f[...].astype(F32)
    high = total.astype(BF16)
    left = total - high.astype(F32)
    middle = left.astype(BF16)
    low = (left - middle.astype(F32)).astype(BF16)
    total = jnp.concatenate([high, middle, low], axis=2)
    row = lax.broadcasted_iota(jnp.int32, (128, 128), 0)
    lane = lax.broadcasted_iota(jnp.int32, (128, 128), 1)
    for g in range(4):
        rows = lax.dot_general(
            place[...],
            jnp.concatenate([total[g]] * 8, axis=0),
            (((1,), (1,)), ((), ())),
            preferred_element_type=F32,
        )
        rows = jnp.where(lane // 16 == row % 8, rows, 0.0).reshape(16, 8, 128).sum(axis=1)
        for at in range(2):
            for part in range(2):
                first_row = 8 * at + 4 * part
                out[part, across(2 * g + at)] = rows[first_row : first_row + 4]
    wait(send_f, send_sem.at[6])


def body(samples, wigner):
    twiddle, step, place = tables()
    anywhere = pl.BlockSpec(memory_space=pl.ANY)
    terms = pl.pallas_call(
        kernel,
        out_shape=jax.ShapeDtypeStruct((2, 8, 4, 128), F32),
        in_specs=[anywhere] * 5,
        out_specs=pl.BlockSpec(memory_space=pltpu.VMEM),
        scratch_shapes=[
            pltpu.VMEM((2, 8, 16, 128), F32),
            pltpu.VMEM((8, 2048, 128), BF16),
            pltpu.VMEM((512, 256), BF16),
            pltpu.VMEM((128, 384), BF16),
            pltpu.VMEM((16, 2, 128), F32),
            pltpu.VMEM((16, 16, 128), F32),
            pltpu.VMEM((16, 16, 128), F32),
            pltpu.VMEM((16, 16, 128), BF16),
            pltpu.VMEM((16, 16, 128), BF16),
            pltpu.VMEM((8, 2, 16, 128), F32),
            pltpu.VMEM((8, 2, 16, 128), F32),
            pltpu.VMEM((8, 2, 16, 128), BF16),
            pltpu.VMEM((8, 2, 16, 128), BF16),
            pltpu.VMEM((8, 2, 16, 128), BF16),
            pltpu.VMEM((8, 2, 16, 128), BF16),
            pltpu.VMEM((4, 64, 128), F32),
            pltpu.VMEM((8, 4, 16, 128), F32),
            pltpu.VMEM((2, 4, 4, 16, 128), BF16),
            pltpu.VMEM((2, 3, 4, 16, 128), BF16),
            pltpu.VMEM((4, 16, 128), BF16),
            pltpu.VMEM((4, 16, 128), BF16),
            pltpu.SemaphoreType.DMA((8,)),
            pltpu.SemaphoreType.DMA((7,)),
            pltpu.SemaphoreType.DMA((8,)),
            pltpu.SemaphoreType.DMA((4,)),
            pltpu.SemaphoreType.DMA((8,)),
        ],
        compiler_params=pltpu.CompilerParams(
            collective_id=0, has_side_effects=True, vmem_limit_bytes=60 * 1024 * 1024
        ),
    )(
        samples,
        wigner.reshape(8, 2048, 128),
        jnp.asarray(step),
        jnp.asarray(place),
        jnp.asarray(twiddle),
    )
    return terms.reshape(2, 8, 16, 2, 16)


def solution(mesh):
    return jax.shard_map(
        body,
        mesh=mesh,
        in_specs=(P(None, None, "wide", "beta"), P(None, "wide", "beta", None, None)),
        out_specs=P(None, None, "wide", None, "beta"),
        check_vma=False,
    )
```

```python
import math

import jax
import jax.numpy as jnp
import ml_dtypes
import numpy as np
from jax import lax
from jax.experimental import pallas as pl
from jax.experimental.pallas import tpu as pltpu
from jax.sharding import PartitionSpec as P

MESH = pl.DeviceIdType.MESH
BF16 = jnp.bfloat16
F32 = jnp.float32


def tables():
    lane = np.arange(128)
    k1, n3 = lane // 16, lane % 16
    rows = []
    for v in range(8):
        angle = 2 * math.pi * ((16 * v + n3) * k1 % 1024) / 1024
        rows.append(np.stack([np.cos(angle), -np.sin(angle)]) / 32)
    for k2 in range(8):
        angle = 2 * math.pi * (n3 * k2 % 128) / 128
        rows.append(np.stack([np.cos(angle), -np.sin(angle)]))
    twiddle = np.stack(rows).astype(np.float32)

    step = np.zeros((2, 8, 16, 2, 2, 8, 8))
    three = np.arange(16)
    for first in range(8):
        for h in range(2):
            for z in range(8):
                angle = 2 * math.pi * (three * (2 * z + h) % 16) / 16
                cosine, sine = np.cos(angle), np.sin(angle)
                step[0, first, :, h, 0, z, first] = cosine
                step[0, first, :, h, 1, z, first] = -sine
                step[1, first, :, h, 0, z, first] = sine
                step[1, first, :, h, 1, z, first] = cosine
    step = step.reshape(256, 256)
    high = step.astype(ml_dtypes.bfloat16)
    low = (step - high.astype(np.float64)).astype(ml_dtypes.bfloat16)
    step = np.concatenate([high, low])

    place = np.zeros((2, 2, 8, 2, 2, 3, 8, 2, 2, 2, 2))
    for m, part, half, low, parity in np.ndindex(2, 2, 8, 2, 2):
        place[m, part, half, low, parity, :, half, parity, low, m, part] = 1
    return twiddle, step, place.reshape(128, 384).astype(ml_dtypes.bfloat16)


def turn(value, eighths):
    re, im = value
    root = math.sqrt(0.5)
    if eighths == 0:
        return value
    if eighths == 1:
        return (re + im) * root, (im - re) * root
    if eighths == 2:
        return im, -re
    return (im - re) * root, -(re + im) * root


def butterfly(values):
    count = len(values)
    if count == 1:
        return values
    even, odd = butterfly(values[0::2]), butterfly(values[1::2])
    low, high = [], []
    for k in range(count // 2):
        a, b = even[k], turn(odd[k], k * 8 // count)
        low.append((a[0] + b[0], a[1] + b[1]))
        high.append((a[0] - b[0], a[1] - b[1]))
    return low + high


def kernel(
    samples_hbm, wigner, step_hbm, place_hbm, twiddle_hbm, out,
    samples, wig, step, place, twiddle, send_a, buf_a, send_m, buf_m, send_b, buf_b, send_c, buf_c, send_d, buf_d,
    gathered, own_e, send_e, buf_e, send_f, buf_f, send_sem, recv_sem, recv_d_sem, load_sem, wigner_sem,
):
    wide, beta = lax.axis_index("wide"), lax.axis_index("beta")
    z, v = wide // 8, wide % 8
    z_hi, x = beta // 4, beta % 4
    other = (beta + 4) % 8

    load_samples = pltpu.make_async_copy(samples_hbm, samples, load_sem.at[0])
    load_twiddle = pltpu.make_async_copy(twiddle_hbm, twiddle, load_sem.at[1])
    load_step = pltpu.make_async_copy(step_hbm, step, load_sem.at[2])
    load_place = pltpu.make_async_copy(place_hbm, place, load_sem.at[3])
    load_wigner = [
        pltpu.make_async_copy(wigner.at[m], wig.at[m], wigner_sem.at[m]) for m in range(8)
    ]
    load_samples.start()

    def across(d):
        return sum((z // bit + d // bit) % 2 * bit for bit in (1, 2, 4))

    line = [(across(d) * 8 + v, beta) for d in range(1, 8)]
    far = [(across(d) * 8 + v, other) for d in range(8)]
    plane = [(z * 8 + (v + d) % 8, beta) for d in range(1, 8)]
    ring = [(wide, z_hi * 4 + (x + d) % 4) for d in range(1, 4)]
    peers = far + line[::-1] + plane + ring
    barrier = pltpu.get_barrier_semaphore()
    for at_wide, at_beta in peers:
        pl.semaphore_signal(
            barrier, inc=1, device_id={"wide": at_wide, "beta": at_beta}, device_id_type=MESH
        )
    for load in (load_twiddle, load_step, load_place, *load_wigner):
        load.start()

    lane = lax.broadcasted_iota(jnp.int32, (16, 128), 1)
    first = lane % 2 == 0
    load_samples.wait()
    for m in range(8):
        for side in range(2):
            cycle = 127 - lane // 2 if side else lane // 2
            re, im = [jnp.take_along_axis(samples[part, m], cycle, axis=1) for part in range(2)]
            send_a[8 * side + m] = jnp.where(first, re, im)
            if side:
                send_m[m] = jnp.where(first, re, im).astype(BF16)
    pl.semaphore_wait(barrier, len(peers))

    def send(source, target, to, sent, arrived):
        pltpu.make_async_remote_copy(
            src_ref=source,
            dst_ref=target,
            send_sem=sent,
            recv_sem=arrived,
            device_id={"wide": to[0], "beta": to[1]},
            device_id_type=MESH,
        ).start()

    def wait(block, semaphore):
        pltpu.make_async_copy(block, block, semaphore).wait()

    pltpu.make_async_copy(send_a.at[z], buf_a.at[z], recv_sem.at[0]).start()

    def send_own():
        for d in range(7, 0, -1):
            source, target = send_a.at[across(d)], buf_a.at[z]
            send(source, target, line[d - 1], send_sem.at[0], recv_sem.at[0])

    @pl.when(z_hi == 0)
    def _():
        for d in range(8):
            source, target = send_m.at[across(d)], buf_m.at[z]
            send(source, target, far[d], send_sem.at[7], recv_sem.at[6])
        send_own()

    @pl.when(z_hi == 1)
    def _():
        send_own()
        for d in range(8):
            source, target = send_a.at[8 + across(d)], buf_a.at[8 + z]
            send(source, target, far[d], send_sem.at[7], recv_sem.at[6])

    load_twiddle.wait()
    wait(buf_a.at[pl.ds(0, 8)], recv_sem.at[0])

    @pl.when(z_hi == 0)
    def _():
        wait(buf_a.at[pl.ds(8, 8)], recv_sem.at[6])

    @pl.when(z_hi == 1)
    def _():
        wait(buf_m, recv_sem.at[6])
        for n in range(8):
            buf_a[8 + n] = buf_m[n].astype(F32)

    sign = (1 - 2 * z_hi).astype(F32)
    values = []
    for n in range(8):
        own, mirror = buf_a[n], buf_a[8 + n]
        even, odd = own + mirror, (own - mirror) * sign
        re = jnp.where(first, even, pltpu.roll(odd, 1, 1))
        im = jnp.where(first, pltpu.roll(even, 127, 1), odd)
        values.append((re, im))
    done = butterfly(values)
    re = jnp.concatenate([value[0] for value in done], axis=0).T
    im = jnp.concatenate([value[1] for value in done], axis=0).T
    factor = twiddle[v]
    cosine, sine = factor[0:1], factor[1:2]
    send_b[:, 0] = (re * cosine - im * sine).reshape(8, 16, 128)
    send_b[:, 1] = (re * sine + im * cosine).reshape(8, 16, 128)

    pltpu.make_async_copy(send_b.at[v], buf_b.at[v], recv_sem.at[1]).start()
    for d in (4, 3, 5, 2, 6, 1, 7):
        source, target = send_b.at[(v + d) % 8], buf_b.at[v]
        send(source, target, plane[d - 1], send_sem.at[1], recv_sem.at[1])
    wait(send_a.at[pl.ds(0, 7)], send_sem.at[0])

    @pl.when(z_hi == 0)
    def _():
        wait(send_m, send_sem.at[7])

    @pl.when(z_hi == 1)
    def _():
        wait(send_a.at[pl.ds(8, 8)], send_sem.at[7])

    load_step.wait()
    load_place.wait()
    wait(buf_b, recv_sem.at[1])
    done = butterfly([(buf_b[n, 0], buf_b[n, 1]) for n in range(8)])
    turned = []
    for k2 in range(8):
        re, im = done[k2]
        factor = twiddle[8 + k2]
        cosine, sine = factor[0:1], factor[1:2]
        turned.append(
            jnp.concatenate([re * cosine - im * sine, re * sine + im * cosine], axis=1)
        )
    values = jnp.concatenate(turned[0::2] + turned[1::2], axis=0)
    high = values.astype(BF16)
    low = (values - high.astype(F32)).astype(BF16)
    both = jnp.concatenate([high, low], axis=0)
    main = jnp.dot(both, step[0:256], preferred_element_type=F32)
    rest = jnp.dot(high, step[256:512], preferred_element_type=F32)
    spectrum = main[0:128] + (main[128:256] + rest)
    first_half = lax.broadcasted_iota(jnp.int32, (64, 128), 1) < 64
    for h in range(2):
        a = spectrum[0:64, 128 * h : 128 * h + 128]
        b = spectrum[64:128, 128 * h : 128 * h + 128]
        re = jnp.where(first_half, a, pltpu.roll(b, 64, 1))
        im = jnp.where(first_half, pltpu.roll(a, 64, 1), b)
        send_c[4 * h : 4 * h + 4, 0] = re.astype(BF16).reshape(4, 16, 128)
        send_c[4 * h : 4 * h + 4, 1] = im.astype(BF16).reshape(4, 16, 128)

    pltpu.make_async_copy(send_c.at[v], buf_c.at[v], recv_sem.at[2]).start()
    for d in (4, 3, 5, 2, 6, 1, 7):
        source, target = send_c.at[(v + d) % 8], buf_c.at[v]
        send(source, target, plane[d - 1], send_sem.at[2], recv_sem.at[2])
    wait(send_b.at[pl.ds(0, 7)], send_sem.at[1])
    wait(buf_c, recv_sem.at[2])
    for part in range(2):
        values = buf_c[:, part].reshape(128, 128).astype(F32).T
        values = [values[64 * e : 64 * e + 64].reshape(8, 8, 128) for e in range(2)]
        send_d[:, part] = jnp.concatenate(values, axis=1).astype(BF16)

    pltpu.make_async_copy(send_d.at[z], buf_d.at[z], recv_d_sem.at[0]).start()
    for d in range(1, 8):
        source, target = send_d.at[across(d)], buf_d.at[z]
        send(source, target, line[d - 1], send_sem.at[3], recv_d_sem.at[d])
    wait(send_c.at[pl.ds(0, 7)], send_sem.at[2])

    row = lax.broadcasted_iota(jnp.int32, (8, 128), 0)
    lane = lax.broadcasted_iota(jnp.int32, (8, 128), 1)
    fits = [[(lane % 2 == parity) & (row // 4 == low) for low in range(2)] for parity in range(2)]
    second = lax.broadcasted_iota(jnp.int32, (16, 128), 0) // 2 % 2 == 1

    def products(g):
        steps = (2 * g, 2 * g + 1)
        orders = [across(d) for d in steps]
        for d, m in zip(steps, orders):
            wait(buf_d.at[m], recv_d_sem.at[d])
        for at, m in enumerate(orders):
            pltpu.make_async_copy(wigner.at[m], wig.at[m], wigner_sem.at[m]).wait()
            for part in range(2):
                gathered[g, pl.ds(2 * at + part, 16, stride=4)] = buf_d[m, part].astype(F32)
        terms = []
        for i in range(8):
            rows = gathered[g, 8 * i : 8 * i + 8]
            pairs = [
                jnp.concatenate([jnp.where(fit, rows, 0.0) for fit in parity], axis=1)
                for parity in fits
            ]
            weights = [wig[m, 256 * i : 256 * i + 256] for m in orders]
            both = jnp.dot(
                jnp.concatenate(pairs, axis=0).astype(BF16),
                jnp.concatenate(weights, axis=1),
                preferred_element_type=F32,
            )
            terms.append(jnp.where(second, both[:, 128:256], both[:, 0:128]))
        terms = jnp.concatenate(terms, axis=0).T
        own_e[:, g] = terms.reshape(8, 16, 128)
        terms = terms.astype(BF16)
        for owner in range(8):
            send_e[owner // 4, owner % 4, g] = terms[16 * owner : 16 * owner + 16]

    def total_of(owner):
        total = own_e[owner * 4 + x]
        for d in range(3):
            total += buf_e[owner, d].astype(F32)
        return total

    for g in range(4):
        products(g)

    for step, owner in ((4, 1 - z_hi), (5, z_hi)):
        for d in (2, 1, 3):
            source, target = send_e.at[owner, (x + d) % 4], buf_e.at[owner, d - 1]
            send(source, target, ring[d - 1], send_sem.at[step], recv_sem.at[step - 1])
    wait(send_d.at[pl.ds(0, 7)], send_sem.at[3])
    wait(buf_e.at[0], recv_sem.at[3])

    send_f[...] = total_of(1 - z_hi).astype(BF16)
    send(send_f, buf_f, far[0], send_sem.at[6], recv_sem.at[5])
    wait(buf_e.at[1], recv_sem.at[4])
    mine = total_of(z_hi)
    for step in (4, 5):
        wait(send_e.at[0, pl.ds(0, 3)], send_sem.at[step])
    wait(buf_f, recv_sem.at[5])
    total = mine + buf_f[...].astype(F32)
    high = total.astype(BF16)
    left = total - high.astype(F32)
    middle = left.astype(BF16)
    low = (left - middle.astype(F32)).astype(BF16)
    total = jnp.concatenate([high, middle, low], axis=2)
    row = lax.broadcasted_iota(jnp.int32, (128, 128), 0)
    lane = lax.broadcasted_iota(jnp.int32, (128, 128), 1)
    for g in range(4):
        rows = lax.dot_general(
            place[...],
            jnp.concatenate([total[g]] * 8, axis=0),
            (((1,), (1,)), ((), ())),
            preferred_element_type=F32,
        )
        rows = jnp.where(lane // 16 == row % 8, rows, 0.0).reshape(16, 8, 128).sum(axis=1)
        for at in range(2):
            for part in range(2):
                first_row = 8 * at + 4 * part
                out[part, across(2 * g + at)] = rows[first_row : first_row + 4]
    wait(send_f, send_sem.at[6])


def body(samples, wigner):
    twiddle, step, place = tables()
    anywhere = pl.BlockSpec(memory_space=pl.ANY)
    terms = pl.pallas_call(
        kernel,
        out_shape=jax.ShapeDtypeStruct((2, 8, 4, 128), F32),
        in_specs=[anywhere] * 5,
        out_specs=pl.BlockSpec(memory_space=pltpu.VMEM),
        scratch_shapes=[
            pltpu.VMEM((2, 8, 16, 128), F32),
            pltpu.VMEM((8, 2048, 128), BF16),
            pltpu.VMEM((512, 256), BF16),
            pltpu.VMEM((128, 384), BF16),
            pltpu.VMEM((16, 2, 128), F32),
            pltpu.VMEM((16, 16, 128), F32),
            pltpu.VMEM((16, 16, 128), F32),
            pltpu.VMEM((8, 16, 128), BF16),
            pltpu.VMEM((8, 16, 128), BF16),
            pltpu.VMEM((8, 2, 16, 128), F32),
            pltpu.VMEM((8, 2, 16, 128), F32),
            pltpu.VMEM((8, 2, 16, 128), BF16),
            pltpu.VMEM((8, 2, 16, 128), BF16),
            pltpu.VMEM((8, 2, 16, 128), BF16),
            pltpu.VMEM((8, 2, 16, 128), BF16),
            pltpu.VMEM((4, 64, 128), F32),
            pltpu.VMEM((8, 4, 16, 128), F32),
            pltpu.VMEM((2, 4, 4, 16, 128), BF16),
            pltpu.VMEM((2, 3, 4, 16, 128), BF16),
            pltpu.VMEM((4, 16, 128), BF16),
            pltpu.VMEM((4, 16, 128), BF16),
            pltpu.SemaphoreType.DMA((8,)),
            pltpu.SemaphoreType.DMA((7,)),
            pltpu.SemaphoreType.DMA((8,)),
            pltpu.SemaphoreType.DMA((4,)),
            pltpu.SemaphoreType.DMA((8,)),
        ],
        compiler_params=pltpu.CompilerParams(
            collective_id=0, has_side_effects=True, vmem_limit_bytes=60 * 1024 * 1024
        ),
    )(
        samples,
        wigner.reshape(8, 2048, 128),
        jnp.asarray(step),
        jnp.asarray(place),
        jnp.asarray(twiddle),
    )
    return terms.reshape(2, 8, 16, 2, 16)


def solution(mesh):
    return jax.shard_map(
        body,
        mesh=mesh,
        in_specs=(P(None, None, "wide", "beta"), P(None, "wide", "beta", None, None)),
        out_specs=P(None, None, "wide", None, "beta"),
        check_vma=False,
    )
```
